32 devices in a mesh: replica: 4 (over y, x), expert: 8 (over z, core).
Axes of the slice: x: 2, y: 2, z: 4, core: 2. Of those that a mesh axis runs over, the one named last changes fastest.
Arguments:
- moe_input: bfloat16 [512, 2048], P(('replica', 'expert')), may hold values from -6 to 6
- expert_ids: int32 [512, 8], P(('replica', 'expert')), may hold values from 0 to 7, all different within a row; in each aligned block of 16 rows (0 to 15, 16 to 31, ...) at most 16 rows name the same one
- route_weight: float32 [512, 8], P(('replica', 'expert')), may hold values from 0.05 to 0.5
- expert_slot: int32 [8], replicated, may hold values from 0 to 7, each once
- w_gate_up: bfloat16 [2048, 12288], P(None, ('replica', 'expert')), may hold values from -0.125 to 0.125
- w_down: bfloat16 [6144, 2048], P(('replica', 'expert')), may hold values from -0.21875 to 0.21875
- queries: bfloat16 [64, 8192], P(('replica', 'expert')), may hold values from -80 to 80
- incoming_key_value: bfloat16 [64, 1024], P(('replica', 'expert')), may hold values from -4 to 4
- key_value_pool: bfloat16 [512, 64, 1024], P(('replica', 'expert')), may hold values from -4 to 4
- block_owner: int32 [512], P(('replica', 'expert')), may hold values from 0 to 7, as said below
- block_tokens: int32 [512], P(('replica', 'expert')), may hold values from 1 to 64
Outputs:
- moe_out: bfloat16 [512, 2048], P(('replica', 'expert'))
- attn_out: bfloat16 [64, 8192], P(('replica', 'expert'))
The draws below stay inside these ranges and needn't reach their ends.
Inputs may be any that keep to these rules, and one draw needn't show every extreme that they name: `expert_ids`: in the rows of one device no expert is named by more than 16 rows, a bound that some block reaches. `expert_slot`: each slot hosts one expert. `block_owner`: on every device at most 2 blocks are owned by requests of any one other replica, and exactly 2 for some other replica.
All inputs are finite; a program needn't handle non-finite values.
Results may differ from the reference program's by a relative error of at most 0.0058.
Values may be sent and summed in bfloat16 or wider, within the bound.
A program may use at most 64 MiB of HBM per device.

```python
import math
import jax
import jax.numpy as jnp
import numpy as np
from jax import lax

D = 2048
FFE = 768
QUART = 4
EXPERTS = 8
TOP = 8
TOK_DEV = 16
CAP = 16
TOKENS = 512
QUERY_HEADS = 64
KEY_VALUE_HEADS = 4
HEAD_DIMENSION = 128
DEVICE_REQUESTS = 2
TOTAL_REQUESTS = 64
DEVICE_BLOCKS = 16
BLOCK_SLOTS = 64
MIG = 2
TOTAL_BLOCKS = 512
N_REPLICA = 4
N_EXPERT = 8


def owner_helper(key):
    devices = N_REPLICA * N_EXPERT
    replica_of = jnp.arange(devices, dtype=jnp.int32) // N_EXPERT
    device_keys = jax.random.split(jax.random.fold_in(key, 11), devices)

    def per_device(device_key, replica):
        first, second, third, fourth = jax.random.split(device_key, 4)
        offsets = jax.random.permutation(first, N_REPLICA - 1).astype(jnp.int32) + 1
        query_group = jnp.arange(DEVICE_BLOCKS, dtype=jnp.int32) // MIG
        coin = jax.random.randint(second, (DEVICE_BLOCKS,), 0, 2)
        picked = offsets[jnp.minimum(query_group, N_REPLICA - 2)]
        offset = jnp.where(query_group == 0, offsets[0], jnp.where((query_group < N_REPLICA - 1) & (coin == 1), picked, 0))
        target = (replica + offset) % N_REPLICA
        tail = jax.random.randint(third, (DEVICE_BLOCKS,), 0, 3)
        request = jnp.where(tail == 0, 0, jax.random.randint(fourth, (DEVICE_BLOCKS,), 0, DEVICE_REQUESTS))
        return (target * DEVICE_REQUESTS + request).astype(jnp.int32)
    return jax.vmap(per_device)(device_keys, replica_of).reshape(-1)


def draw_block_owner(key, part):
    return owner_helper(key)


def draw_block_tokens(key, part):
    cached_value_rows = jax.random.randint(jax.random.fold_in(key, 23), (TOTAL_BLOCKS,), 1, BLOCK_SLOTS + 1)
    local = jnp.arange(TOTAL_BLOCKS, dtype=jnp.int32) % DEVICE_BLOCKS
    return jnp.where(local == 0, BLOCK_SLOTS, cached_value_rows).astype(jnp.int32)


def draw_queries(key, part):
    base_offset = jnp.clip(jax.random.normal(jax.random.fold_in(key, 41), (TOTAL_REQUESTS, QUERY_HEADS * HEAD_DIMENSION), jnp.float32), -4.0, 4.0)
    return base_offset.astype(jnp.bfloat16)


def draw_incoming_key_value(key, part):
    base_offset = jnp.clip(jax.random.normal(jax.random.fold_in(key, 43), (TOTAL_REQUESTS, 2 * KEY_VALUE_HEADS * HEAD_DIMENSION), jnp.float32), -4.0, 4.0)
    return base_offset.astype(jnp.bfloat16)


def draw_key_value_pool(key, part):
    base_offset = jnp.clip(jax.random.normal(jax.random.fold_in(key, 47), (TOTAL_BLOCKS, BLOCK_SLOTS, 2 * KEY_VALUE_HEADS * HEAD_DIMENSION), jnp.float32), -4.0, 4.0)
    return base_offset.astype(jnp.bfloat16)


def steps_of(stream_key, extent, shards, low, largest):
    level, own = 1.0, jax.random.fold_in(stream_key, 6)
    for dim, parts in shards:
        draws = jnp.exp(jax.random.uniform(jax.random.fold_in(own, dim), (parts,), jnp.float32, low / len(shards), largest / len(shards)))
        level = level * jnp.repeat(draws, extent[dim] // parts).reshape([-1 if axis == dim else 1 for axis in range(len(extent))])
    return level


def shared_out(stream_key, own, number, rows, number_of, top, bound, lean):
    sequence = jax.random.permutation(stream_key, number_of)
    heavy_load, common = shares(number_of, rows * top, bound, lean, True), shares(number_of, rows * top, bound, lean, False)
    places = jnp.arange(number_of)

    def named(tallies, offset_by):
        used = int((tallies > 0).sum())
        fixed = max(1, used // 4)
        shifted = fixed + (places - fixed + offset_by * (used - fixed)) % max(1, number_of - fixed)
        return jnp.zeros((number_of,), jnp.int32).at[sequence[jnp.where(places < fixed, places, shifted)]].set(jnp.asarray(tallies, jnp.int32))

    tallies = jnp.where(number % 4 == 0, named(heavy_load, number // 4), named(common, number - number // 4 - 1))
    mixed = jax.random.permutation(jax.random.fold_in(own, 3), number_of)
    source_of, taker = mixed[0:number_of // 2 * 2:2], mixed[1:number_of // 2 * 2:2]
    margin = jnp.minimum(tallies[source_of] - 1, bound - tallies[taker]) // 2
    margin = jnp.where((source_of == sequence[0]) | (taker == sequence[0]) | (tallies[taker] == 0), 0, jnp.maximum(margin, 0))
    shifted = jax.random.randint(jax.random.fold_in(own, 4), (number_of // 2,), 0, 1 << 20) % (margin + 1)
    tallies = tallies.at[source_of].add(-shifted).at[taker].add(shifted)
    members = jnp.searchsorted(jnp.cumsum(tallies), jnp.arange(rows * top), side="right").astype(jnp.int32)
    grid = members.reshape(top, rows).T
    grid = grid[jax.random.permutation(jax.random.fold_in(own, 1), rows)]
    offset_by = jax.random.randint(jax.random.fold_in(own, 2), (rows, 1), 0, top)
    return jnp.take_along_axis(grid, (jnp.arange(top)[None, :] + offset_by) % top, axis=1)


def shares(amount, total, limit, lean, full):
    weights = [(1 << 20) // math.isqrt(grade ** lean) + 1 for grade in range(1, amount + 1)]
    largest = limit if full else min(limit, max(-(-total // amount), total * weights[0] // sum(weights)))
    least = 1 if total - largest >= amount - 1 else 0
    holding, spare = [largest] + [least] * (amount - 1), total - largest - least * (amount - 1)
    while spare > 0:
        movable = [i for i in range(1, amount) if holding[i] < largest] or [i for i in range(1, amount) if holding[i] < limit]
        pool, left = sum([weights[i] for i in movable]), spare
        for i in movable:
            extra = min(limit - holding[i], max(1, left * weights[i] // pool), spare)
            holding[i] = holding[i] + extra
            spare = spare - extra
    return np.array(holding)


def normal_values(rng, shape, deviation, most, pieces=(), kind=jnp.bfloat16):
    level = steps_of(rng, shape, pieces, -0.22, 0.18) if pieces else 1.0
    array = jax.random.normal(rng, shape, jnp.float32) * deviation * level
    return jnp.minimum(jnp.maximum(array, -most), most).astype(kind)


def setup_inputs(seed: int = 0) -> dict:
    streams_of = jax.random.split(jax.random.key(seed), 12)
    moe_input = normal_values(streams_of[0], (TOKENS, D), 1.0, 6.0, ((0, 32),))
    expert_ids_keys = jax.random.split(jax.random.fold_in(streams_of[1], 1), TOKENS // TOK_DEV)
    expert_ids_turns = jax.random.permutation(jax.random.fold_in(streams_of[1], 3), TOKENS // TOK_DEV)
    expert_ids = jax.vmap(lambda own, number: shared_out(jax.random.fold_in(streams_of[1], 2), own, number, TOK_DEV, EXPERTS, TOP, CAP, 2))(expert_ids_keys, expert_ids_turns).reshape((TOKENS, TOP))
    route_weight = jnp.clip(jnp.exp(math.log(0.5) - 2.3025851 * jax.random.uniform(streams_of[2], (TOKENS, TOP), jnp.float32) ** steps_of(streams_of[2], (TOKENS, TOP), ((0, 32),), -0.2, 0.2)), 0.05, 0.5)
    expert_slot = jax.random.permutation(streams_of[3], EXPERTS).astype(jnp.int32)
    w_gate_up = normal_values(streams_of[4], (D, 2 * EXPERTS * FFE), D ** -0.5, 0.125, ((1, 32),))
    w_down = normal_values(streams_of[5], (EXPERTS * FFE, D), FFE ** -0.5, 0.21875, ((0, 32),))
    queries = draw_queries(jax.random.fold_in(streams_of[11], 71), 0)
    incoming_key_value = draw_incoming_key_value(jax.random.fold_in(streams_of[11], 71), 0)
    key_value_pool = draw_key_value_pool(jax.random.fold_in(streams_of[11], 71), 0)
    block_owner = draw_block_owner(jax.random.fold_in(streams_of[11], 71), 0)
    block_tokens = draw_block_tokens(jax.random.fold_in(streams_of[11], 71), 0)
    return dict(moe_input=moe_input, expert_ids=expert_ids, route_weight=route_weight, expert_slot=expert_slot, w_gate_up=w_gate_up, w_down=w_down, queries=queries, incoming_key_value=incoming_key_value, key_value_pool=key_value_pool, block_owner=block_owner, block_tokens=block_tokens)


HIGHEST = lax.Precision.HIGHEST

def mixture_reference(moe_input, expert_ids, route_weight, expert_slot, w_gate_up, w_down):
    devices = N_REPLICA * N_EXPERT
    quarter = FFE // QUART
    token_count = moe_input.shape[0]
    ids_by_device = expert_ids.reshape(devices, TOK_DEV * TOP)
    onehot = (ids_by_device[:, :, None] == jnp.arange(EXPERTS, dtype=jnp.int32)[None, None, :]).astype(jnp.int32)
    rank_before = jnp.cumsum(onehot, axis=1) - onehot
    position = lax.optimization_barrier(jnp.sum(rank_before * onehot, axis=2)).astype(jnp.int32)
    source = jnp.broadcast_to(jnp.arange(devices, dtype=jnp.int32)[:, None], ids_by_device.shape)
    token_index = source * TOK_DEV + jnp.arange(TOK_DEV * TOP, dtype=jnp.int32)[None, :] // TOP
    token_table = jnp.full((EXPERTS, devices, CAP), token_count, dtype=jnp.int32)
    token_table = token_table.at[ids_by_device, source, position].set(token_index)
    weight_table = jnp.zeros((EXPERTS, devices, CAP), jnp.float32)
    weight_table = weight_table.at[ids_by_device, source, position].set(route_weight.reshape(devices, TOK_DEV * TOP).astype(jnp.float32))
    hosted = jnp.zeros((EXPERTS,), jnp.int32).at[expert_slot].set(jnp.arange(EXPERTS, dtype=jnp.int32))
    padded = jnp.concatenate([moe_input, jnp.zeros((1, D), moe_input.dtype)], axis=0)
    gate_up_slots = w_gate_up.reshape(D, EXPERTS, QUART * 2 * quarter)
    down_slots = w_down.reshape(EXPERTS, QUART * quarter, D)

    def one_slot(running, slot_index):
        expert = hosted[slot_index]
        row_index = token_table[expert].reshape(-1)
        gathered = padded[row_index]
        halves = jnp.dot(gathered, gate_up_slots[:, slot_index, :], preferred_element_type=jnp.float32)
        halves = halves.reshape(-1, QUART, 2, quarter)
        activation = (jax.nn.silu(halves[:, :, 0]) * halves[:, :, 1]).astype(jnp.bfloat16)
        down_slot = down_slots[slot_index]
        output_sum = jnp.zeros((gathered.shape[0], D), jnp.float32)
        for quarter_id in range(QUART):
            quarter_part = jnp.dot(activation[:, quarter_id], down_slot[quarter_id * quarter:(quarter_id + 1) * quarter], preferred_element_type=jnp.float32).astype(jnp.bfloat16)
            output_sum = output_sum + quarter_part.astype(jnp.float32)
        scaled = output_sum * weight_table[expert].reshape(-1)[:, None]
        return (running.at[row_index].add(scaled), None)
    running = jnp.zeros((token_count + 1, D), jnp.float32)
    running, _ = lax.scan(one_slot, running, jnp.arange(EXPERTS, dtype=jnp.int32))
    return running[:token_count].astype(jnp.bfloat16)

def attention_reference(queries, incoming_key_value, key_value_pool, block_owner, block_tokens):
    query_group = QUERY_HEADS // KEY_VALUE_HEADS
    scale = 1.0 / math.sqrt(HEAD_DIMENSION)
    requests_per_column = N_REPLICA * DEVICE_REQUESTS
    block_pool = key_value_pool.reshape(N_REPLICA, N_EXPERT, DEVICE_BLOCKS, BLOCK_SLOTS, 2 * KEY_VALUE_HEADS * HEAD_DIMENSION)
    block_pool = jnp.transpose(block_pool, (1, 0, 2, 3, 4)).reshape(N_EXPERT, N_REPLICA * DEVICE_BLOCKS, BLOCK_SLOTS, 2 * KEY_VALUE_HEADS * HEAD_DIMENSION)
    owners = jnp.transpose(block_owner.reshape(N_REPLICA, N_EXPERT, DEVICE_BLOCKS), (1, 0, 2)).reshape(N_EXPERT, N_REPLICA * DEVICE_BLOCKS)
    counts = jnp.transpose(block_tokens.reshape(N_REPLICA, N_EXPERT, DEVICE_BLOCKS), (1, 0, 2)).reshape(N_EXPERT, N_REPLICA * DEVICE_BLOCKS)
    query_rows = jnp.transpose(queries.reshape(N_REPLICA, N_EXPERT, DEVICE_REQUESTS, QUERY_HEADS * HEAD_DIMENSION), (1, 0, 2, 3)).reshape(N_EXPERT, requests_per_column, KEY_VALUE_HEADS, query_group, HEAD_DIMENSION)
    latest_entry = jnp.transpose(incoming_key_value.reshape(N_REPLICA, N_EXPERT, DEVICE_REQUESTS, 2 * KEY_VALUE_HEADS * HEAD_DIMENSION), (1, 0, 2, 3)).reshape(N_EXPERT, requests_per_column, 2 * KEY_VALUE_HEADS * HEAD_DIMENSION)

    def one_column(inputs):
        block_pool_column, owner_column, count_column, query_column, latest_column = inputs
        cached_key_rows = block_pool_column[:, :, :KEY_VALUE_HEADS * HEAD_DIMENSION].reshape(-1, BLOCK_SLOTS, KEY_VALUE_HEADS, HEAD_DIMENSION).astype(jnp.float32)
        cached_value_rows = block_pool_column[:, :, KEY_VALUE_HEADS * HEAD_DIMENSION:].reshape(-1, BLOCK_SLOTS, KEY_VALUE_HEADS, HEAD_DIMENSION).astype(jnp.float32)
        query_f = query_column.astype(jnp.float32)
        incoming_keys = latest_column[:, :KEY_VALUE_HEADS * HEAD_DIMENSION].reshape(-1, KEY_VALUE_HEADS, HEAD_DIMENSION).astype(jnp.float32)
        incoming_values = latest_column[:, KEY_VALUE_HEADS * HEAD_DIMENSION:].reshape(-1, KEY_VALUE_HEADS, HEAD_DIMENSION).astype(jnp.float32)
        new_score = jnp.einsum('rgjd,rgd->rgj', query_f, incoming_keys, precision=HIGHEST) * scale
        block_query = query_f[owner_column]
        scores = jnp.einsum('bgjd,btgd->bgjt', block_query, cached_key_rows, precision=HIGHEST) * scale
        valid = jnp.arange(BLOCK_SLOTS, dtype=jnp.int32)[None, :] < count_column[:, None]
        block_top = lax.optimization_barrier(jnp.max(jnp.where(valid[:, None, None, :], scores, -jnp.inf), axis=3))
        member = owner_column[:, None] == jnp.arange(requests_per_column, dtype=jnp.int32)[None, :]
        request_top = lax.optimization_barrier(jnp.max(jnp.where(member[:, :, None, None], block_top[:, None, :, :], -jnp.inf), axis=0))
        best = jnp.maximum(request_top, new_score)
        weights = jnp.where(valid[:, None, None, :], jnp.exp(scores - best[owner_column][..., None]), 0.0)
        block_denom = lax.optimization_barrier(jnp.sum(weights, axis=3))
        block_sum = jnp.einsum('bgjt,btgd->bgjd', weights, cached_value_rows, precision=HIGHEST)
        member_f = member.astype(jnp.float32)
        own_weight = jnp.exp(new_score - best)
        denom = jnp.einsum('br,bgj->rgj', member_f, block_denom, precision=HIGHEST) + own_weight
        mixed = jnp.einsum('br,bgjd->rgjd', member_f, block_sum, precision=HIGHEST) + own_weight[..., None] * incoming_values[:, :, None, :]
        return (mixed / denom[..., None]).reshape(requests_per_column, QUERY_HEADS * HEAD_DIMENSION).astype(jnp.bfloat16)
    result = lax.map(one_column, (block_pool, owners, counts, query_rows, latest_entry))
    result = jnp.transpose(result.reshape(N_EXPERT, N_REPLICA, DEVICE_REQUESTS, QUERY_HEADS * HEAD_DIMENSION), (1, 0, 2, 3))
    return result.reshape(N_REPLICA * N_EXPERT * DEVICE_REQUESTS, QUERY_HEADS * HEAD_DIMENSION)

def reference(moe_input, expert_ids, route_weight, expert_slot, w_gate_up, w_down, queries, incoming_key_value, key_value_pool, block_owner, block_tokens):
    moe_out = mixture_reference(moe_input, expert_ids, route_weight, expert_slot, w_gate_up, w_down)
    attn_out = attention_reference(queries, incoming_key_value, key_value_pool, block_owner, block_tokens)
    return (moe_out, attn_out)
```

```python
import functools
import math

import jax
import jax.numpy as jnp
from jax import lax
from jax.experimental import pallas as pl
from jax.experimental.pallas import tpu as pltpu
from jax.sharding import PartitionSpec as P

QUART = 4
QUERY_HEADS = 64
KEY_VALUE_HEADS = 4
HEAD_DIMENSION = 128
DEVICE_REQUESTS = 2
DEVICE_BLOCKS = 16
BLOCK_SLOTS = 64
MIG = 2


HIGHEST = lax.Precision.HIGHEST


def partial_state(query_rows, rows, mask, scale):
    heads_kv = query_rows.shape[1]
    head_size = query_rows.shape[3]
    maxima = []
    totals = []
    weighted = []
    for head in range(heads_kv):
        cached_key_rows = rows[:, head * head_size : (head + 1) * head_size]
        cached_value_rows = rows[
            :, (heads_kv + head) * head_size : (heads_kv + head + 1) * head_size
        ].astype(jnp.float32)
        scores = (
            jnp.einsum(
                "rjd,nd->rjn",
                query_rows[:, head],
                cached_key_rows,
                preferred_element_type=jnp.float32,
            )
            * scale
        )
        keep = mask[:, None, :]
        largest = jnp.max(jnp.where(keep, scores, -1e30), axis=2)
        weights = jnp.where(keep, jnp.exp(scores - largest[:, :, None]), 0.0)
        maxima.append(largest)
        totals.append(jnp.sum(weights, axis=2))
        weighted.append(jnp.einsum("rjn,nd->rjd", weights, cached_value_rows, precision=HIGHEST))
    return (jnp.stack(maxima, 1), jnp.stack(totals, 1), jnp.stack(weighted, 1))


def finish(maxima, totals, weighted, new_score, incoming_values):
    best = jnp.maximum(jnp.max(maxima, axis=0), new_score)
    own_weight = jnp.exp(new_score - best)
    factor = jnp.exp(maxima - best[None])
    denom = own_weight + jnp.sum(factor * totals, axis=0)
    mixed = own_weight[..., None] * incoming_values + jnp.sum(factor[..., None] * weighted, axis=0)
    return mixed / denom[..., None]


def attend_migrate(query_rows, key_value_pool, block_owner, block_tokens, scale):
    replicas = lax.axis_size("replica")
    mine = lax.axis_index("replica")
    kv_width = key_value_pool.shape[2]
    target = block_owner // DEVICE_REQUESTS
    request = block_owner % DEVICE_REQUESTS
    leaving = target != mine
    to_replica = (
        (target[:, None] == jnp.arange(replicas, dtype=jnp.int32)[None, :]) & leaving[:, None]
    ).astype(jnp.int32)
    before = jnp.cumsum(to_replica, axis=0) - to_replica
    place = target * MIG + jnp.sum(before * to_replica, axis=1)
    select = (place[None, :] == jnp.arange(replicas * MIG, dtype=jnp.int32)[:, None]) & leaving[
        None, :
    ]
    chosen = select.astype(jnp.int32)
    send_blocks = jnp.dot(
        select.astype(jnp.bfloat16),
        key_value_pool.reshape(DEVICE_BLOCKS, BLOCK_SLOTS * kv_width),
        preferred_element_type=jnp.float32,
    ).astype(jnp.bfloat16)
    send_request = jnp.sum(chosen * request[None, :], axis=1)
    send_count = jnp.sum(chosen * block_tokens[None, :], axis=1)
    got_blocks, got_request, got_count = (
        lax.all_to_all(
            send_blocks.reshape(replicas, MIG, BLOCK_SLOTS * kv_width),
            "replica",
            split_axis=0,
            concat_axis=0,
            tiled=True,
        ),
        lax.all_to_all(
            send_request.reshape(replicas, MIG), "replica", split_axis=0, concat_axis=0, tiled=True
        ),
        lax.all_to_all(
            send_count.reshape(replicas, MIG), "replica", split_axis=0, concat_axis=0, tiled=True
        ),
    )
    positions = jnp.arange(BLOCK_SLOTS, dtype=jnp.int32)
    requests = jnp.arange(DEVICE_REQUESTS, dtype=jnp.int32)
    local_valid = (positions[None, :] < block_tokens[:, None]).reshape(-1)
    local_owner = jnp.repeat(block_owner, BLOCK_SLOTS)
    local_mask = (local_owner[None, :] == mine * DEVICE_REQUESTS + requests[:, None]) & local_valid[
        None, :
    ]
    local_state = partial_state(
        query_rows, key_value_pool.reshape(DEVICE_BLOCKS * BLOCK_SLOTS, kv_width), local_mask, scale
    )
    got_valid = (positions[None, :] < got_count.reshape(-1)[:, None]).reshape(-1)
    got_owner = jnp.repeat(got_request.reshape(-1), BLOCK_SLOTS)
    got_mask = (got_owner[None, :] == requests[:, None]) & got_valid[None, :]
    got_state = partial_state(query_rows, got_blocks.reshape(-1, kv_width), got_mask, scale)
    maxima = jnp.stack([local_state[0], got_state[0]], axis=0)
    totals = jnp.stack([local_state[1], got_state[1]], axis=0)
    weighted = jnp.stack([local_state[2], got_state[2]], axis=0)
    return (maxima, totals, weighted)


def expert_local(rows, w_gate_up, w_down):
    quarter = w_down.shape[0]
    halves = jnp.dot(rows, w_gate_up, preferred_element_type=jnp.float32)
    activation = (jax.nn.silu(halves[:, :quarter]) * halves[:, quarter:]).astype(jnp.bfloat16)
    return jnp.dot(activation, w_down, preferred_element_type=jnp.float32).astype(jnp.bfloat16)


def mixture(moe_input, expert_ids, route_weight, expert_slot, w_gate_up, w_down):
    token_rows = moe_input.shape[0]
    width = moe_input.shape[1]
    top_k = expert_ids.shape[1]
    experts = expert_slot.shape[0]
    replicas = lax.axis_size("replica")
    columns = lax.axis_size("expert")
    capacity = min(token_rows, max(2, 2 * token_rows * top_k // experts))
    flat_ids = expert_ids.reshape(-1)
    onehot = (flat_ids[:, None] == jnp.arange(experts, dtype=jnp.int32)[None, :]).astype(jnp.int32)
    before = jnp.cumsum(onehot, axis=0) - onehot
    position = jnp.sum(before * onehot, axis=1)
    slot_of = jnp.sum(onehot * expert_slot[None, :], axis=1)
    target = slot_of * capacity + position
    assign = (target[:, None] == jnp.arange(experts * capacity, dtype=jnp.int32)[None, :]).reshape(
        token_rows, top_k, experts * capacity
    )
    dispatch_map = jnp.sum(assign.astype(jnp.int32), axis=1).astype(jnp.bfloat16)
    send_rows = jnp.einsum(
        "tc,td->cd", dispatch_map, moe_input, preferred_element_type=jnp.float32
    ).astype(jnp.bfloat16)
    send = jnp.broadcast_to(
        send_rows.reshape(experts, 1, capacity, width), (experts, QUART, capacity, width)
    )
    send = send.reshape(replicas, columns, capacity, width)
    received = lax.all_to_all(
        lax.all_to_all(send, "replica", split_axis=0, concat_axis=0, tiled=True),
        "expert",
        split_axis=1,
        concat_axis=1,
        tiled=True,
    )
    quarter_part = expert_local(received.reshape(-1, width), w_gate_up, w_down)
    returned = lax.all_to_all(
        lax.all_to_all(
            quarter_part.reshape(send.shape), "replica", split_axis=0, concat_axis=0, tiled=True
        ),
        "expert",
        split_axis=1,
        concat_axis=1,
        tiled=True,
    )
    expert_out = jnp.sum(
        returned.reshape(experts, QUART, capacity, width).astype(jnp.float32), axis=1
    ).reshape(experts * capacity, width)
    mixing = jnp.sum(assign.astype(jnp.float32) * route_weight[:, :, None], axis=1)
    return jnp.dot(
        mixing, expert_out, precision=HIGHEST, preferred_element_type=jnp.float32
    ).astype(jnp.bfloat16)


CORES = 2
PAD = 128
MESH = pl.DeviceIdType.MESH


def fits_fused(expert_ids, expert_slot):
    experts = expert_slot.shape[0]
    devices = lax.axis_size("replica") * lax.axis_size("expert")
    return (
        expert_ids.shape[1] == experts
        and 3 * experts <= PAD
        and devices == experts * QUART
        and lax.axis_size("expert") % CORES == 0
    )


def fused_kernel(
    replicas,
    depth,
    experts,
    slot_ref,
    owner_ref,
    tokens_ref,
    x_ref,
    ids_ref,
    rw_ref,
    q_ref,
    new_ref,
    wgu_hbm,
    wd_hbm,
    kv_hbm,
    moe_ref,
    attn_ref,
    xb,
    wgu,
    wd,
    kv,
    pf,
    cs,
    cr,
    xs,
    xr,
    zf,
    zs,
    zr,
    qb,
    accf,
    accb,
    mlb,
    ar,
    mr,
    load_sem,
    z_send,
    z_recv,
    r_send,
    r_recv,
    c_send,
    c_recv,
    q_send,
    q_recv,
    cs_send,
    cs_recv,
    xs_send,
    xs_recv,
    zs_send,
    zs_recv,
    a_send,
    a_recv,
    m_send,
    m_recv,
):
    r = lax.axis_index("replica")
    e = lax.axis_index("expert")
    z = e // CORES
    c = e % CORES
    sib = 1 - c
    rows, width = x_ref.shape
    quarter = wd_hbm.shape[0]
    heads = KEY_VALUE_HEADS
    hd = HEAD_DIMENSION
    group = QUERY_HEADS // KEY_VALUE_HEADS
    per = DEVICE_REQUESTS * group
    scale = 1.0 / math.sqrt(HEAD_DIMENSION)
    sent = []

    def rdev(k):
        return ((r + k) % replicas, e)

    def zdev(k):
        return (r, ((z + k) % depth) * CORES + c)

    cdev = (r, z * CORES + sib)

    def remote(src, dst, ssem, rsem, dev):
        return pltpu.make_async_remote_copy(
            src_ref=src, dst_ref=dst, send_sem=ssem, recv_sem=rsem, device_id=dev, device_id_type=MESH
        )

    def push(*args):
        d = remote(*args)
        d.start()
        sent.append(d)

    loads = [
        pltpu.make_async_copy(wgu_hbm, wgu, load_sem.at[0]),
        pltpu.make_async_copy(wd_hbm, wd, load_sem.at[1]),
        pltpu.make_async_copy(kv_hbm, kv, load_sem.at[2]),
    ]
    for d in loads:
        d.start()

    barrier = pltpu.get_barrier_semaphore()
    for k in range(1, replicas):
        pl.semaphore_signal(barrier, inc=1, device_id=rdev(k), device_id_type=MESH)
    for k in range(1, depth):
        pl.semaphore_signal(barrier, inc=1, device_id=zdev(k), device_id_type=MESH)
    pl.semaphore_signal(barrier, inc=1, device_id=cdev, device_id_type=MESH)

    lane = lax.broadcasted_iota(jnp.int32, (rows, PAD), 1)
    mix = jnp.zeros((rows, PAD), jnp.float32)
    for k in range(experts):
        chosen = ids_ref[:, k : k + 1]
        slot = jnp.zeros((rows, 1), jnp.int32)
        for n in range(experts):
            slot = jnp.where(chosen == n, slot_ref[n], slot)
        mix = mix + jnp.where(lane % experts == slot, rw_ref[:, k : k + 1], 0.0)
    high = mix.astype(jnp.bfloat16).astype(jnp.float32)
    rest = mix - high
    mid = rest.astype(jnp.bfloat16).astype(jnp.float32)
    low = rest - mid
    terms = jnp.where(lane < experts, high, jnp.where(lane < 2 * experts, mid, low))
    xb[z, c, r, :, :width] = x_ref[...]
    xb[z, c, r, :, width:] = terms.astype(jnp.bfloat16)
    qb[r] = q_ref[...]

    pl.semaphore_wait(barrier, replicas - 1 + depth - 1 + 1)

    def xy_out(zo):
        piece = xb.at[(z + depth - zo) % depth, c, r]
        for k in range(1, replicas):
            push(piece, piece, r_send.at[zo, k], r_recv.at[zo, k], rdev(k))

    def core_out(zo, k):
        piece = xb.at[(z + depth - zo) % depth, c, (r + replicas - k) % replicas]
        push(piece, piece, c_send.at[zo, k], c_recv.at[zo, k], cdev)

    own = xb.at[z, c, r]
    for k in range(1, depth):
        push(own, own, z_send.at[k], z_recv.at[k], zdev(k))
    for k in range(1, replicas):
        push(qb.at[r], qb.at[r], q_send.at[k], q_recv.at[k], rdev(k))
    xy_out(0)
    core_out(0, 0)
    for zo in range(1, depth):
        got = xb.at[(z + depth - zo) % depth, c, r]
        remote(got, got, z_send.at[zo], z_recv.at[zo], cdev).wait_recv()
        xy_out(zo)
        core_out(zo, 0)

    for k in range(1, replicas):
        got = qb.at[(r + replicas - k) % replicas]
        remote(got, got, q_send.at[k], q_recv.at[k], cdev).wait_recv()
    loads[2].wait()
    blocks, slots = owner_ref.shape[0], kv.shape[0] // owner_ref.shape[0]
    keys = kv.shape[0]
    place = lax.broadcasted_iota(jnp.int32, (1, keys), 1)
    holder = jnp.full((1, keys), -1, jnp.int32)
    for b in range(blocks):
        inside = (place >= b * slots) & (place < b * slots + tokens_ref[b])
        holder = jnp.where(inside, owner_ref[b], holder)
    total = replicas * per
    asker = lax.broadcasted_iota(jnp.int32, (total, 1), 0) // group
    keep = holder == asker
    mlane = lax.broadcasted_iota(jnp.int32, (total, PAD), 1)

    def head(g, ml):
        col = pl.ds(pl.multiple_of(g * hd, hd), hd)
        vcol = pl.ds(pl.multiple_of((heads + g) * hd, hd), hd)
        qg = qb[:, pl.ds(pl.multiple_of(g * per, per), per), :].reshape(total, hd)
        scores = (
            lax.dot_general(
                qg, kv[:, col], (((1,), (1,)), ((), ())), preferred_element_type=jnp.float32
            )
            * scale
        )
        top = jnp.max(jnp.where(keep, scores, -1e30), axis=1, keepdims=True)
        weights = jnp.where(keep, jnp.exp(scores - top), 0.0)
        mass = jnp.sum(weights, axis=1, keepdims=True)
        acc = jnp.dot(
            weights.astype(jnp.bfloat16), kv[:, vcol], preferred_element_type=jnp.float32
        ).reshape(replicas, per, hd)
        accf[:, g] = acc
        accb[:, g] = acc.astype(jnp.bfloat16)
        return jnp.where(mlane == g, top, jnp.where(mlane == heads + g, mass, ml))

    ml = lax.fori_loop(0, heads, head, jnp.zeros((total, PAD), jnp.float32))
    mlb[...] = ml.reshape(replicas, per, PAD)
    for k in range(1, replicas):
        to = (r + k) % replicas
        push(accb.at[to], ar.at[k], a_send.at[k], a_recv.at[k], rdev(k))
        push(mlb.at[to], mr.at[k], m_send.at[k], m_recv.at[k], rdev(k))

    def finish_attention():
        for k in range(1, replicas):
            remote(ar.at[k], ar.at[k], a_send.at[k], a_recv.at[k], cdev).wait_recv()
            remote(mr.at[k], mr.at[k], m_send.at[k], m_recv.at[k], cdev).wait_recv()
        plane = lax.broadcasted_iota(jnp.int32, (per, PAD), 1)
        mls = [mlb[r]] + [mr[k] for k in range(1, replicas)]

        def pick(values, n):
            return jnp.sum(jnp.where(plane == n, values, 0.0), axis=1, keepdims=True)

        def spread(n):
            pieces = [
                jnp.broadcast_to(
                    new_ref[i : i + 1, n * hd : (n + 1) * hd].astype(jnp.float32), (group, hd)
                )
                for i in range(DEVICE_REQUESTS)
            ]
            return jnp.concatenate(pieces, axis=0)

        for g in range(heads):
            query = q_ref[g * per : (g + 1) * per, :].astype(jnp.float32)
            fresh = jnp.sum(query * spread(g), axis=1, keepdims=True) * scale
            tops = [pick(v, g) for v in mls]
            best = fresh
            for t in tops:
                best = jnp.maximum(best, t)
            weight = jnp.exp(fresh - best)
            denom = weight
            mixed = weight * spread(heads + g)
            for k in range(replicas):
                factor = jnp.exp(tops[k] - best)
                part = accf[r, g] if k == 0 else ar[k, g].astype(jnp.float32)
                denom = denom + factor * pick(mls[k], heads + g)
                mixed = mixed + factor * part
            attn_ref[g * per : (g + 1) * per, :] = (mixed / denom).astype(attn_ref.dtype)

    my_slot = (r * (depth * CORES) + e) // QUART
    chunk = CORES * replicas * rows
    slane = lax.broadcasted_iota(jnp.int32, (chunk, PAD), 1)
    mine = (slane % experts == my_slot) & (slane < 3 * experts)

    def gather(zo):
        for k in range(1, replicas):
            got = xb.at[(z + depth - zo) % depth, c, (r + replicas - k) % replicas]
            remote(got, got, r_send.at[zo, k], r_recv.at[zo, k], cdev).wait_recv()
            core_out(zo, k)

    def expert(zo):
        zi = (z + depth - zo) % depth
        for k in range(replicas):
            got = xb.at[zi, sib, (r + replicas - k) % replicas]
            remote(got, got, c_send.at[zo, k], c_recv.at[zo, k], cdev).wait_recv()
        block = xb[zi].reshape(chunk, width + PAD)
        gain = jnp.sum(
            jnp.where(mine, block[:, width:].astype(jnp.float32), 0.0), axis=1, keepdims=True
        )
        halves = jnp.dot(block[:, :width], wgu[...], preferred_element_type=jnp.float32)
        gate, up = halves[:, :quarter], halves[:, quarter:]
        act = (gate / (1.0 + jnp.exp(-gate)) * up).astype(jnp.bfloat16)
        step = width // 4
        for n in range(4):
            cols = slice(n * step, (n + 1) * step)
            part = jnp.dot(act, wd[:, cols], preferred_element_type=jnp.float32) * gain
            part = part.reshape(CORES, replicas * rows, step)
            pf[zo, :, :, cols] = part
            cs[zo, :, :, cols] = part.astype(jnp.bfloat16)
        push(cs.at[zo, sib], cr.at[zo], cs_send.at[zo], cs_recv.at[zo], cdev)

    def across(zo):
        remote(cr.at[zo], cr.at[zo], cs_send.at[zo], cs_recv.at[zo], cdev).wait_recv()
        both = pf[zo, c] + cr[zo].astype(jnp.float32)
        pf[zo, c] = both
        xs[zo] = both.astype(jnp.bfloat16).reshape(replicas, rows, width)
        for k in range(1, replicas):
            to = (r + k) % replicas
            push(xs.at[zo, to], xr.at[zo, k], xs_send.at[zo, k], xs_recv.at[zo, k], rdev(k))

    def along(zo):
        total = pf[zo, c, pl.ds(pl.multiple_of(r * rows, rows), rows), :]
        for k in range(1, replicas):
            remote(
                xr.at[zo, k], xr.at[zo, k], xs_send.at[zo, k], xs_recv.at[zo, k], cdev
            ).wait_recv()
            total = total + xr[zo, k].astype(jnp.float32)
        if zo == 0:
            zf[...] = total
        else:
            zs[zo] = total.astype(jnp.bfloat16)
            push(zs.at[zo], zr.at[zo], zs_send.at[zo], zs_recv.at[zo], zdev(depth - zo))

    gather(0)
    loads[0].wait()
    loads[1].wait()
    for zo in range(depth):
        expert(zo)
        if zo >= 1:
            across(zo - 1)
        if zo + 1 < depth:
            gather(zo + 1)
        if zo >= 2:
            along(zo - 2)
    across(depth - 1)
    finish_attention()
    if depth >= 2:
        along(depth - 2)
    along(depth - 1)
    result = zf[...]
    for zo in range(1, depth):
        remote(zr.at[zo], zr.at[zo], zs_send.at[zo], zs_recv.at[zo], cdev).wait_recv()
        result = result + zr[zo].astype(jnp.float32)
    moe_ref[...] = result.astype(moe_ref.dtype)
    for d in sent:
        d.wait_send()


def fused(
    moe_input,
    expert_ids,
    route_weight,
    expert_slot,
    w_gate_up,
    w_down,
    queries,
    incoming_key_value,
    key_value_pool,
    block_owner,
    block_tokens,
):
    replicas = lax.axis_size("replica")
    depth = lax.axis_size("expert") // CORES
    experts = expert_slot.shape[0]
    rows, width = moe_input.shape
    group = QUERY_HEADS // KEY_VALUE_HEADS
    per = DEVICE_REQUESTS * group
    hd = HEAD_DIMENSION
    keys = key_value_pool.shape[0] * key_value_pool.shape[1]
    q = (
        queries.reshape(DEVICE_REQUESTS, KEY_VALUE_HEADS, group, hd)
        .transpose(1, 0, 2, 3)
        .reshape(KEY_VALUE_HEADS * per, hd)
    )
    smem = pl.BlockSpec(memory_space=pltpu.SMEM)
    vmem = pl.BlockSpec(memory_space=pltpu.VMEM)
    hbm = pl.BlockSpec(memory_space=pl.ANY)
    bf, f32 = jnp.bfloat16, jnp.float32
    dma = pltpu.SemaphoreType.DMA
    moe_out, attn = pl.pallas_call(
        functools.partial(fused_kernel, replicas, depth, experts),
        out_shape=(
            jax.ShapeDtypeStruct((rows, width), bf),
            jax.ShapeDtypeStruct((KEY_VALUE_HEADS * per, hd), bf),
        ),
        in_specs=[smem] * 3 + [vmem] * 5 + [hbm] * 3,
        out_specs=(vmem, vmem),
        scratch_shapes=[
            pltpu.VMEM((depth, CORES, replicas, rows, width + PAD), bf),
            pltpu.VMEM(w_gate_up.shape, bf),
            pltpu.VMEM(w_down.shape, bf),
            pltpu.VMEM((keys, key_value_pool.shape[2]), bf),
            pltpu.VMEM((depth, CORES, replicas * rows, width), f32),
            pltpu.VMEM((depth, CORES, replicas * rows, width), bf),
            pltpu.VMEM((depth, replicas * rows, width), bf),
            pltpu.VMEM((depth, replicas, rows, width), bf),
            pltpu.VMEM((depth, replicas, rows, width), bf),
            pltpu.VMEM((rows, width), f32),
            pltpu.VMEM((depth, rows, width), bf),
            pltpu.VMEM((depth, rows, width), bf),
            pltpu.VMEM((replicas, KEY_VALUE_HEADS * per, hd), bf),
            pltpu.VMEM((replicas, KEY_VALUE_HEADS, per, hd), f32),
            pltpu.VMEM((replicas, KEY_VALUE_HEADS, per, hd), bf),
            pltpu.VMEM((replicas, per, PAD), f32),
            pltpu.VMEM((replicas, KEY_VALUE_HEADS, per, hd), bf),
            pltpu.VMEM((replicas, per, PAD), f32),
            dma((3,)),
            dma((depth,)),
            dma((depth,)),
            dma((depth, replicas)),
            dma((depth, replicas)),
            dma((depth, replicas)),
            dma((depth, replicas)),
            dma((replicas,)),
            dma((replicas,)),
            dma((depth,)),
            dma((depth,)),
            dma((depth, replicas)),
            dma((depth, replicas)),
            dma((depth,)),
            dma((depth,)),
            dma((replicas,)),
            dma((replicas,)),
            dma((replicas,)),
            dma((replicas,)),
        ],
        compiler_params=pltpu.CompilerParams(
            collective_id=0, has_side_effects=True, vmem_limit_bytes=48 * 1024 * 1024
        ),
    )(
        expert_slot,
        block_owner,
        block_tokens,
        moe_input,
        expert_ids,
        route_weight,
        q,
        incoming_key_value,
        w_gate_up,
        w_down,
        key_value_pool.reshape(keys, key_value_pool.shape[2]),
    )
    attn_out = (
        attn.reshape(KEY_VALUE_HEADS, DEVICE_REQUESTS, group, hd)
        .transpose(1, 0, 2, 3)
        .reshape(DEVICE_REQUESTS, QUERY_HEADS * hd)
    )
    return (moe_out, attn_out)


def shards(
    moe_input,
    expert_ids,
    route_weight,
    expert_slot,
    w_gate_up,
    w_down,
    queries,
    incoming_key_value,
    key_value_pool,
    block_owner,
    block_tokens,
):
    if fits_fused(expert_ids, expert_slot):
        return fused(
            moe_input,
            expert_ids,
            route_weight,
            expert_slot,
            w_gate_up,
            w_down,
            queries,
            incoming_key_value,
            key_value_pool,
            block_owner,
            block_tokens,
        )
    moe_out = mixture(moe_input, expert_ids, route_weight, expert_slot, w_gate_up, w_down)
    scale = 1.0 / math.sqrt(HEAD_DIMENSION)
    query_rows = queries.reshape(
        DEVICE_REQUESTS, KEY_VALUE_HEADS, QUERY_HEADS // KEY_VALUE_HEADS, HEAD_DIMENSION
    )
    latest_keys = incoming_key_value[:, : KEY_VALUE_HEADS * HEAD_DIMENSION].reshape(
        DEVICE_REQUESTS, KEY_VALUE_HEADS, HEAD_DIMENSION
    )
    new_score = (
        jnp.einsum("rgjd,rgd->rgj", query_rows, latest_keys, preferred_element_type=jnp.float32)
        * scale
    )
    incoming_values = (
        incoming_key_value[:, KEY_VALUE_HEADS * HEAD_DIMENSION :]
        .reshape(DEVICE_REQUESTS, KEY_VALUE_HEADS, 1, HEAD_DIMENSION)
        .astype(jnp.float32)
    )
    maxima, totals, weighted = attend_migrate(
        query_rows, key_value_pool, block_owner, block_tokens, scale
    )
    attn_out = (
        finish(maxima, totals, weighted, new_score, incoming_values)
        .reshape(DEVICE_REQUESTS, QUERY_HEADS * HEAD_DIMENSION)
        .astype(jnp.bfloat16)
    )
    return (moe_out, attn_out)


def solution(mesh):
    placed = (
        P(("replica", "expert"), None),
        P(("replica", "expert"), None),
        P(("replica", "expert"), None),
        P(),
        P(None, ("replica", "expert")),
        P(("replica", "expert"), None),
        P(("replica", "expert"), None),
        P(("replica", "expert"), None),
        P(("replica", "expert"), None, None),
        P(("replica", "expert")),
        P(("replica", "expert")),
    )
    return jax.shard_map(
        shards,
        mesh=mesh,
        in_specs=placed,
        out_specs=(P(("replica", "expert"), None), P(("replica", "expert"), None)),
        check_vma=False,
    )
```

```python
import functools
import math

import jax
import jax.numpy as jnp
from jax import lax
from jax.experimental import pallas as pl
from jax.experimental.pallas import tpu as pltpu
from jax.sharding import PartitionSpec as P

QUART = 4
QUERY_HEADS = 64
KEY_VALUE_HEADS = 4
HEAD_DIMENSION = 128
DEVICE_REQUESTS = 2
DEVICE_BLOCKS = 16
BLOCK_SLOTS = 64
MIG = 2


HIGHEST = lax.Precision.HIGHEST


def partial_state(query_rows, rows, mask, scale):
    heads_kv = query_rows.shape[1]
    head_size = query_rows.shape[3]
    maxima = []
    totals = []
    weighted = []
    for head in range(heads_kv):
        cached_key_rows = rows[:, head * head_size : (head + 1) * head_size]
        cached_value_rows = rows[
            :, (heads_kv + head) * head_size : (heads_kv + head + 1) * head_size
        ].astype(jnp.float32)
        scores = (
            jnp.einsum(
                "rjd,nd->rjn",
                query_rows[:, head],
                cached_key_rows,
                preferred_element_type=jnp.float32,
            )
            * scale
        )
        keep = mask[:, None, :]
        largest = jnp.max(jnp.where(keep, scores, -1e30), axis=2)
        weights = jnp.where(keep, jnp.exp(scores - largest[:, :, None]), 0.0)
        maxima.append(largest)
        totals.append(jnp.sum(weights, axis=2))
        weighted.append(jnp.einsum("rjn,nd->rjd", weights, cached_value_rows, precision=HIGHEST))
    return (jnp.stack(maxima, 1), jnp.stack(totals, 1), jnp.stack(weighted, 1))


def finish(maxima, totals, weighted, new_score, incoming_values):
    best = jnp.maximum(jnp.max(maxima, axis=0), new_score)
    own_weight = jnp.exp(new_score - best)
    factor = jnp.exp(maxima - best[None])
    denom = own_weight + jnp.sum(factor * totals, axis=0)
    mixed = own_weight[..., None] * incoming_values + jnp.sum(factor[..., None] * weighted, axis=0)
    return mixed / denom[..., None]


def attend_migrate(query_rows, key_value_pool, block_owner, block_tokens, scale):
    replicas = lax.axis_size("replica")
    mine = lax.axis_index("replica")
    kv_width = key_value_pool.shape[2]
    target = block_owner // DEVICE_REQUESTS
    request = block_owner % DEVICE_REQUESTS
    leaving = target != mine
    to_replica = (
        (target[:, None] == jnp.arange(replicas, dtype=jnp.int32)[None, :]) & leaving[:, None]
    ).astype(jnp.int32)
    before = jnp.cumsum(to_replica, axis=0) - to_replica
    place = target * MIG + jnp.sum(before * to_replica, axis=1)
    select = (place[None, :] == jnp.arange(replicas * MIG, dtype=jnp.int32)[:, None]) & leaving[
        None, :
    ]
    chosen = select.astype(jnp.int32)
    send_blocks = jnp.dot(
        select.astype(jnp.bfloat16),
        key_value_pool.reshape(DEVICE_BLOCKS, BLOCK_SLOTS * kv_width),
        preferred_element_type=jnp.float32,
    ).astype(jnp.bfloat16)
    send_request = jnp.sum(chosen * request[None, :], axis=1)
    send_count = jnp.sum(chosen * block_tokens[None, :], axis=1)
    got_blocks, got_request, got_count = (
        lax.all_to_all(
            send_blocks.reshape(replicas, MIG, BLOCK_SLOTS * kv_width),
            "replica",
            split_axis=0,
            concat_axis=0,
            tiled=True,
        ),
        lax.all_to_all(
            send_request.reshape(replicas, MIG), "replica", split_axis=0, concat_axis=0, tiled=True
        ),
        lax.all_to_all(
            send_count.reshape(replicas, MIG), "replica", split_axis=0, concat_axis=0, tiled=True
        ),
    )
    positions = jnp.arange(BLOCK_SLOTS, dtype=jnp.int32)
    requests = jnp.arange(DEVICE_REQUESTS, dtype=jnp.int32)
    local_valid = (positions[None, :] < block_tokens[:, None]).reshape(-1)
    local_owner = jnp.repeat(block_owner, BLOCK_SLOTS)
    local_mask = (local_owner[None, :] == mine * DEVICE_REQUESTS + requests[:, None]) & local_valid[
        None, :
    ]
    local_state = partial_state(
        query_rows, key_value_pool.reshape(DEVICE_BLOCKS * BLOCK_SLOTS, kv_width), local_mask, scale
    )
    got_valid = (positions[None, :] < got_count.reshape(-1)[:, None]).reshape(-1)
    got_owner = jnp.repeat(got_request.reshape(-1), BLOCK_SLOTS)
    got_mask = (got_owner[None, :] == requests[:, None]) & got_valid[None, :]
    got_state = partial_state(query_rows, got_blocks.reshape(-1, kv_width), got_mask, scale)
    maxima = jnp.stack([local_state[0], got_state[0]], axis=0)
    totals = jnp.stack([local_state[1], got_state[1]], axis=0)
    weighted = jnp.stack([local_state[2], got_state[2]], axis=0)
    return (maxima, totals, weighted)


def expert_local(rows, w_gate_up, w_down):
    quarter = w_down.shape[0]
    halves = jnp.dot(rows, w_gate_up, preferred_element_type=jnp.float32)
    activation = (jax.nn.silu(halves[:, :quarter]) * halves[:, quarter:]).astype(jnp.bfloat16)
    return jnp.dot(activation, w_down, preferred_element_type=jnp.float32).astype(jnp.bfloat16)


def mixture(moe_input, expert_ids, route_weight, expert_slot, w_gate_up, w_down):
    token_rows = moe_input.shape[0]
    width = moe_input.shape[1]
    top_k = expert_ids.shape[1]
    experts = expert_slot.shape[0]
    replicas = lax.axis_size("replica")
    columns = lax.axis_size("expert")
    capacity = min(token_rows, max(2, 2 * token_rows * top_k // experts))
    flat_ids = expert_ids.reshape(-1)
    onehot = (flat_ids[:, None] == jnp.arange(experts, dtype=jnp.int32)[None, :]).astype(jnp.int32)
    before = jnp.cumsum(onehot, axis=0) - onehot
    position = jnp.sum(before * onehot, axis=1)
    slot_of = jnp.sum(onehot * expert_slot[None, :], axis=1)
    target = slot_of * capacity + position
    assign = (target[:, None] == jnp.arange(experts * capacity, dtype=jnp.int32)[None, :]).reshape(
        token_rows, top_k, experts * capacity
    )
    dispatch_map = jnp.sum(assign.astype(jnp.int32), axis=1).astype(jnp.bfloat16)
    send_rows = jnp.einsum(
        "tc,td->cd", dispatch_map, moe_input, preferred_element_type=jnp.float32
    ).astype(jnp.bfloat16)
    send = jnp.broadcast_to(
        send_rows.reshape(experts, 1, capacity, width), (experts, QUART, capacity, width)
    )
    send = send.reshape(replicas, columns, capacity, width)
    received = lax.all_to_all(
        lax.all_to_all(send, "replica", split_axis=0, concat_axis=0, tiled=True),
        "expert",
        split_axis=1,
        concat_axis=1,
        tiled=True,
    )
    quarter_part = expert_local(received.reshape(-1, width), w_gate_up, w_down)
    returned = lax.all_to_all(
        lax.all_to_all(
            quarter_part.reshape(send.shape), "replica", split_axis=0, concat_axis=0, tiled=True
        ),
        "expert",
        split_axis=1,
        concat_axis=1,
        tiled=True,
    )
    expert_out = jnp.sum(
        returned.reshape(experts, QUART, capacity, width).astype(jnp.float32), axis=1
    ).reshape(experts * capacity, width)
    mixing = jnp.sum(assign.astype(jnp.float32) * route_weight[:, :, None], axis=1)
    return jnp.dot(
        mixing, expert_out, precision=HIGHEST, preferred_element_type=jnp.float32
    ).astype(jnp.bfloat16)


CORES = 2
PAD = 128
VMEM_LIMIT = 60 * 1024 * 1024
MESH = pl.DeviceIdType.MESH


def fits_fused(expert_ids, expert_slot):
    experts = expert_slot.shape[0]
    devices = lax.axis_size("replica") * lax.axis_size("expert")
    return (
        expert_ids.shape[1] == experts
        and 3 * experts <= PAD
        and devices == experts * QUART
        and lax.axis_size("expert") % CORES == 0
    )


def fused_kernel(
    replicas,
    depth,
    experts,
    slot_ref,
    owner_ref,
    tokens_ref,
    ids_ref,
    rw_ref,
    q_ref,
    new_ref,
    x_hbm,
    wgu_hbm,
    wd_hbm,
    kv_hbm,
    moe_ref,
    attn_ref,
    xb,
    wgu,
    wd,
    kv,
    pf,
    cs,
    cr,
    xs,
    xr,
    zf,
    zs,
    zr,
    qb,
    accf,
    accb,
    mlb,
    ar,
    mr,
    load_sem,
    z_send,
    z_recv,
    r_send,
    r_recv,
    c_send,
    c_recv,
    q_send,
    q_recv,
    cs_send,
    cs_recv,
    xs_send,
    xs_recv,
    zs_send,
    zs_recv,
    a_send,
    a_recv,
    m_send,
    m_recv,
):
    r = lax.axis_index("replica")
    e = lax.axis_index("expert")
    z = e // CORES
    c = e % CORES
    sib = 1 - c
    rows, width = x_hbm.shape
    quarter = wd_hbm.shape[0]
    heads = KEY_VALUE_HEADS
    hd = HEAD_DIMENSION
    group = QUERY_HEADS // KEY_VALUE_HEADS
    per = DEVICE_REQUESTS * group
    scale = 1.0 / math.sqrt(HEAD_DIMENSION)
    sent = []

    def rdev(k):
        return ((r + k) % replicas, e)

    def zdev(k):
        return (r, ((z + k) % depth) * CORES + c)

    cdev = (r, z * CORES + sib)

    def remote(src, dst, ssem, rsem, dev):
        return pltpu.make_async_remote_copy(
            src_ref=src, dst_ref=dst, send_sem=ssem, recv_sem=rsem, device_id=dev, device_id_type=MESH
        )

    def push(*args):
        d = remote(*args)
        d.start()
        sent.append(d)

    loads = [
        pltpu.make_async_copy(wgu_hbm, wgu, load_sem.at[0]),
        pltpu.make_async_copy(wd_hbm, wd, load_sem.at[1]),
        pltpu.make_async_copy(kv_hbm, kv, load_sem.at[2]),
        pltpu.make_async_copy(x_hbm, xb.at[z, c, r, :, pl.ds(0, width)], load_sem.at[3]),
    ]
    for d in loads:
        d.start()

    barrier = pltpu.get_barrier_semaphore()
    for k in range(1, replicas):
        pl.semaphore_signal(barrier, inc=1, device_id=rdev(k), device_id_type=MESH)
    for k in range(1, depth):
        pl.semaphore_signal(barrier, inc=1, device_id=zdev(k), device_id_type=MESH)
    pl.semaphore_signal(barrier, inc=1, device_id=cdev, device_id_type=MESH)

    line = lax.broadcasted_iota(jnp.int32, (PAD, rows), 0)
    mix = jnp.zeros((PAD, rows), jnp.float32)
    for k in range(experts):
        chosen = ids_ref[k : k + 1, :]
        slot = jnp.zeros((1, rows), jnp.int32)
        for n in range(experts):
            slot = jnp.where(chosen == n, slot_ref[n], slot)
        mix = mix + jnp.where(line % experts == slot, rw_ref[k : k + 1, :], 0.0)
    high = mix.astype(jnp.bfloat16).astype(jnp.float32)
    rest = mix - high
    mid = rest.astype(jnp.bfloat16).astype(jnp.float32)
    low = rest - mid
    terms = jnp.where(line < experts, high, jnp.where(line < 2 * experts, mid, low))
    unit = (
        lax.broadcasted_iota(jnp.int32, (rows, rows), 0)
        == lax.broadcasted_iota(jnp.int32, (rows, rows), 1)
    ).astype(jnp.bfloat16)
    xb[z, c, r, :, width:] = lax.dot_general(
        unit,
        terms.astype(jnp.bfloat16),
        (((1,), (1,)), ((), ())),
        preferred_element_type=jnp.float32,
    ).astype(jnp.bfloat16)
    asked = q_ref[...].astype(jnp.float32)
    for g in range(heads):
        pieces = [asked[:, (g * group + j) * hd : (g * group + j + 1) * hd] for j in range(group)]
        qb[r, g * per : (g + 1) * per, :] = jnp.concatenate(pieces, axis=0).astype(jnp.bfloat16)
    loads[3].wait()

    pl.semaphore_wait(barrier, replicas - 1 + depth - 1 + 1)

    def xy_out(zo):
        piece = xb.at[(z + depth - zo) % depth, c, r]
        for k in range(1, replicas):
            push(piece, piece, r_send.at[zo, k], r_recv.at[zo, k], rdev(k))

    def core_out(zo, k):
        piece = xb.at[(z + depth - zo) % depth, c, (r + replicas - k) % replicas]
        push(piece, piece, c_send.at[zo, k], c_recv.at[zo, k], cdev)

    own = xb.at[z, c, r]
    for k in range(1, depth):
        push(own, own, z_send.at[k], z_recv.at[k], zdev(k))
    for k in range(1, replicas):
        push(qb.at[r], qb.at[r], q_send.at[k], q_recv.at[k], rdev(k))
    xy_out(0)
    core_out(0, 0)
    for zo in range(1, depth):
        got = xb.at[(z + depth - zo) % depth, c, r]
        remote(got, got, z_send.at[zo], z_recv.at[zo], cdev).wait_recv()
        xy_out(zo)
        core_out(zo, 0)

    for k in range(1, replicas):
        got = qb.at[(r + replicas - k) % replicas]
        remote(got, got, q_send.at[k], q_recv.at[k], cdev).wait_recv()
    loads[2].wait()
    blocks, slots = owner_ref.shape[0], kv.shape[0] // owner_ref.shape[0]
    keys = kv.shape[0]
    place = lax.broadcasted_iota(jnp.int32, (1, keys), 1)
    holder = jnp.full((1, keys), -1, jnp.int32)
    for b in range(blocks):
        inside = (place >= b * slots) & (place < b * slots + tokens_ref[b])
        holder = jnp.where(inside, owner_ref[b], holder)
    total = replicas * per
    row = lax.broadcasted_iota(jnp.int32, (total, 1), 0)
    asker = row // per * DEVICE_REQUESTS + row % DEVICE_REQUESTS
    keep = holder == asker
    mlane = lax.broadcasted_iota(jnp.int32, (total, PAD), 1)

    def head(g, ml):
        col = pl.ds(pl.multiple_of(g * hd, hd), hd)
        vcol = pl.ds(pl.multiple_of((heads + g) * hd, hd), hd)
        qg = qb[:, pl.ds(pl.multiple_of(g * per, per), per), :].reshape(total, hd)
        scores = (
            lax.dot_general(
                qg, kv[:, col], (((1,), (1,)), ((), ())), preferred_element_type=jnp.float32
            )
            * scale
        )
        top = jnp.max(jnp.where(keep, scores, -1e30), axis=1, keepdims=True)
        weights = jnp.where(keep, jnp.exp(scores - top), 0.0)
        mass = jnp.sum(weights, axis=1, keepdims=True)
        acc = jnp.dot(
            weights.astype(jnp.bfloat16), kv[:, vcol], preferred_element_type=jnp.float32
        ).reshape(replicas, per, hd)
        accf[:, g] = acc
        accb[:, g] = acc.astype(jnp.bfloat16)
        return jnp.where(mlane == g, top, jnp.where(mlane == heads + g, mass, ml))

    ml = lax.fori_loop(0, heads, head, jnp.zeros((total, PAD), jnp.float32))
    mlb[...] = ml.reshape(replicas, per, PAD)
    for k in range(1, replicas):
        to = (r + k) % replicas
        push(accb.at[to], ar.at[k], a_send.at[k], a_recv.at[k], rdev(k))
        push(mlb.at[to], mr.at[k], m_send.at[k], m_recv.at[k], rdev(k))

    def finish_attention():
        for k in range(1, replicas):
            remote(ar.at[k], ar.at[k], a_send.at[k], a_recv.at[k], cdev).wait_recv()
            remote(mr.at[k], mr.at[k], m_send.at[k], m_recv.at[k], cdev).wait_recv()
        plane = lax.broadcasted_iota(jnp.int32, (per, PAD), 1)
        mls = [mlb[r]] + [mr[k] for k in range(1, replicas)]

        def pick(values, n):
            return jnp.sum(jnp.where(plane == n, values, 0.0), axis=1, keepdims=True)

        turn = lax.broadcasted_iota(jnp.int32, (per, hd), 0) % DEVICE_REQUESTS

        def spread(n):
            values = new_ref[:, n * hd : (n + 1) * hd].astype(jnp.float32)
            wide = values[:1]
            for i in range(1, DEVICE_REQUESTS):
                wide = jnp.where(turn == i, values[i : i + 1], wide)
            return jnp.broadcast_to(wide, (per, hd))

        for g in range(heads):
            query = qb[r, g * per : (g + 1) * per, :].astype(jnp.float32)
            fresh = jnp.sum(query * spread(g), axis=1, keepdims=True) * scale
            tops = [pick(v, g) for v in mls]
            best = fresh
            for t in tops:
                best = jnp.maximum(best, t)
            weight = jnp.exp(fresh - best)
            denom = weight
            mixed = weight * spread(heads + g)
            for k in range(replicas):
                factor = jnp.exp(tops[k] - best)
                part = accf[r, g] if k == 0 else ar[k, g].astype(jnp.float32)
                denom = denom + factor * pick(mls[k], heads + g)
                mixed = mixed + factor * part
            attn_ref[g * per : (g + 1) * per, :] = (mixed / denom).astype(attn_ref.dtype)

    my_slot = (r * (depth * CORES) + e) // QUART
    chunk = CORES * replicas * rows
    slane = lax.broadcasted_iota(jnp.int32, (chunk, PAD), 1)
    mine = (slane % experts == my_slot) & (slane < 3 * experts)

    def gather(zo):
        for k in range(1, replicas):
            got = xb.at[(z + depth - zo) % depth, c, (r + replicas - k) % replicas]
            remote(got, got, r_send.at[zo, k], r_recv.at[zo, k], cdev).wait_recv()
            core_out(zo, k)

    def expert(zo):
        zi = (z + depth - zo) % depth
        for k in range(replicas):
            got = xb.at[zi, sib, (r + replicas - k) % replicas]
            remote(got, got, c_send.at[zo, k], c_recv.at[zo, k], cdev).wait_recv()
        block = xb[zi].reshape(chunk, width + PAD)
        gain = jnp.sum(
            jnp.where(mine, block[:, width:].astype(jnp.float32), 0.0), axis=1, keepdims=True
        )
        halves = jnp.dot(block[:, :width], wgu[...], preferred_element_type=jnp.float32)
        gate, up = halves[:, :quarter], halves[:, quarter:]
        act = (gate / (1.0 + jnp.exp(-gate)) * up).astype(jnp.bfloat16)
        step = width // 4
        for n in range(4):
            cols = slice(n * step, (n + 1) * step)
            part = jnp.dot(act, wd[:, cols], preferred_element_type=jnp.float32) * gain
            part = part.reshape(CORES, replicas * rows, step)
            pf[zo, :, :, cols] = part
            cs[zo, :, :, cols] = part.astype(jnp.bfloat16)
        push(cs.at[zo, sib], cr.at[zo], cs_send.at[zo], cs_recv.at[zo], cdev)

    def across(zo):
        remote(cr.at[zo], cr.at[zo], cs_send.at[zo], cs_recv.at[zo], cdev).wait_recv()
        both = pf[zo, c] + cr[zo].astype(jnp.float32)
        pf[zo, c] = both
        xs[zo] = both.astype(jnp.bfloat16).reshape(replicas, rows, width)
        for k in range(1, replicas):
            to = (r + k) % replicas
            push(xs.at[zo, to], xr.at[zo, k], xs_send.at[zo, k], xs_recv.at[zo, k], rdev(k))

    def along(zo):
        total = pf[zo, c, pl.ds(pl.multiple_of(r * rows, rows), rows), :]
        for k in range(1, replicas):
            remote(
                xr.at[zo, k], xr.at[zo, k], xs_send.at[zo, k], xs_recv.at[zo, k], cdev
            ).wait_recv()
            total = total + xr[zo, k].astype(jnp.float32)
        if zo == 0:
            zf[...] = total
        else:
            zs[zo] = total.astype(jnp.bfloat16)
            push(zs.at[zo], zr.at[zo], zs_send.at[zo], zs_recv.at[zo], zdev(depth - zo))

    gather(0)
    loads[0].wait()
    loads[1].wait()
    for zo in range(depth):
        expert(zo)
        if zo >= 1:
            across(zo - 1)
        if zo + 1 < depth:
            gather(zo + 1)
        if zo >= 2:
            along(zo - 2)
    across(depth - 1)
    finish_attention()
    if depth >= 2:
        along(depth - 2)
    along(depth - 1)
    result = zf[...]
    for zo in range(1, depth):
        remote(zr.at[zo], zr.at[zo], zs_send.at[zo], zs_recv.at[zo], cdev).wait_recv()
        result = result + zr[zo].astype(jnp.float32)
    moe_ref[...] = result.astype(moe_ref.dtype)
    for d in sent:
        d.wait_send()


def fused(
    moe_input,
    expert_ids,
    route_weight,
    expert_slot,
    w_gate_up,
    w_down,
    queries,
    incoming_key_value,
    key_value_pool,
    block_owner,
    block_tokens,
):
    replicas = lax.axis_size("replica")
    depth = lax.axis_size("expert") // CORES
    experts = expert_slot.shape[0]
    rows, width = moe_input.shape
    group = QUERY_HEADS // KEY_VALUE_HEADS
    per = DEVICE_REQUESTS * group
    hd = HEAD_DIMENSION
    keys = key_value_pool.shape[0] * key_value_pool.shape[1]
    smem = pl.BlockSpec(memory_space=pltpu.SMEM)
    vmem = pl.BlockSpec(memory_space=pltpu.VMEM)
    hbm = pl.BlockSpec(memory_space=pl.ANY)
    bf, f32 = jnp.bfloat16, jnp.float32
    dma = pltpu.SemaphoreType.DMA
    moe_out, attn = pl.pallas_call(
        functools.partial(fused_kernel, replicas, depth, experts),
        out_shape=(
            jax.ShapeDtypeStruct((rows, width), bf),
            jax.ShapeDtypeStruct((KEY_VALUE_HEADS * per, hd), bf),
        ),
        in_specs=[smem] * 3 + [vmem] * 4 + [hbm] * 4,
        out_specs=(vmem, vmem),
        scratch_shapes=[
            pltpu.VMEM((depth, CORES, replicas, rows, width + PAD), bf),
            pltpu.VMEM(w_gate_up.shape, bf),
            pltpu.VMEM(w_down.shape, bf),
            pltpu.VMEM((keys, key_value_pool.shape[2]), bf),
            pltpu.VMEM((depth, CORES, replicas * rows, width), f32),
            pltpu.VMEM((depth, CORES, replicas * rows, width), bf),
            pltpu.VMEM((depth, replicas * rows, width), bf),
            pltpu.VMEM((depth, replicas, rows, width), bf),
            pltpu.VMEM((depth, replicas, rows, width), bf),
            pltpu.VMEM((rows, width), f32),
            pltpu.VMEM((depth, rows, width), bf),
            pltpu.VMEM((depth, rows, width), bf),
            pltpu.VMEM((replicas, KEY_VALUE_HEADS * per, hd), bf),
            pltpu.VMEM((replicas, KEY_VALUE_HEADS, per, hd), f32),
            pltpu.VMEM((replicas, KEY_VALUE_HEADS, per, hd), bf),
            pltpu.VMEM((replicas, per, PAD), f32),
            pltpu.VMEM((replicas, KEY_VALUE_HEADS, per, hd), bf),
            pltpu.VMEM((replicas, per, PAD), f32),
            dma((4,)),
            dma((depth,)),
            dma((depth,)),
            dma((depth, replicas)),
            dma((depth, replicas)),
            dma((depth, replicas)),
            dma((depth, replicas)),
            dma((replicas,)),
            dma((replicas,)),
            dma((depth,)),
            dma((depth,)),
            dma((depth, replicas)),
            dma((depth, replicas)),
            dma((depth,)),
            dma((depth,)),
            dma((replicas,)),
            dma((replicas,)),
            dma((replicas,)),
            dma((replicas,)),
        ],
        compiler_params=pltpu.CompilerParams(
            collective_id=0, has_side_effects=True, vmem_limit_bytes=VMEM_LIMIT
        ),
    )(
        expert_slot,
        block_owner,
        block_tokens,
        expert_ids.T,
        route_weight.T,
        queries,
        incoming_key_value,
        moe_input,
        w_gate_up,
        w_down,
        key_value_pool.reshape(keys, key_value_pool.shape[2]),
    )
    attn_out = (
        attn.reshape(KEY_VALUE_HEADS, group, DEVICE_REQUESTS, hd)
        .transpose(2, 0, 1, 3)
        .reshape(DEVICE_REQUESTS, QUERY_HEADS * hd)
    )
    return (moe_out, attn_out)


def shards(
    moe_input,
    expert_ids,
    route_weight,
    expert_slot,
    w_gate_up,
    w_down,
    queries,
    incoming_key_value,
    key_value_pool,
    block_owner,
    block_tokens,
):
    if fits_fused(expert_ids, expert_slot):
        return fused(
            moe_input,
            expert_ids,
            route_weight,
            expert_slot,
            w_gate_up,
            w_down,
            queries,
            incoming_key_value,
            key_value_pool,
            block_owner,
            block_tokens,
        )
    moe_out = mixture(moe_input, expert_ids, route_weight, expert_slot, w_gate_up, w_down)
    scale = 1.0 / math.sqrt(HEAD_DIMENSION)
    query_rows = queries.reshape(
        DEVICE_REQUESTS, KEY_VALUE_HEADS, QUERY_HEADS // KEY_VALUE_HEADS, HEAD_DIMENSION
    )
    latest_keys = incoming_key_value[:, : KEY_VALUE_HEADS * HEAD_DIMENSION].reshape(
        DEVICE_REQUESTS, KEY_VALUE_HEADS, HEAD_DIMENSION
    )
    new_score = (
        jnp.einsum("rgjd,rgd->rgj", query_rows, latest_keys, preferred_element_type=jnp.float32)
        * scale
    )
    incoming_values = (
        incoming_key_value[:, KEY_VALUE_HEADS * HEAD_DIMENSION :]
        .reshape(DEVICE_REQUESTS, KEY_VALUE_HEADS, 1, HEAD_DIMENSION)
        .astype(jnp.float32)
    )
    maxima, totals, weighted = attend_migrate(
        query_rows, key_value_pool, block_owner, block_tokens, scale
    )
    attn_out = (
        finish(maxima, totals, weighted, new_score, incoming_values)
        .reshape(DEVICE_REQUESTS, QUERY_HEADS * HEAD_DIMENSION)
        .astype(jnp.bfloat16)
    )
    return (moe_out, attn_out)


def solution(mesh):
    placed = (
        P(("replica", "expert"), None),
        P(("replica", "expert"), None),
        P(("replica", "expert"), None),
        P(),
        P(None, ("replica", "expert")),
        P(("replica", "expert"), None),
        P(("replica", "expert"), None),
        P(("replica", "expert"), None),
        P(("replica", "expert"), None, None),
        P(("replica", "expert")),
        P(("replica", "expert")),
    )
    return jax.shard_map(
        shards,
        mesh=mesh,
        in_specs=placed,
        out_specs=(P(("replica", "expert"), None), P(("replica", "expert"), None)),
        check_vma=False,
    )
```

```python
import functools
import math

import jax
import jax.numpy as jnp
from jax import lax
from jax.experimental import pallas as pl
from jax.experimental.pallas import tpu as pltpu
from jax.sharding import PartitionSpec as P

QUART = 4
QUERY_HEADS = 64
KEY_VALUE_HEADS = 4
HEAD_DIMENSION = 128
DEVICE_REQUESTS = 2
DEVICE_BLOCKS = 16
BLOCK_SLOTS = 64
MIG = 2


HIGHEST = lax.Precision.HIGHEST


def partial_state(query_rows, rows, mask, scale):
    heads_kv = query_rows.shape[1]
    head_size = query_rows.shape[3]
    maxima = []
    totals = []
    weighted = []
    for head in range(heads_kv):
        cached_key_rows = rows[:, head * head_size : (head + 1) * head_size]
        cached_value_rows = rows[
            :, (heads_kv + head) * head_size : (heads_kv + head + 1) * head_size
        ].astype(jnp.float32)
        scores = (
            jnp.einsum(
                "rjd,nd->rjn",
                query_rows[:, head],
                cached_key_rows,
                preferred_element_type=jnp.float32,
            )
            * scale
        )
        keep = mask[:, None, :]
        largest = jnp.max(jnp.where(keep, scores, -1e30), axis=2)
        weights = jnp.where(keep, jnp.exp(scores - largest[:, :, None]), 0.0)
        maxima.append(largest)
        totals.append(jnp.sum(weights, axis=2))
        weighted.append(jnp.einsum("rjn,nd->rjd", weights, cached_value_rows, precision=HIGHEST))
    return (jnp.stack(maxima, 1), jnp.stack(totals, 1), jnp.stack(weighted, 1))


def finish(maxima, totals, weighted, new_score, incoming_values):
    best = jnp.maximum(jnp.max(maxima, axis=0), new_score)
    own_weight = jnp.exp(new_score - best)
    factor = jnp.exp(maxima - best[None])
    denom = own_weight + jnp.sum(factor * totals, axis=0)
    mixed = own_weight[..., None] * incoming_values + jnp.sum(factor[..., None] * weighted, axis=0)
    return mixed / denom[..., None]


def attend_migrate(query_rows, key_value_pool, block_owner, block_tokens, scale):
    replicas = lax.axis_size("replica")
    mine = lax.axis_index("replica")
    kv_width = key_value_pool.shape[2]
    target = block_owner // DEVICE_REQUESTS
    request = block_owner % DEVICE_REQUESTS
    leaving = target != mine
    to_replica = (
        (target[:, None] == jnp.arange(replicas, dtype=jnp.int32)[None, :]) & leaving[:, None]
    ).astype(jnp.int32)
    before = jnp.cumsum(to_replica, axis=0) - to_replica
    place = target * MIG + jnp.sum(before * to_replica, axis=1)
    select = (place[None, :] == jnp.arange(replicas * MIG, dtype=jnp.int32)[:, None]) & leaving[
        None, :
    ]
    chosen = select.astype(jnp.int32)
    send_blocks = jnp.dot(
        select.astype(jnp.bfloat16),
        key_value_pool.reshape(DEVICE_BLOCKS, BLOCK_SLOTS * kv_width),
        preferred_element_type=jnp.float32,
    ).astype(jnp.bfloat16)
    send_request = jnp.sum(chosen * request[None, :], axis=1)
    send_count = jnp.sum(chosen * block_tokens[None, :], axis=1)
    got_blocks, got_request, got_count = (
        lax.all_to_all(
            send_blocks.reshape(replicas, MIG, BLOCK_SLOTS * kv_width),
            "replica",
            split_axis=0,
            concat_axis=0,
            tiled=True,
        ),
        lax.all_to_all(
            send_request.reshape(replicas, MIG), "replica", split_axis=0, concat_axis=0, tiled=True
        ),
        lax.all_to_all(
            send_count.reshape(replicas, MIG), "replica", split_axis=0, concat_axis=0, tiled=True
        ),
    )
    positions = jnp.arange(BLOCK_SLOTS, dtype=jnp.int32)
    requests = jnp.arange(DEVICE_REQUESTS, dtype=jnp.int32)
    local_valid = (positions[None, :] < block_tokens[:, None]).reshape(-1)
    local_owner = jnp.repeat(block_owner, BLOCK_SLOTS)
    local_mask = (local_owner[None, :] == mine * DEVICE_REQUESTS + requests[:, None]) & local_valid[
        None, :
    ]
    local_state = partial_state(
        query_rows, key_value_pool.reshape(DEVICE_BLOCKS * BLOCK_SLOTS, kv_width), local_mask, scale
    )
    got_valid = (positions[None, :] < got_count.reshape(-1)[:, None]).reshape(-1)
    got_owner = jnp.repeat(got_request.reshape(-1), BLOCK_SLOTS)
    got_mask = (got_owner[None, :] == requests[:, None]) & got_valid[None, :]
    got_state = partial_state(query_rows, got_blocks.reshape(-1, kv_width), got_mask, scale)
    maxima = jnp.stack([local_state[0], got_state[0]], axis=0)
    totals = jnp.stack([local_state[1], got_state[1]], axis=0)
    weighted = jnp.stack([local_state[2], got_state[2]], axis=0)
    return (maxima, totals, weighted)


def expert_local(rows, w_gate_up, w_down):
    quarter = w_down.shape[0]
    halves = jnp.dot(rows, w_gate_up, preferred_element_type=jnp.float32)
    activation = (jax.nn.silu(halves[:, :quarter]) * halves[:, quarter:]).astype(jnp.bfloat16)
    return jnp.dot(activation, w_down, preferred_element_type=jnp.float32).astype(jnp.bfloat16)


def mixture(moe_input, expert_ids, route_weight, expert_slot, w_gate_up, w_down):
    token_rows = moe_input.shape[0]
    width = moe_input.shape[1]
    top_k = expert_ids.shape[1]
    experts = expert_slot.shape[0]
    replicas = lax.axis_size("replica")
    columns = lax.axis_size("expert")
    capacity = min(token_rows, max(2, 2 * token_rows * top_k // experts))
    flat_ids = expert_ids.reshape(-1)
    onehot = (flat_ids[:, None] == jnp.arange(experts, dtype=jnp.int32)[None, :]).astype(jnp.int32)
    before = jnp.cumsum(onehot, axis=0) - onehot
    position = jnp.sum(before * onehot, axis=1)
    slot_of = jnp.sum(onehot * expert_slot[None, :], axis=1)
    target = slot_of * capacity + position
    assign = (target[:, None] == jnp.arange(experts * capacity, dtype=jnp.int32)[None, :]).reshape(
        token_rows, top_k, experts * capacity
    )
    dispatch_map = jnp.sum(assign.astype(jnp.int32), axis=1).astype(jnp.bfloat16)
    send_rows = jnp.einsum(
        "tc,td->cd", dispatch_map, moe_input, preferred_element_type=jnp.float32
    ).astype(jnp.bfloat16)
    send = jnp.broadcast_to(
        send_rows.reshape(experts, 1, capacity, width), (experts, QUART, capacity, width)
    )
    send = send.reshape(replicas, columns, capacity, width)
    received = lax.all_to_all(
        lax.all_to_all(send, "replica", split_axis=0, concat_axis=0, tiled=True),
        "expert",
        split_axis=1,
        concat_axis=1,
        tiled=True,
    )
    quarter_part = expert_local(received.reshape(-1, width), w_gate_up, w_down)
    returned = lax.all_to_all(
        lax.all_to_all(
            quarter_part.reshape(send.shape), "replica", split_axis=0, concat_axis=0, tiled=True
        ),
        "expert",
        split_axis=1,
        concat_axis=1,
        tiled=True,
    )
    expert_out = jnp.sum(
        returned.reshape(experts, QUART, capacity, width).astype(jnp.float32), axis=1
    ).reshape(experts * capacity, width)
    mixing = jnp.sum(assign.astype(jnp.float32) * route_weight[:, :, None], axis=1)
    return jnp.dot(
        mixing, expert_out, precision=HIGHEST, preferred_element_type=jnp.float32
    ).astype(jnp.bfloat16)


CORES = 2
PAD = 128
SIDE = 2
VMEM_LIMIT = 60 * 1024 * 1024
MESH = pl.DeviceIdType.MESH


def fits_fused(expert_ids, expert_slot):
    experts = expert_slot.shape[0]
    devices = lax.axis_size("replica") * lax.axis_size("expert")
    return (
        expert_ids.shape[1] == experts
        and 3 * experts <= PAD
        and devices == experts * QUART
        and lax.axis_size("replica") == SIDE * SIDE
        and lax.axis_size("expert") % CORES == 0
    )


def fused_kernel(
    replicas,
    depth,
    experts,
    slot_ref,
    owner_ref,
    tokens_ref,
    ids_ref,
    rw_ref,
    q_ref,
    new_ref,
    x_hbm,
    wgu_hbm,
    wd_hbm,
    kv_hbm,
    moe_ref,
    attn_ref,
    xb,
    wgu,
    wd,
    kv,
    pf,
    cs,
    cr,
    xs1,
    xr1,
    xs2,
    xr2,
    zf,
    zs,
    zr,
    qb,
    accf,
    accb,
    mlb,
    ar,
    mr,
    load_sem,
    z_send,
    z_recv,
    r_send,
    r_recv,
    d_send,
    d_recv,
    c_send,
    c_recv,
    q_send,
    q_recv,
    cs_send,
    cs_recv,
    xs1_send,
    xs1_recv,
    xs2_send,
    xs2_recv,
    zs_send,
    zs_recv,
    a_send,
    a_recv,
    m_send,
    m_recv,
):
    r = lax.axis_index("replica")
    e = lax.axis_index("expert")
    z = e // CORES
    c = e % CORES
    sib = 1 - c
    rows, width = x_hbm.shape
    quarter = wd_hbm.shape[0]
    heads = KEY_VALUE_HEADS
    hd = HEAD_DIMENSION
    group = QUERY_HEADS // KEY_VALUE_HEADS
    per = DEVICE_REQUESTS * group
    scale = 1.0 / math.sqrt(HEAD_DIMENSION)
    sent = []

    def rdev(k):
        return ((r + k) % replicas, e)

    def zdev(k):
        return (r, ((z + k) % depth) * CORES + c)

    cdev = (r, z * CORES + sib)
    rx = r + 1 - 2 * (r % SIDE)
    ry = (r + SIDE) % replicas
    rd = replicas - 1 - r
    near = (rx, ry)
    half = width // 2

    def remote(src, dst, ssem, rsem, dev):
        return pltpu.make_async_remote_copy(
            src_ref=src, dst_ref=dst, send_sem=ssem, recv_sem=rsem, device_id=dev, device_id_type=MESH
        )

    def push(*args):
        d = remote(*args)
        d.start()
        sent.append(d)

    loads = [
        pltpu.make_async_copy(wgu_hbm, wgu, load_sem.at[0]),
        pltpu.make_async_copy(wd_hbm, wd, load_sem.at[1]),
        pltpu.make_async_copy(kv_hbm, kv, load_sem.at[2]),
        pltpu.make_async_copy(x_hbm, xb.at[z, c, r, :, pl.ds(0, width)], load_sem.at[3]),
    ]
    for d in loads:
        d.start()

    barrier = pltpu.get_barrier_semaphore()
    for k in range(1, replicas):
        pl.semaphore_signal(barrier, inc=1, device_id=rdev(k), device_id_type=MESH)
    for k in range(1, depth):
        pl.semaphore_signal(barrier, inc=1, device_id=zdev(k), device_id_type=MESH)
    pl.semaphore_signal(barrier, inc=1, device_id=cdev, device_id_type=MESH)

    line = lax.broadcasted_iota(jnp.int32, (PAD, rows), 0)
    mix = jnp.zeros((PAD, rows), jnp.float32)
    for k in range(experts):
        chosen = ids_ref[k : k + 1, :]
        slot = jnp.zeros((1, rows), jnp.int32)
        for n in range(experts):
            slot = jnp.where(chosen == n, slot_ref[n], slot)
        mix = mix + jnp.where(line % experts == slot, rw_ref[k : k + 1, :], 0.0)
    high = mix.astype(jnp.bfloat16).astype(jnp.float32)
    rest = mix - high
    mid = rest.astype(jnp.bfloat16).astype(jnp.float32)
    low = rest - mid
    terms = jnp.where(line < experts, high, jnp.where(line < 2 * experts, mid, low))
    unit = (
        lax.broadcasted_iota(jnp.int32, (rows, rows), 0)
        == lax.broadcasted_iota(jnp.int32, (rows, rows), 1)
    ).astype(jnp.bfloat16)
    xb[z, c, r, :, width:] = lax.dot_general(
        unit,
        terms.astype(jnp.bfloat16),
        (((1,), (1,)), ((), ())),
        preferred_element_type=jnp.float32,
    ).astype(jnp.bfloat16)
    asked = q_ref[...].astype(jnp.float32)
    for g in range(heads):
        pieces = [asked[:, (g * group + j) * hd : (g * group + j + 1) * hd] for j in range(group)]
        qb[r, g * per : (g + 1) * per, :] = jnp.concatenate(pieces, axis=0).astype(jnp.bfloat16)
    loads[3].wait()

    pl.semaphore_wait(barrier, replicas - 1 + depth - 1 + 1)

    def piece(zo, core, of):
        return xb.at[(z + depth - zo) % depth, core, of]

    def part(zo, of, h):
        cols = pl.ds(0, half) if h == 0 else pl.ds(half, width + PAD - half)
        return xb.at[(z + depth - zo) % depth, c, of, :, cols]

    def xy_out(zo):
        for h in range(2):
            p = piece(zo, c, r)
            push(p, p, r_send.at[zo, h], r_recv.at[zo, h], (near[h], e))

    def core_out(zo, n, of):
        p = piece(zo, c, of)
        push(p, p, c_send.at[zo, n], c_recv.at[zo, n], cdev)

    def relay(zo):
        for h in range(2):
            p = piece(zo, c, near[h])
            remote(p, p, r_send.at[zo, h], r_recv.at[zo, h], cdev).wait_recv()
            p = part(zo, near[h], h)
            push(p, p, d_send.at[zo, h], d_recv.at[zo, h], (near[1 - h], e))
            core_out(zo, 1 + h, near[h])

    def gather(zo):
        for h in range(2):
            p = part(zo, rd, h)
            remote(p, p, d_send.at[zo, h], d_recv.at[zo, h], cdev).wait_recv()
        core_out(zo, 3, rd)

    own = xb.at[z, c, r]
    for k in range(1, depth):
        push(own, own, z_send.at[k], z_recv.at[k], zdev(k))
    for k in range(1, replicas):
        push(qb.at[r], qb.at[r], q_send.at[k], q_recv.at[k], rdev(k))
    xy_out(0)
    core_out(0, 0, r)

    def onward(zo):
        p = piece(zo, c, r)
        remote(p, p, z_send.at[zo], z_recv.at[zo], cdev).wait_recv()
        xy_out(zo)
        core_out(zo, 0, r)

    onward(1)
    relay(0)

    for k in range(1, replicas):
        got = qb.at[(r + replicas - k) % replicas]
        remote(got, got, q_send.at[k], q_recv.at[k], cdev).wait_recv()
    loads[2].wait()
    blocks, slots = owner_ref.shape[0], kv.shape[0] // owner_ref.shape[0]
    keys = kv.shape[0]
    place = lax.broadcasted_iota(jnp.int32, (1, keys), 1)
    holder = jnp.full((1, keys), -1, jnp.int32)
    for b in range(blocks):
        inside = (place >= b * slots) & (place < b * slots + tokens_ref[b])
        holder = jnp.where(inside, owner_ref[b], holder)
    total = replicas * per
    row = lax.broadcasted_iota(jnp.int32, (total, 1), 0)
    asker = row // per * DEVICE_REQUESTS + row % DEVICE_REQUESTS
    keep = holder == asker
    mlane = lax.broadcasted_iota(jnp.int32, (total, PAD), 1)

    def head(g, ml):
        col = slice(g * hd, (g + 1) * hd)
        vcol = slice((heads + g) * hd, (heads + g + 1) * hd)
        qg = qb[:, g * per : (g + 1) * per, :].reshape(total, hd)
        scores = (
            lax.dot_general(
                qg, kv[:, col], (((1,), (1,)), ((), ())), preferred_element_type=jnp.float32
            )
            * scale
        )
        top = jnp.max(jnp.where(keep, scores, -1e30), axis=1, keepdims=True)
        weights = jnp.where(keep, jnp.exp(scores - top), 0.0)
        mass = jnp.sum(weights, axis=1, keepdims=True)
        acc = jnp.dot(
            weights.astype(jnp.bfloat16), kv[:, vcol], preferred_element_type=jnp.float32
        ).reshape(replicas, per, hd)
        accf[:, g] = acc
        accb[:, g] = acc.astype(jnp.bfloat16)
        return jnp.where(mlane == g, top, jnp.where(mlane == heads + g, mass, ml))

    ml = jnp.zeros((total, PAD), jnp.float32)
    for g in range(max(heads, depth - 1)):
        if g < heads:
            ml = head(g, ml)
        if g + 2 < depth:
            onward(g + 2)
        if g + 1 < depth:
            relay(g + 1)
    mlb[...] = ml.reshape(replicas, per, PAD)
    for k in range(1, replicas):
        to = (r + k) % replicas
        push(accb.at[to], ar.at[k], a_send.at[k], a_recv.at[k], rdev(k))
        push(mlb.at[to], mr.at[k], m_send.at[k], m_recv.at[k], rdev(k))

    def finish_attention():
        for k in range(1, replicas):
            remote(ar.at[k], ar.at[k], a_send.at[k], a_recv.at[k], cdev).wait_recv()
            remote(mr.at[k], mr.at[k], m_send.at[k], m_recv.at[k], cdev).wait_recv()
        plane = lax.broadcasted_iota(jnp.int32, (per, PAD), 1)
        mls = [mlb[r]] + [mr[k] for k in range(1, replicas)]

        def pick(values, n):
            return jnp.sum(jnp.where(plane == n, values, 0.0), axis=1, keepdims=True)

        turn = lax.broadcasted_iota(jnp.int32, (per, hd), 0) % DEVICE_REQUESTS

        def spread(n):
            values = new_ref[:, n * hd : (n + 1) * hd].astype(jnp.float32)
            wide = values[:1]
            for i in range(1, DEVICE_REQUESTS):
                wide = jnp.where(turn == i, values[i : i + 1], wide)
            return jnp.broadcast_to(wide, (per, hd))

        for g in range(heads):
            query = qb[r, g * per : (g + 1) * per, :].astype(jnp.float32)
            fresh = jnp.sum(query * spread(g), axis=1, keepdims=True) * scale
            tops = [pick(v, g) for v in mls]
            best = fresh
            for t in tops:
                best = jnp.maximum(best, t)
            weight = jnp.exp(fresh - best)
            denom = weight
            mixed = weight * spread(heads + g)
            for k in range(replicas):
                factor = jnp.exp(tops[k] - best)
                share = accf[r, g] if k == 0 else ar[k, g].astype(jnp.float32)
                denom = denom + factor * pick(mls[k], heads + g)
                mixed = mixed + factor * share
            mixed = mixed / denom
            for j in range(group):
                cols = slice((g * group + j) * hd, (g * group + j + 1) * hd)
                attn_ref[:, cols] = mixed[
                    j * DEVICE_REQUESTS : (j + 1) * DEVICE_REQUESTS, :
                ].astype(attn_ref.dtype)

    my_slot = (r * (depth * CORES) + e) // QUART
    chunk = CORES * replicas * rows
    slane = lax.broadcasted_iota(jnp.int32, (chunk, PAD), 1)
    mine = (slane % experts == my_slot) & (slane < 3 * experts)

    def expert(zo):
        zi = (z + depth - zo) % depth
        for n, of in enumerate((r, rx, ry, rd)):
            p = piece(zo, sib, of)
            remote(p, p, c_send.at[zo, n], c_recv.at[zo, n], cdev).wait_recv()
        block = xb[zi].reshape(chunk, width + PAD)
        gain = jnp.sum(
            jnp.where(mine, block[:, width:].astype(jnp.float32), 0.0), axis=1, keepdims=True
        )
        halves = jnp.dot(block[:, :width], wgu[...], preferred_element_type=jnp.float32)
        gate, up = halves[:, :quarter], halves[:, quarter:]
        act = (gate / (1.0 + jnp.exp(-gate)) * up).astype(jnp.bfloat16)
        step = width // 4
        for n in range(4):
            cols = slice(n * step, (n + 1) * step)
            out = jnp.dot(act, wd[:, cols], preferred_element_type=jnp.float32) * gain
            out = out.reshape(CORES, replicas * rows, step)
            pf[zo, :, :, cols] = out
            cs[zo, :, :, cols] = out.astype(jnp.bfloat16)
        push(cs.at[zo, sib], cr.at[zo], cs_send.at[zo], cs_recv.at[zo], cdev)

    def mine_of(zo, of, h):
        return pf[
            zo, c, pl.ds(pl.multiple_of(of * rows, rows), rows), h * half : (h + 1) * half
        ]

    def across(zo):
        remote(cr.at[zo], cr.at[zo], cs_send.at[zo], cs_recv.at[zo], cdev).wait_recv()
        pf[zo, c] = pf[zo, c] + cr[zo].astype(jnp.float32)
        for h in range(2):
            to = near[1 - h]
            xs1[zo, h, 0] = mine_of(zo, rd, h).astype(jnp.bfloat16)
            xs1[zo, h, 1] = mine_of(zo, to, h).astype(jnp.bfloat16)
            push(xs1.at[zo, h], xr1.at[zo, h], xs1_send.at[zo, h], xs1_recv.at[zo, h], (to, e))

    def around(zo):
        for h in range(2):
            p = xr1.at[zo, h]
            remote(p, p, xs1_send.at[zo, h], xs1_recv.at[zo, h], cdev).wait_recv()
            both = mine_of(zo, near[h], h) + xr1[zo, h, 0].astype(jnp.float32)
            xs2[zo, h] = both.astype(jnp.bfloat16)
            push(
                xs2.at[zo, h], xr2.at[zo, h], xs2_send.at[zo, h], xs2_recv.at[zo, h], (near[h], e)
            )

    def along(zo):
        for h in range(2):
            p = xr2.at[zo, h]
            remote(p, p, xs2_send.at[zo, h], xs2_recv.at[zo, h], cdev).wait_recv()
            cols = slice(h * half, (h + 1) * half)
            sums = mine_of(zo, r, h) + xr1[zo, h, 1].astype(jnp.float32)
            sums = sums + xr2[zo, h].astype(jnp.float32)
            if zo == 0:
                zf[:, cols] = sums
            else:
                zs[zo, :, cols] = sums.astype(jnp.bfloat16)
        if zo != 0:
            push(zs.at[zo], zr.at[zo], zs_send.at[zo], zs_recv.at[zo], zdev(depth - zo))

    gather(0)
    loads[0].wait()
    loads[1].wait()
    for zo in range(depth + 3):
        if zo < depth:
            expert(zo)
        if 0 <= zo - 1 < depth:
            across(zo - 1)
        if zo + 1 < depth:
            gather(zo + 1)
        if 0 <= zo - 2 < depth:
            around(zo - 2)
        if 0 <= zo - 3 < depth:
            along(zo - 3)
        if zo == depth + 1:
            finish_attention()
    result = zf[...]
    for zo in range(1, depth):
        remote(zr.at[zo], zr.at[zo], zs_send.at[zo], zs_recv.at[zo], cdev).wait_recv()
        result = result + zr[zo].astype(jnp.float32)
    moe_ref[...] = result.astype(moe_ref.dtype)
    for d in sent:
        d.wait_send()


def place_results(moe_ref, attn_ref, moe_out, attn_out, sem):
    first = pltpu.make_async_copy(moe_ref, moe_out, sem.at[0])
    second = pltpu.make_async_copy(attn_ref, attn_out, sem.at[1])
    first.start()
    second.start()
    first.wait()
    second.wait()


def fused(
    moe_input,
    expert_ids,
    route_weight,
    expert_slot,
    w_gate_up,
    w_down,
    queries,
    incoming_key_value,
    key_value_pool,
    block_owner,
    block_tokens,
):
    replicas = lax.axis_size("replica")
    depth = lax.axis_size("expert") // CORES
    experts = expert_slot.shape[0]
    rows, width = moe_input.shape
    group = QUERY_HEADS // KEY_VALUE_HEADS
    per = DEVICE_REQUESTS * group
    hd = HEAD_DIMENSION
    keys = key_value_pool.shape[0] * key_value_pool.shape[1]
    smem = pl.BlockSpec(memory_space=pltpu.SMEM)
    vmem = pl.BlockSpec(memory_space=pltpu.VMEM)
    hbm = pl.BlockSpec(memory_space=pl.ANY)
    bf, f32 = jnp.bfloat16, jnp.float32
    dma = pltpu.SemaphoreType.DMA
    moe_out, attn = pl.pallas_call(
        functools.partial(fused_kernel, replicas, depth, experts),
        out_shape=(
            jax.ShapeDtypeStruct((rows, width), bf),
            jax.ShapeDtypeStruct(queries.shape, bf),
        ),
        in_specs=[smem] * 3 + [vmem] * 4 + [hbm] * 4,
        out_specs=(vmem, vmem),
        scratch_shapes=[
            pltpu.VMEM((depth, CORES, replicas, rows, width + PAD), bf),
            pltpu.VMEM(w_gate_up.shape, bf),
            pltpu.VMEM(w_down.shape, bf),
            pltpu.VMEM((keys, key_value_pool.shape[2]), bf),
            pltpu.VMEM((depth, CORES, replicas * rows, width), f32),
            pltpu.VMEM((depth, CORES, replicas * rows, width), bf),
            pltpu.VMEM((depth, replicas * rows, width), bf),
            pltpu.VMEM((depth, 2, 2, rows, width // 2), bf),
            pltpu.VMEM((depth, 2, 2, rows, width // 2), bf),
            pltpu.VMEM((depth, 2, rows, width // 2), bf),
            pltpu.VMEM((depth, 2, rows, width // 2), bf),
            pltpu.VMEM((rows, width), f32),
            pltpu.VMEM((depth, rows, width), bf),
            pltpu.VMEM((depth, rows, width), bf),
            pltpu.VMEM((replicas, KEY_VALUE_HEADS * per, hd), bf),
            pltpu.VMEM((replicas, KEY_VALUE_HEADS, per, hd), f32),
            pltpu.VMEM((replicas, KEY_VALUE_HEADS, per, hd), bf),
            pltpu.VMEM((replicas, per, PAD), f32),
            pltpu.VMEM((replicas, KEY_VALUE_HEADS, per, hd), bf),
            pltpu.VMEM((replicas, per, PAD), f32),
            dma((4,)),
            dma((depth,)),
            dma((depth,)),
            dma((depth, 2)),
            dma((depth, 2)),
            dma((depth, 2)),
            dma((depth, 2)),
            dma((depth, replicas)),
            dma((depth, replicas)),
            dma((replicas,)),
            dma((replicas,)),
            dma((depth,)),
            dma((depth,)),
            dma((depth, 2)),
            dma((depth, 2)),
            dma((depth, 2)),
            dma((depth, 2)),
            dma((depth,)),
            dma((depth,)),
            dma((replicas,)),
            dma((replicas,)),
            dma((replicas,)),
            dma((replicas,)),
        ],
        compiler_params=pltpu.CompilerParams(
            collective_id=0, has_side_effects=True, vmem_limit_bytes=VMEM_LIMIT
        ),
    )(
        expert_slot,
        block_owner,
        block_tokens,
        expert_ids.T,
        route_weight.T,
        queries,
        incoming_key_value,
        moe_input,
        w_gate_up,
        w_down,
        key_value_pool.reshape(keys, key_value_pool.shape[2]),
    )
    return pl.pallas_call(
        place_results,
        out_shape=(
            jax.ShapeDtypeStruct(moe_out.shape, bf),
            jax.ShapeDtypeStruct(attn.shape, bf),
        ),
        in_specs=[hbm] * 2,
        out_specs=(hbm, hbm),
        scratch_shapes=[dma((2,))],
        compiler_params=pltpu.CompilerParams(vmem_limit_bytes=VMEM_LIMIT),
    )(moe_out, attn)


def shards(
    moe_input,
    expert_ids,
    route_weight,
    expert_slot,
    w_gate_up,
    w_down,
    queries,
    incoming_key_value,
    key_value_pool,
    block_owner,
    block_tokens,
):
    if fits_fused(expert_ids, expert_slot):
        return fused(
            moe_input,
            expert_ids,
            route_weight,
            expert_slot,
            w_gate_up,
            w_down,
            queries,
            incoming_key_value,
            key_value_pool,
            block_owner,
            block_tokens,
        )
    moe_out = mixture(moe_input, expert_ids, route_weight, expert_slot, w_gate_up, w_down)
    scale = 1.0 / math.sqrt(HEAD_DIMENSION)
    query_rows = queries.reshape(
        DEVICE_REQUESTS, KEY_VALUE_HEADS, QUERY_HEADS // KEY_VALUE_HEADS, HEAD_DIMENSION
    )
    latest_keys = incoming_key_value[:, : KEY_VALUE_HEADS * HEAD_DIMENSION].reshape(
        DEVICE_REQUESTS, KEY_VALUE_HEADS, HEAD_DIMENSION
    )
    new_score = (
        jnp.einsum("rgjd,rgd->rgj", query_rows, latest_keys, preferred_element_type=jnp.float32)
        * scale
    )
    incoming_values = (
        incoming_key_value[:, KEY_VALUE_HEADS * HEAD_DIMENSION :]
        .reshape(DEVICE_REQUESTS, KEY_VALUE_HEADS, 1, HEAD_DIMENSION)
        .astype(jnp.float32)
    )
    maxima, totals, weighted = attend_migrate(
        query_rows, key_value_pool, block_owner, block_tokens, scale
    )
    attn_out = (
        finish(maxima, totals, weighted, new_score, incoming_values)
        .reshape(DEVICE_REQUESTS, QUERY_HEADS * HEAD_DIMENSION)
        .astype(jnp.bfloat16)
    )
    return (moe_out, attn_out)


def solution(mesh):
    placed = (
        P(("replica", "expert"), None),
        P(("replica", "expert"), None),
        P(("replica", "expert"), None),
        P(),
        P(None, ("replica", "expert")),
        P(("replica", "expert"), None),
        P(("replica", "expert"), None),
        P(("replica", "expert"), None),
        P(("replica", "expert"), None, None),
        P(("replica", "expert")),
        P(("replica", "expert")),
    )
    return jax.shard_map(
        shards,
        mesh=mesh,
        in_specs=placed,
        out_specs=(P(("replica", "expert"), None), P(("replica", "expert"), None)),
        check_vma=False,
    )
```

```python
import functools
import math

import jax
import jax.numpy as jnp
from jax import lax
from jax.experimental import pallas as pl
from jax.experimental.pallas import tpu as pltpu
from jax.sharding import PartitionSpec as P

QUART = 4
QUERY_HEADS = 64
KEY_VALUE_HEADS = 4
HEAD_DIMENSION = 128
DEVICE_REQUESTS = 2
DEVICE_BLOCKS = 16
BLOCK_SLOTS = 64
MIG = 2


HIGHEST = lax.Precision.HIGHEST


def partial_state(query_rows, rows, mask, scale):
    heads_kv = query_rows.shape[1]
    head_size = query_rows.shape[3]
    maxima = []
    totals = []
    weighted = []
    for head in range(heads_kv):
        cached_key_rows = rows[:, head * head_size : (head + 1) * head_size]
        cached_value_rows = rows[
            :, (heads_kv + head) * head_size : (heads_kv + head + 1) * head_size
        ].astype(jnp.float32)
        scores = (
            jnp.einsum(
                "rjd,nd->rjn",
                query_rows[:, head],
                cached_key_rows,
                preferred_element_type=jnp.float32,
            )
            * scale
        )
        keep = mask[:, None, :]
        largest = jnp.max(jnp.where(keep, scores, -1e30), axis=2)
        weights = jnp.where(keep, jnp.exp(scores - largest[:, :, None]), 0.0)
        maxima.append(largest)
        totals.append(jnp.sum(weights, axis=2))
        weighted.append(jnp.einsum("rjn,nd->rjd", weights, cached_value_rows, precision=HIGHEST))
    return (jnp.stack(maxima, 1), jnp.stack(totals, 1), jnp.stack(weighted, 1))


def finish(maxima, totals, weighted, new_score, incoming_values):
    best = jnp.maximum(jnp.max(maxima, axis=0), new_score)
    own_weight = jnp.exp(new_score - best)
    factor = jnp.exp(maxima - best[None])
    denom = own_weight + jnp.sum(factor * totals, axis=0)
    mixed = own_weight[..., None] * incoming_values + jnp.sum(factor[..., None] * weighted, axis=0)
    return mixed / denom[..., None]


def attend_migrate(query_rows, key_value_pool, block_owner, block_tokens, scale):
    replicas = lax.axis_size("replica")
    mine = lax.axis_index("replica")
    kv_width = key_value_pool.shape[2]
    target = block_owner // DEVICE_REQUESTS
    request = block_owner % DEVICE_REQUESTS
    leaving = target != mine
    to_replica = (
        (target[:, None] == jnp.arange(replicas, dtype=jnp.int32)[None, :]) & leaving[:, None]
    ).astype(jnp.int32)
    before = jnp.cumsum(to_replica, axis=0) - to_replica
    place = target * MIG + jnp.sum(before * to_replica, axis=1)
    select = (place[None, :] == jnp.arange(replicas * MIG, dtype=jnp.int32)[:, None]) & leaving[
        None, :
    ]
    chosen = select.astype(jnp.int32)
    send_blocks = jnp.dot(
        select.astype(jnp.bfloat16),
        key_value_pool.reshape(DEVICE_BLOCKS, BLOCK_SLOTS * kv_width),
        preferred_element_type=jnp.float32,
    ).astype(jnp.bfloat16)
    send_request = jnp.sum(chosen * request[None, :], axis=1)
    send_count = jnp.sum(chosen * block_tokens[None, :], axis=1)
    got_blocks, got_request, got_count = (
        lax.all_to_all(
            send_blocks.reshape(replicas, MIG, BLOCK_SLOTS * kv_width),
            "replica",
            split_axis=0,
            concat_axis=0,
            tiled=True,
        ),
        lax.all_to_all(
            send_request.reshape(replicas, MIG), "replica", split_axis=0, concat_axis=0, tiled=True
        ),
        lax.all_to_all(
            send_count.reshape(replicas, MIG), "replica", split_axis=0, concat_axis=0, tiled=True
        ),
    )
    positions = jnp.arange(BLOCK_SLOTS, dtype=jnp.int32)
    requests = jnp.arange(DEVICE_REQUESTS, dtype=jnp.int32)
    local_valid = (positions[None, :] < block_tokens[:, None]).reshape(-1)
    local_owner = jnp.repeat(block_owner, BLOCK_SLOTS)
    local_mask = (local_owner[None, :] == mine * DEVICE_REQUESTS + requests[:, None]) & local_valid[
        None, :
    ]
    local_state = partial_state(
        query_rows, key_value_pool.reshape(DEVICE_BLOCKS * BLOCK_SLOTS, kv_width), local_mask, scale
    )
    got_valid = (positions[None, :] < got_count.reshape(-1)[:, None]).reshape(-1)
    got_owner = jnp.repeat(got_request.reshape(-1), BLOCK_SLOTS)
    got_mask = (got_owner[None, :] == requests[:, None]) & got_valid[None, :]
    got_state = partial_state(query_rows, got_blocks.reshape(-1, kv_width), got_mask, scale)
    maxima = jnp.stack([local_state[0], got_state[0]], axis=0)
    totals = jnp.stack([local_state[1], got_state[1]], axis=0)
    weighted = jnp.stack([local_state[2], got_state[2]], axis=0)
    return (maxima, totals, weighted)


def expert_local(rows, w_gate_up, w_down):
    quarter = w_down.shape[0]
    halves = jnp.dot(rows, w_gate_up, preferred_element_type=jnp.float32)
    activation = (jax.nn.silu(halves[:, :quarter]) * halves[:, quarter:]).astype(jnp.bfloat16)
    return jnp.dot(activation, w_down, preferred_element_type=jnp.float32).astype(jnp.bfloat16)


def mixture(moe_input, expert_ids, route_weight, expert_slot, w_gate_up, w_down):
    token_rows = moe_input.shape[0]
    width = moe_input.shape[1]
    top_k = expert_ids.shape[1]
    experts = expert_slot.shape[0]
    replicas = lax.axis_size("replica")
    columns = lax.axis_size("expert")
    capacity = min(token_rows, max(2, 2 * token_rows * top_k // experts))
    flat_ids = expert_ids.reshape(-1)
    onehot = (flat_ids[:, None] == jnp.arange(experts, dtype=jnp.int32)[None, :]).astype(jnp.int32)
    before = jnp.cumsum(onehot, axis=0) - onehot
    position = jnp.sum(before * onehot, axis=1)
    slot_of = jnp.sum(onehot * expert_slot[None, :], axis=1)
    target = slot_of * capacity + position
    assign = (target[:, None] == jnp.arange(experts * capacity, dtype=jnp.int32)[None, :]).reshape(
        token_rows, top_k, experts * capacity
    )
    dispatch_map = jnp.sum(assign.astype(jnp.int32), axis=1).astype(jnp.bfloat16)
    send_rows = jnp.einsum(
        "tc,td->cd", dispatch_map, moe_input, preferred_element_type=jnp.float32
    ).astype(jnp.bfloat16)
    send = jnp.broadcast_to(
        send_rows.reshape(experts, 1, capacity, width), (experts, QUART, capacity, width)
    )
    send = send.reshape(replicas, columns, capacity, width)
    received = lax.all_to_all(
        lax.all_to_all(send, "replica", split_axis=0, concat_axis=0, tiled=True),
        "expert",
        split_axis=1,
        concat_axis=1,
        tiled=True,
    )
    quarter_part = expert_local(received.reshape(-1, width), w_gate_up, w_down)
    returned = lax.all_to_all(
        lax.all_to_all(
            quarter_part.reshape(send.shape), "replica", split_axis=0, concat_axis=0, tiled=True
        ),
        "expert",
        split_axis=1,
        concat_axis=1,
        tiled=True,
    )
    expert_out = jnp.sum(
        returned.reshape(experts, QUART, capacity, width).astype(jnp.float32), axis=1
    ).reshape(experts * capacity, width)
    mixing = jnp.sum(assign.astype(jnp.float32) * route_weight[:, :, None], axis=1)
    return jnp.dot(
        mixing, expert_out, precision=HIGHEST, preferred_element_type=jnp.float32
    ).astype(jnp.bfloat16)


CORES = 2
PAD = 128
VMEM_LIMIT = 60 * 1024 * 1024
MESH = pl.DeviceIdType.MESH


def fits_fused(expert_ids, expert_slot):
    experts = expert_slot.shape[0]
    devices = lax.axis_size("replica") * lax.axis_size("expert")
    return (
        expert_ids.shape[1] == experts
        and 3 * experts <= PAD
        and devices == experts * QUART
        and lax.axis_size("expert") % CORES == 0
    )


def fused_kernel(
    replicas,
    depth,
    experts,
    slot_ref,
    owner_ref,
    tokens_ref,
    ids_hbm,
    rw_hbm,
    q_hbm,
    new_hbm,
    x_hbm,
    wgu_hbm,
    wd_hbm,
    kv_hbm,
    moe_ref,
    attn_ref,
    ids_ref,
    rw_ref,
    q_ref,
    new_ref,
    xb,
    wgu,
    wd,
    kv,
    pf,
    cs,
    cr,
    xs,
    xr,
    zf,
    zs,
    zr,
    qb,
    accf,
    accb,
    mlb,
    ar,
    mr,
    load_sem,
    z_send,
    z_recv,
    r_send,
    r_recv,
    c_send,
    c_recv,
    q_send,
    q_recv,
    cs_send,
    cs_recv,
    xs_send,
    xs_recv,
    zs_send,
    zs_recv,
    a_send,
    a_recv,
    m_send,
    m_recv,
):
    r = lax.axis_index("replica")
    e = lax.axis_index("expert")
    z = e // CORES
    c = e % CORES
    sib = 1 - c
    rows, width = x_hbm.shape
    quarter = wd_hbm.shape[0]
    heads = KEY_VALUE_HEADS
    hd = HEAD_DIMENSION
    group = QUERY_HEADS // KEY_VALUE_HEADS
    per = DEVICE_REQUESTS * group
    scale = 1.0 / math.sqrt(HEAD_DIMENSION)
    sent = []

    def rdev(k):
        return ((r + k) % replicas, e)

    def zdev(k):
        return (r, ((z + k) % depth) * CORES + c)

    cdev = (r, z * CORES + sib)

    def remote(src, dst, ssem, rsem, dev):
        return pltpu.make_async_remote_copy(
            src_ref=src, dst_ref=dst, send_sem=ssem, recv_sem=rsem, device_id=dev, device_id_type=MESH
        )

    def push(*args):
        d = remote(*args)
        d.start()
        sent.append(d)

    loads = [
        pltpu.make_async_copy(wgu_hbm, wgu, load_sem.at[0]),
        pltpu.make_async_copy(wd_hbm, wd, load_sem.at[1]),
        pltpu.make_async_copy(kv_hbm, kv, load_sem.at[2]),
        pltpu.make_async_copy(x_hbm, xb.at[z, c, r, :, pl.ds(0, width)], load_sem.at[3]),
        pltpu.make_async_copy(ids_hbm, ids_ref, load_sem.at[4]),
        pltpu.make_async_copy(rw_hbm, rw_ref, load_sem.at[5]),
        pltpu.make_async_copy(q_hbm, q_ref, load_sem.at[6]),
        pltpu.make_async_copy(new_hbm, new_ref, load_sem.at[7]),
    ]
    for n in (3, 4, 5, 6, 7, 2, 0, 1):
        loads[n].start()

    barrier = pltpu.get_barrier_semaphore()
    for k in range(1, replicas):
        pl.semaphore_signal(barrier, inc=1, device_id=rdev(k), device_id_type=MESH)
    for k in range(1, depth):
        pl.semaphore_signal(barrier, inc=1, device_id=zdev(k), device_id_type=MESH)
    pl.semaphore_signal(barrier, inc=1, device_id=cdev, device_id_type=MESH)

    loads[4].wait()
    loads[5].wait()
    line = lax.broadcasted_iota(jnp.int32, (PAD, rows), 0)
    mix = jnp.zeros((PAD, rows), jnp.float32)
    for k in range(experts):
        chosen = ids_ref[k : k + 1, :]
        slot = jnp.zeros((1, rows), jnp.int32)
        for n in range(experts):
            slot = jnp.where(chosen == n, slot_ref[n], slot)
        mix = mix + jnp.where(line % experts == slot, rw_ref[k : k + 1, :], 0.0)
    high = mix.astype(jnp.bfloat16).astype(jnp.float32)
    rest = mix - high
    mid = rest.astype(jnp.bfloat16).astype(jnp.float32)
    low = rest - mid
    terms = jnp.where(line < experts, high, jnp.where(line < 2 * experts, mid, low))
    unit = (
        lax.broadcasted_iota(jnp.int32, (rows, rows), 0)
        == lax.broadcasted_iota(jnp.int32, (rows, rows), 1)
    ).astype(jnp.bfloat16)
    xb[z, c, r, :, width:] = lax.dot_general(
        unit,
        terms.astype(jnp.bfloat16),
        (((1,), (1,)), ((), ())),
        preferred_element_type=jnp.float32,
    ).astype(jnp.bfloat16)
    loads[6].wait()
    asked = q_ref[...].astype(jnp.float32)
    for g in range(heads):
        pieces = [asked[:, (g * group + j) * hd : (g * group + j + 1) * hd] for j in range(group)]
        qb[r, g * per : (g + 1) * per, :] = jnp.concatenate(pieces, axis=0).astype(jnp.bfloat16)
    loads[3].wait()

    pl.semaphore_wait(barrier, replicas - 1 + depth - 1 + 1)

    def xy_out(zo):
        piece = xb.at[(z + depth - zo) % depth, c, r]
        for k in range(1, replicas):
            push(piece, piece, r_send.at[zo, k], r_recv.at[zo, k], rdev(k))

    def core_out(zo, k):
        piece = xb.at[(z + depth - zo) % depth, c, (r + replicas - k) % replicas]
        push(piece, piece, c_send.at[zo, k], c_recv.at[zo, k], cdev)

    own = xb.at[z, c, r]
    for k in range(1, depth):
        push(own, own, z_send.at[k], z_recv.at[k], zdev(k))
    for k in range(1, replicas):
        push(qb.at[r], qb.at[r], q_send.at[k], q_recv.at[k], rdev(k))
    xy_out(0)
    core_out(0, 0)

    def onward(zo):
        got = xb.at[(z + depth - zo) % depth, c, r]
        remote(got, got, z_send.at[zo], z_recv.at[zo], cdev).wait_recv()
        xy_out(zo)
        core_out(zo, 0)

    if depth > 1:
        onward(1)

    for k in range(1, replicas):
        got = qb.at[(r + replicas - k) % replicas]
        remote(got, got, q_send.at[k], q_recv.at[k], cdev).wait_recv()
    loads[2].wait()
    blocks, slots = owner_ref.shape[0], kv.shape[0] // owner_ref.shape[0]
    keys = kv.shape[0]
    place = lax.broadcasted_iota(jnp.int32, (1, keys), 1)
    holder = jnp.full((1, keys), -1, jnp.int32)
    for b in range(blocks):
        inside = (place >= b * slots) & (place < b * slots + tokens_ref[b])
        holder = jnp.where(inside, owner_ref[b], holder)
    total = replicas * per
    row = lax.broadcasted_iota(jnp.int32, (total, 1), 0)
    asker = row // per * DEVICE_REQUESTS + row % DEVICE_REQUESTS
    keep = holder == asker
    mlane = lax.broadcasted_iota(jnp.int32, (total, PAD), 1)

    def head(g, ml):
        col = slice(g * hd, (g + 1) * hd)
        vcol = slice((heads + g) * hd, (heads + g + 1) * hd)
        qg = qb[:, g * per : (g + 1) * per, :].reshape(total, hd)
        scores = (
            lax.dot_general(
                qg, kv[:, col], (((1,), (1,)), ((), ())), preferred_element_type=jnp.float32
            )
            * scale
        )
        top = jnp.max(jnp.where(keep, scores, -1e30), axis=1, keepdims=True)
        weights = jnp.where(keep, jnp.exp(scores - top), 0.0)
        mass = jnp.sum(weights, axis=1, keepdims=True)
        acc = jnp.dot(
            weights.astype(jnp.bfloat16), kv[:, vcol], preferred_element_type=jnp.float32
        ).reshape(replicas, per, hd)
        accf[:, g] = acc
        accb[:, g] = acc.astype(jnp.bfloat16)
        return jnp.where(mlane == g, top, jnp.where(mlane == heads + g, mass, ml))

    def hand_back(ml):
        mlb[...] = ml.reshape(replicas, per, PAD)
        for k in range(1, replicas):
            to = (r + k) % replicas
            push(accb.at[to], ar.at[k], a_send.at[k], a_recv.at[k], rdev(k))
            push(mlb.at[to], mr.at[k], m_send.at[k], m_recv.at[k], rdev(k))

    def finish_attention():
        loads[7].wait()
        for k in range(1, replicas):
            remote(ar.at[k], ar.at[k], a_send.at[k], a_recv.at[k], cdev).wait_recv()
            remote(mr.at[k], mr.at[k], m_send.at[k], m_recv.at[k], cdev).wait_recv()
        plane = lax.broadcasted_iota(jnp.int32, (per, PAD), 1)
        mls = [mlb[r]] + [mr[k] for k in range(1, replicas)]

        def pick(values, n):
            return jnp.sum(jnp.where(plane == n, values, 0.0), axis=1, keepdims=True)

        turn = lax.broadcasted_iota(jnp.int32, (per, hd), 0) % DEVICE_REQUESTS

        def spread(n):
            values = new_ref[:, n * hd : (n + 1) * hd].astype(jnp.float32)
            wide = values[:1]
            for i in range(1, DEVICE_REQUESTS):
                wide = jnp.where(turn == i, values[i : i + 1], wide)
            return jnp.broadcast_to(wide, (per, hd))

        for g in range(heads):
            query = qb[r, g * per : (g + 1) * per, :].astype(jnp.float32)
            fresh = jnp.sum(query * spread(g), axis=1, keepdims=True) * scale
            tops = [pick(v, g) for v in mls]
            best = fresh
            for t in tops:
                best = jnp.maximum(best, t)
            weight = jnp.exp(fresh - best)
            denom = weight
            mixed = weight * spread(heads + g)
            for k in range(replicas):
                factor = jnp.exp(tops[k] - best)
                part = accf[r, g] if k == 0 else ar[k, g].astype(jnp.float32)
                denom = denom + factor * pick(mls[k], heads + g)
                mixed = mixed + factor * part
            mixed = mixed / denom
            for j in range(group):
                cols = slice((g * group + j) * hd, (g * group + j + 1) * hd)
                attn_ref[:, cols] = mixed[
                    j * DEVICE_REQUESTS : (j + 1) * DEVICE_REQUESTS, :
                ].astype(attn_ref.dtype)

    my_slot = (r * (depth * CORES) + e) // QUART
    chunk = CORES * replicas * rows
    slane = lax.broadcasted_iota(jnp.int32, (chunk, PAD), 1)
    mine = (slane % experts == my_slot) & (slane < 3 * experts)

    def gather(zo):
        for k in range(1, replicas):
            got = xb.at[(z + depth - zo) % depth, c, (r + replicas - k) % replicas]
            remote(got, got, r_send.at[zo, k], r_recv.at[zo, k], cdev).wait_recv()
            core_out(zo, k)

    def expert(zo):
        zi = (z + depth - zo) % depth
        for k in range(replicas):
            got = xb.at[zi, sib, (r + replicas - k) % replicas]
            remote(got, got, c_send.at[zo, k], c_recv.at[zo, k], cdev).wait_recv()
        block = jnp.concatenate(
            [
                xb[zi, sib].reshape(chunk // 2, width + PAD),
                xb[zi, c].reshape(chunk // 2, width + PAD),
            ],
            axis=0,
        )
        gain = jnp.sum(
            jnp.where(mine, block[:, width:].astype(jnp.float32), 0.0), axis=1, keepdims=True
        )
        halves = jnp.dot(block[:, :width], wgu[...], preferred_element_type=jnp.float32)
        gate, up = halves[:, :quarter], halves[:, quarter:]
        act = (gate / (1.0 + jnp.exp(-gate)) * up).astype(jnp.bfloat16)
        step = width // 4
        for n in range(4):
            cols = slice(n * step, (n + 1) * step)
            part = jnp.dot(act, wd[:, cols], preferred_element_type=jnp.float32) * gain
            cs[zo, :, cols] = part[: chunk // 2].astype(jnp.bfloat16)
            pf[zo, :, cols] = part[chunk // 2 :]
        push(cs.at[zo], cr.at[zo], cs_send.at[zo], cs_recv.at[zo], cdev)

    def across(zo):
        remote(cr.at[zo], cr.at[zo], cs_send.at[zo], cs_recv.at[zo], cdev).wait_recv()
        both = pf[zo] + cr[zo].astype(jnp.float32)
        pf[zo] = both
        xs[zo] = both.astype(jnp.bfloat16).reshape(replicas, rows, width)
        for k in range(1, replicas):
            to = (r + k) % replicas
            push(xs.at[zo, to], xr.at[zo, k], xs_send.at[zo, k], xs_recv.at[zo, k], rdev(k))

    def along(zo):
        total = pf[zo, pl.ds(pl.multiple_of(r * rows, rows), rows), :]
        for k in range(1, replicas):
            remote(
                xr.at[zo, k], xr.at[zo, k], xs_send.at[zo, k], xs_recv.at[zo, k], cdev
            ).wait_recv()
            total = total + xr[zo, k].astype(jnp.float32)
        if zo == 0:
            zf[...] = total
        else:
            zs[zo] = total.astype(jnp.bfloat16)
            push(zs.at[zo], zr.at[zo], zs_send.at[zo], zs_recv.at[zo], zdev(depth - zo))

    ml = head(0, jnp.zeros((total, PAD), jnp.float32))
    if depth > 2:
        onward(2)
    gather(0)
    done = 1
    if heads > 1:
        ml = head(1, ml)
        done = 2
    for zo in range(3, depth):
        onward(zo)
    loads[0].wait()
    loads[1].wait()
    for zo in range(depth + 2):
        if zo < depth:
            expert(zo)
        if 0 <= zo - 1 < depth:
            across(zo - 1)
        if zo + 1 < depth:
            gather(zo + 1)
        last = heads if zo == 1 else min(done + 1, heads)
        if done < heads:
            for g in range(done, last):
                ml = head(g, ml)
            done = last
            if done == heads:
                hand_back(ml)
        if zo == depth + 1:
            finish_attention()
        if 0 <= zo - 2 < depth:
            along(zo - 2)
    result = zf[...]
    for zo in range(1, depth):
        remote(zr.at[zo], zr.at[zo], zs_send.at[zo], zs_recv.at[zo], cdev).wait_recv()
        result = result + zr[zo].astype(jnp.float32)
    moe_ref[...] = result.astype(moe_ref.dtype)
    for d in sent:
        d.wait_send()


def place_results(moe_ref, attn_ref, moe_out, attn_out, moe_v, attn_v, sem):
    ins = [
        pltpu.make_async_copy(moe_ref, moe_v, sem.at[0]),
        pltpu.make_async_copy(attn_ref, attn_v, sem.at[1]),
    ]
    outs = [
        pltpu.make_async_copy(moe_v, moe_out, sem.at[2]),
        pltpu.make_async_copy(attn_v, attn_out, sem.at[3]),
    ]
    for d in ins:
        d.start()
    for i, o in zip(ins, outs):
        i.wait()
        o.start()
    for o in outs:
        o.wait()


def fused(
    moe_input,
    expert_ids,
    route_weight,
    expert_slot,
    w_gate_up,
    w_down,
    queries,
    incoming_key_value,
    key_value_pool,
    block_owner,
    block_tokens,
):
    replicas = lax.axis_size("replica")
    depth = lax.axis_size("expert") // CORES
    experts = expert_slot.shape[0]
    rows, width = moe_input.shape
    group = QUERY_HEADS // KEY_VALUE_HEADS
    per = DEVICE_REQUESTS * group
    hd = HEAD_DIMENSION
    keys = key_value_pool.shape[0] * key_value_pool.shape[1]
    smem = pl.BlockSpec(memory_space=pltpu.SMEM)
    vmem = pl.BlockSpec(memory_space=pltpu.VMEM)
    hbm = pl.BlockSpec(memory_space=pl.ANY)
    bf, f32 = jnp.bfloat16, jnp.float32
    dma = pltpu.SemaphoreType.DMA
    moe_out, attn = pl.pallas_call(
        functools.partial(fused_kernel, replicas, depth, experts),
        out_shape=(
            jax.ShapeDtypeStruct((rows, width), bf),
            jax.ShapeDtypeStruct(queries.shape, bf),
        ),
        in_specs=[smem] * 3 + [hbm] * 8,
        out_specs=(vmem, vmem),
        scratch_shapes=[
            pltpu.VMEM(expert_ids.shape[::-1], expert_ids.dtype),
            pltpu.VMEM(route_weight.shape[::-1], f32),
            pltpu.VMEM(queries.shape, bf),
            pltpu.VMEM(incoming_key_value.shape, bf),
            pltpu.VMEM((depth, CORES, replicas, rows, width + PAD), bf),
            pltpu.VMEM(w_gate_up.shape, bf),
            pltpu.VMEM(w_down.shape, bf),
            pltpu.VMEM((keys, key_value_pool.shape[2]), bf),
            pltpu.VMEM((depth, replicas * rows, width), f32),
            pltpu.VMEM((depth, replicas * rows, width), bf),
            pltpu.VMEM((depth, replicas * rows, width), bf),
            pltpu.VMEM((depth, replicas, rows, width), bf),
            pltpu.VMEM((depth, replicas, rows, width), bf),
            pltpu.VMEM((rows, width), f32),
            pltpu.VMEM((depth, rows, width), bf),
            pltpu.VMEM((depth, rows, width), bf),
            pltpu.VMEM((replicas, KEY_VALUE_HEADS * per, hd), bf),
            pltpu.VMEM((replicas, KEY_VALUE_HEADS, per, hd), f32),
            pltpu.VMEM((replicas, KEY_VALUE_HEADS, per, hd), bf),
            pltpu.VMEM((replicas, per, PAD), f32),
            pltpu.VMEM((replicas, KEY_VALUE_HEADS, per, hd), bf),
            pltpu.VMEM((replicas, per, PAD), f32),
            dma((8,)),
            dma((depth,)),
            dma((depth,)),
            dma((depth, replicas)),
            dma((depth, replicas)),
            dma((depth, replicas)),
            dma((depth, replicas)),
            dma((replicas,)),
            dma((replicas,)),
            dma((depth,)),
            dma((depth,)),
            dma((depth, replicas)),
            dma((depth, replicas)),
            dma((depth,)),
            dma((depth,)),
            dma((replicas,)),
            dma((replicas,)),
            dma((replicas,)),
            dma((replicas,)),
        ],
        compiler_params=pltpu.CompilerParams(
            collective_id=0, has_side_effects=True, vmem_limit_bytes=VMEM_LIMIT
        ),
    )(
        expert_slot,
        block_owner,
        block_tokens,
        expert_ids.T,
        route_weight.T,
        queries,
        incoming_key_value,
        moe_input,
        w_gate_up,
        w_down,
        key_value_pool.reshape(keys, key_value_pool.shape[2]),
    )
    return pl.pallas_call(
        place_results,
        out_shape=(
            jax.ShapeDtypeStruct(moe_out.shape, bf),
            jax.ShapeDtypeStruct(attn.shape, bf),
        ),
        in_specs=[hbm] * 2,
        out_specs=(hbm, hbm),
        scratch_shapes=[
            pltpu.VMEM(moe_out.shape, bf),
            pltpu.VMEM(attn.shape, bf),
            dma((4,)),
        ],
        compiler_params=pltpu.CompilerParams(vmem_limit_bytes=VMEM_LIMIT),
    )(moe_out, attn)


def shards(
    moe_input,
    expert_ids,
    route_weight,
    expert_slot,
    w_gate_up,
    w_down,
    queries,
    incoming_key_value,
    key_value_pool,
    block_owner,
    block_tokens,
):
    if fits_fused(expert_ids, expert_slot):
        return fused(
            moe_input,
            expert_ids,
            route_weight,
            expert_slot,
            w_gate_up,
            w_down,
            queries,
            incoming_key_value,
            key_value_pool,
            block_owner,
            block_tokens,
        )
    moe_out = mixture(moe_input, expert_ids, route_weight, expert_slot, w_gate_up, w_down)
    scale = 1.0 / math.sqrt(HEAD_DIMENSION)
    query_rows = queries.reshape(
        DEVICE_REQUESTS, KEY_VALUE_HEADS, QUERY_HEADS // KEY_VALUE_HEADS, HEAD_DIMENSION
    )
    latest_keys = incoming_key_value[:, : KEY_VALUE_HEADS * HEAD_DIMENSION].reshape(
        DEVICE_REQUESTS, KEY_VALUE_HEADS, HEAD_DIMENSION
    )
    new_score = (
        jnp.einsum("rgjd,rgd->rgj", query_rows, latest_keys, preferred_element_type=jnp.float32)
        * scale
    )
    incoming_values = (
        incoming_key_value[:, KEY_VALUE_HEADS * HEAD_DIMENSION :]
        .reshape(DEVICE_REQUESTS, KEY_VALUE_HEADS, 1, HEAD_DIMENSION)
        .astype(jnp.float32)
    )
    maxima, totals, weighted = attend_migrate(
        query_rows, key_value_pool, block_owner, block_tokens, scale
    )
    attn_out = (
        finish(maxima, totals, weighted, new_score, incoming_values)
        .reshape(DEVICE_REQUESTS, QUERY_HEADS * HEAD_DIMENSION)
        .astype(jnp.bfloat16)
    )
    return (moe_out, attn_out)


def solution(mesh):
    placed = (
        P(("replica", "expert"), None),
        P(("replica", "expert"), None),
        P(("replica", "expert"), None),
        P(),
        P(None, ("replica", "expert")),
        P(("replica", "expert"), None),
        P(("replica", "expert"), None),
        P(("replica", "expert"), None),
        P(("replica", "expert"), None, None),
        P(("replica", "expert")),
        P(("replica", "expert")),
    )
    return jax.shard_map(
        shards,
        mesh=mesh,
        in_specs=placed,
        out_specs=(P(("replica", "expert"), None), P(("replica", "expert"), None)),
        check_vma=False,
    )
```

```python
import functools
import math

import jax
import jax.numpy as jnp
from jax import lax
from jax.experimental import pallas as pl
from jax.experimental.pallas import tpu as pltpu
from jax.sharding import PartitionSpec as P

QUART = 4
QUERY_HEADS = 64
KEY_VALUE_HEADS = 4
HEAD_DIMENSION = 128
DEVICE_REQUESTS = 2
DEVICE_BLOCKS = 16
BLOCK_SLOTS = 64
MIG = 2


HIGHEST = lax.Precision.HIGHEST


def partial_state(query_rows, rows, mask, scale):
    heads_kv = query_rows.shape[1]
    head_size = query_rows.shape[3]
    maxima = []
    totals = []
    weighted = []
    for head in range(heads_kv):
        cached_key_rows = rows[:, head * head_size : (head + 1) * head_size]
        cached_value_rows = rows[
            :, (heads_kv + head) * head_size : (heads_kv + head + 1) * head_size
        ].astype(jnp.float32)
        scores = (
            jnp.einsum(
                "rjd,nd->rjn",
                query_rows[:, head],
                cached_key_rows,
                preferred_element_type=jnp.float32,
            )
            * scale
        )
        keep = mask[:, None, :]
        largest = jnp.max(jnp.where(keep, scores, -1e30), axis=2)
        weights = jnp.where(keep, jnp.exp(scores - largest[:, :, None]), 0.0)
        maxima.append(largest)
        totals.append(jnp.sum(weights, axis=2))
        weighted.append(jnp.einsum("rjn,nd->rjd", weights, cached_value_rows, precision=HIGHEST))
    return (jnp.stack(maxima, 1), jnp.stack(totals, 1), jnp.stack(weighted, 1))


def finish(maxima, totals, weighted, new_score, incoming_values):
    best = jnp.maximum(jnp.max(maxima, axis=0), new_score)
    own_weight = jnp.exp(new_score - best)
    factor = jnp.exp(maxima - best[None])
    denom = own_weight + jnp.sum(factor * totals, axis=0)
    mixed = own_weight[..., None] * incoming_values + jnp.sum(factor[..., None] * weighted, axis=0)
    return mixed / denom[..., None]


def attend_migrate(query_rows, key_value_pool, block_owner, block_tokens, scale):
    replicas = lax.axis_size("replica")
    mine = lax.axis_index("replica")
    kv_width = key_value_pool.shape[2]
    target = block_owner // DEVICE_REQUESTS
    request = block_owner % DEVICE_REQUESTS
    leaving = target != mine
    to_replica = (
        (target[:, None] == jnp.arange(replicas, dtype=jnp.int32)[None, :]) & leaving[:, None]
    ).astype(jnp.int32)
    before = jnp.cumsum(to_replica, axis=0) - to_replica
    place = target * MIG + jnp.sum(before * to_replica, axis=1)
    select = (place[None, :] == jnp.arange(replicas * MIG, dtype=jnp.int32)[:, None]) & leaving[
        None, :
    ]
    chosen = select.astype(jnp.int32)
    send_blocks = jnp.dot(
        select.astype(jnp.bfloat16),
        key_value_pool.reshape(DEVICE_BLOCKS, BLOCK_SLOTS * kv_width),
        preferred_element_type=jnp.float32,
    ).astype(jnp.bfloat16)
    send_request = jnp.sum(chosen * request[None, :], axis=1)
    send_count = jnp.sum(chosen * block_tokens[None, :], axis=1)
    got_blocks, got_request, got_count = (
        lax.all_to_all(
            send_blocks.reshape(replicas, MIG, BLOCK_SLOTS * kv_width),
            "replica",
            split_axis=0,
            concat_axis=0,
            tiled=True,
        ),
        lax.all_to_all(
            send_request.reshape(replicas, MIG), "replica", split_axis=0, concat_axis=0, tiled=True
        ),
        lax.all_to_all(
            send_count.reshape(replicas, MIG), "replica", split_axis=0, concat_axis=0, tiled=True
        ),
    )
    positions = jnp.arange(BLOCK_SLOTS, dtype=jnp.int32)
    requests = jnp.arange(DEVICE_REQUESTS, dtype=jnp.int32)
    local_valid = (positions[None, :] < block_tokens[:, None]).reshape(-1)
    local_owner = jnp.repeat(block_owner, BLOCK_SLOTS)
    local_mask = (local_owner[None, :] == mine * DEVICE_REQUESTS + requests[:, None]) & local_valid[
        None, :
    ]
    local_state = partial_state(
        query_rows, key_value_pool.reshape(DEVICE_BLOCKS * BLOCK_SLOTS, kv_width), local_mask, scale
    )
    got_valid = (positions[None, :] < got_count.reshape(-1)[:, None]).reshape(-1)
    got_owner = jnp.repeat(got_request.reshape(-1), BLOCK_SLOTS)
    got_mask = (got_owner[None, :] == requests[:, None]) & got_valid[None, :]
    got_state = partial_state(query_rows, got_blocks.reshape(-1, kv_width), got_mask, scale)
    maxima = jnp.stack([local_state[0], got_state[0]], axis=0)
    totals = jnp.stack([local_state[1], got_state[1]], axis=0)
    weighted = jnp.stack([local_state[2], got_state[2]], axis=0)
    return (maxima, totals, weighted)


def expert_local(rows, w_gate_up, w_down):
    quarter = w_down.shape[0]
    halves = jnp.dot(rows, w_gate_up, preferred_element_type=jnp.float32)
    activation = (jax.nn.silu(halves[:, :quarter]) * halves[:, quarter:]).astype(jnp.bfloat16)
    return jnp.dot(activation, w_down, preferred_element_type=jnp.float32).astype(jnp.bfloat16)


def mixture(moe_input, expert_ids, route_weight, expert_slot, w_gate_up, w_down):
    token_rows = moe_input.shape[0]
    width = moe_input.shape[1]
    top_k = expert_ids.shape[1]
    experts = expert_slot.shape[0]
    replicas = lax.axis_size("replica")
    columns = lax.axis_size("expert")
    capacity = min(token_rows, max(2, 2 * token_rows * top_k // experts))
    flat_ids = expert_ids.reshape(-1)
    onehot = (flat_ids[:, None] == jnp.arange(experts, dtype=jnp.int32)[None, :]).astype(jnp.int32)
    before = jnp.cumsum(onehot, axis=0) - onehot
    position = jnp.sum(before * onehot, axis=1)
    slot_of = jnp.sum(onehot * expert_slot[None, :], axis=1)
    target = slot_of * capacity + position
    assign = (target[:, None] == jnp.arange(experts * capacity, dtype=jnp.int32)[None, :]).reshape(
        token_rows, top_k, experts * capacity
    )
    dispatch_map = jnp.sum(assign.astype(jnp.int32), axis=1).astype(jnp.bfloat16)
    send_rows = jnp.einsum(
        "tc,td->cd", dispatch_map, moe_input, preferred_element_type=jnp.float32
    ).astype(jnp.bfloat16)
    send = jnp.broadcast_to(
        send_rows.reshape(experts, 1, capacity, width), (experts, QUART, capacity, width)
    )
    send = send.reshape(replicas, columns, capacity, width)
    received = lax.all_to_all(
        lax.all_to_all(send, "replica", split_axis=0, concat_axis=0, tiled=True),
        "expert",
        split_axis=1,
        concat_axis=1,
        tiled=True,
    )
    quarter_part = expert_local(received.reshape(-1, width), w_gate_up, w_down)
    returned = lax.all_to_all(
        lax.all_to_all(
            quarter_part.reshape(send.shape), "replica", split_axis=0, concat_axis=0, tiled=True
        ),
        "expert",
        split_axis=1,
        concat_axis=1,
        tiled=True,
    )
    expert_out = jnp.sum(
        returned.reshape(experts, QUART, capacity, width).astype(jnp.float32), axis=1
    ).reshape(experts * capacity, width)
    mixing = jnp.sum(assign.astype(jnp.float32) * route_weight[:, :, None], axis=1)
    return jnp.dot(
        mixing, expert_out, precision=HIGHEST, preferred_element_type=jnp.float32
    ).astype(jnp.bfloat16)


CORES = 2
PAD = 128
VMEM_LIMIT = 60 * 1024 * 1024
MESH = pl.DeviceIdType.MESH


def fits_fused(expert_ids, expert_slot):
    experts = expert_slot.shape[0]
    devices = lax.axis_size("replica") * lax.axis_size("expert")
    return (
        expert_ids.shape[1] == experts
        and 3 * experts <= PAD
        and devices == experts * QUART
        and lax.axis_size("expert") % CORES == 0
        and lax.axis_size("expert") >= 2 * CORES
        and QUART % CORES == 0
    )


def fused_kernel(
    replicas,
    depth,
    experts,
    slot_ref,
    owner_ref,
    tokens_ref,
    ids_hbm,
    rw_hbm,
    q_hbm,
    new_hbm,
    x_hbm,
    wgu_hbm,
    wd_hbm,
    kv_hbm,
    moe_ref,
    attn_ref,
    ids_ref,
    rw_ref,
    q_ref,
    new_ref,
    xb,
    wgu,
    wd,
    kv,
    pf,
    xs,
    xr,
    zf,
    zs,
    zr,
    qb,
    accf,
    accb,
    mlb,
    ar,
    mr,
    load_sem,
    z_send,
    z_recv,
    r_send,
    r_recv,
    w_send,
    w_recv,
    q_send,
    q_recv,
    xs_send,
    xs_recv,
    zs_send,
    zs_recv,
    a_send,
    a_recv,
    m_send,
    m_recv,
):
    r = lax.axis_index("replica")
    e = lax.axis_index("expert")
    z = e // CORES
    c = e % CORES
    sib = 1 - c
    rows, width = x_hbm.shape
    quarter = wd_hbm.shape[0]
    heads = KEY_VALUE_HEADS
    hd = HEAD_DIMENSION
    group = QUERY_HEADS // KEY_VALUE_HEADS
    per = DEVICE_REQUESTS * group
    scale = 1.0 / math.sqrt(HEAD_DIMENSION)
    sent = []

    def rdev(k):
        return ((r + k) % replicas, e)

    def zdev(k):
        return (r, ((z + k) % depth) * CORES + c)

    cdev = (r, z * CORES + sib)

    def remote(src, dst, ssem, rsem, dev):
        return pltpu.make_async_remote_copy(
            src_ref=src, dst_ref=dst, send_sem=ssem, recv_sem=rsem, device_id=dev, device_id_type=MESH
        )

    def push(*args):
        d = remote(*args)
        d.start()
        sent.append(d)

    loads = [
        pltpu.make_async_copy(wgu_hbm, wgu.at[:, pl.ds(0, 2 * quarter)], load_sem.at[0]),
        pltpu.make_async_copy(wd_hbm, wd.at[pl.ds(0, quarter)], load_sem.at[1]),
        pltpu.make_async_copy(kv_hbm, kv, load_sem.at[2]),
        pltpu.make_async_copy(x_hbm, xb.at[z, r, :, pl.ds(0, width)], load_sem.at[3]),
        pltpu.make_async_copy(ids_hbm, ids_ref, load_sem.at[4]),
        pltpu.make_async_copy(rw_hbm, rw_ref, load_sem.at[5]),
        pltpu.make_async_copy(q_hbm, q_ref, load_sem.at[6]),
        pltpu.make_async_copy(new_hbm, new_ref, load_sem.at[7]),
    ]
    for n in (3, 4, 5, 6, 7, 2, 0, 1):
        loads[n].start()

    barrier = pltpu.get_barrier_semaphore()
    for k in range(1, replicas):
        pl.semaphore_signal(barrier, inc=1, device_id=rdev(k), device_id_type=MESH)
    for k in range(1, depth):
        pl.semaphore_signal(barrier, inc=1, device_id=zdev(k), device_id_type=MESH)
    pl.semaphore_signal(barrier, inc=1, device_id=cdev, device_id_type=MESH)

    loads[4].wait()
    loads[5].wait()
    line = lax.broadcasted_iota(jnp.int32, (PAD, rows), 0)
    mix = jnp.zeros((PAD, rows), jnp.float32)
    for k in range(experts):
        chosen = ids_ref[k : k + 1, :]
        slot = jnp.zeros((1, rows), jnp.int32)
        for n in range(experts):
            slot = jnp.where(chosen == n, slot_ref[n], slot)
        mix = mix + jnp.where(line % experts == slot, rw_ref[k : k + 1, :], 0.0)
    high = mix.astype(jnp.bfloat16).astype(jnp.float32)
    rest = mix - high
    mid = rest.astype(jnp.bfloat16).astype(jnp.float32)
    low = rest - mid
    terms = jnp.where(line < experts, high, jnp.where(line < 2 * experts, mid, low))
    unit = (
        lax.broadcasted_iota(jnp.int32, (rows, rows), 0)
        == lax.broadcasted_iota(jnp.int32, (rows, rows), 1)
    ).astype(jnp.bfloat16)
    xb[z, r, :, width:] = lax.dot_general(
        unit,
        terms.astype(jnp.bfloat16),
        (((1,), (1,)), ((), ())),
        preferred_element_type=jnp.float32,
    ).astype(jnp.bfloat16)
    loads[6].wait()
    asked = q_ref[...].astype(jnp.float32)
    for g in range(heads):
        pieces = [asked[:, (g * group + j) * hd : (g * group + j + 1) * hd] for j in range(group)]
        qb[r, g * per : (g + 1) * per, :] = jnp.concatenate(pieces, axis=0).astype(jnp.bfloat16)
    loads[3].wait()

    pl.semaphore_wait(barrier, replicas - 1 + depth - 1 + 1)

    def xy_out(zo):
        piece = xb.at[(z + depth - zo) % depth, r]
        for k in range(1, replicas):
            push(piece, piece, r_send.at[zo, k], r_recv.at[zo, k], rdev(k))

    def weights_in():
        both = [
            (
                wgu_hbm.at[pl.ds(n * (width // 4), width // 4)],
                wgu.at[pl.ds(n * (width // 4), width // 4), pl.ds(2 * quarter, 2 * quarter)],
            )
            for n in range(4)
        ] + [(wd_hbm, wd.at[pl.ds(quarter, quarter)])]
        return [
            remote(src, dst, w_send.at[n], w_recv.at[n], cdev) for n, (src, dst) in enumerate(both)
        ]

    own = xb.at[z, r]
    for k in range(1, depth):
        push(own, own, z_send.at[k], z_recv.at[k], zdev(k))
    for k in range(1, replicas):
        push(qb.at[r], qb.at[r], q_send.at[k], q_recv.at[k], rdev(k))
    xy_out(0)
    for d in weights_in():
        d.start()
        sent.append(d)

    def onward(zo):
        got = xb.at[(z + depth - zo) % depth, r]
        remote(got, got, z_send.at[zo], z_recv.at[zo], cdev).wait_recv()
        xy_out(zo)

    if depth > 1:
        onward(1)

    for k in range(1, replicas):
        got = qb.at[(r + replicas - k) % replicas]
        remote(got, got, q_send.at[k], q_recv.at[k], cdev).wait_recv()
    loads[2].wait()
    blocks, slots = owner_ref.shape[0], kv.shape[0] // owner_ref.shape[0]
    keys = kv.shape[0]
    place = lax.broadcasted_iota(jnp.int32, (1, keys), 1)
    holder = jnp.full((1, keys), -1, jnp.int32)
    for b in range(blocks):
        inside = (place >= b * slots) & (place < b * slots + tokens_ref[b])
        holder = jnp.where(inside, owner_ref[b], holder)
    total = replicas * per
    row = lax.broadcasted_iota(jnp.int32, (total, 1), 0)
    asker = row // per * DEVICE_REQUESTS + row % DEVICE_REQUESTS
    keep = holder == asker
    mlane = lax.broadcasted_iota(jnp.int32, (total, PAD), 1)

    def head(g, ml):
        col = slice(g * hd, (g + 1) * hd)
        vcol = slice((heads + g) * hd, (heads + g + 1) * hd)
        qg = qb[:, g * per : (g + 1) * per, :].reshape(total, hd)
        scores = (
            lax.dot_general(
                qg, kv[:, col], (((1,), (1,)), ((), ())), preferred_element_type=jnp.float32
            )
            * scale
        )
        top = jnp.max(jnp.where(keep, scores, -1e30), axis=1, keepdims=True)
        weights = jnp.where(keep, jnp.exp(scores - top), 0.0)
        mass = jnp.sum(weights, axis=1, keepdims=True)
        acc = jnp.dot(
            weights.astype(jnp.bfloat16), kv[:, vcol], preferred_element_type=jnp.float32
        ).reshape(replicas, per, hd)
        accf[:, g] = acc
        accb[:, g] = acc.astype(jnp.bfloat16)
        return jnp.where(mlane == g, top, jnp.where(mlane == heads + g, mass, ml))

    def hand_back(ml):
        mlb[...] = ml.reshape(replicas, per, PAD)
        for k in range(1, replicas):
            to = (r + k) % replicas
            push(accb.at[to], ar.at[k], a_send.at[k], a_recv.at[k], rdev(k))
            push(mlb.at[to], mr.at[k], m_send.at[k], m_recv.at[k], rdev(k))

    def finish_attention():
        loads[7].wait()
        for k in range(1, replicas):
            remote(ar.at[k], ar.at[k], a_send.at[k], a_recv.at[k], cdev).wait_recv()
            remote(mr.at[k], mr.at[k], m_send.at[k], m_recv.at[k], cdev).wait_recv()
        plane = lax.broadcasted_iota(jnp.int32, (per, PAD), 1)
        mls = [mlb[r]] + [mr[k] for k in range(1, replicas)]

        def pick(values, n):
            return jnp.sum(jnp.where(plane == n, values, 0.0), axis=1, keepdims=True)

        turn = lax.broadcasted_iota(jnp.int32, (per, hd), 0) % DEVICE_REQUESTS

        def spread(n):
            values = new_ref[:, n * hd : (n + 1) * hd].astype(jnp.float32)
            wide = values[:1]
            for i in range(1, DEVICE_REQUESTS):
                wide = jnp.where(turn == i, values[i : i + 1], wide)
            return jnp.broadcast_to(wide, (per, hd))

        for g in range(heads):
            query = qb[r, g * per : (g + 1) * per, :].astype(jnp.float32)
            fresh = jnp.sum(query * spread(g), axis=1, keepdims=True) * scale
            tops = [pick(v, g) for v in mls]
            best = fresh
            for t in tops:
                best = jnp.maximum(best, t)
            weight = jnp.exp(fresh - best)
            denom = weight
            mixed = weight * spread(heads + g)
            for k in range(replicas):
                factor = jnp.exp(tops[k] - best)
                part = accf[r, g] if k == 0 else ar[k, g].astype(jnp.float32)
                denom = denom + factor * pick(mls[k], heads + g)
                mixed = mixed + factor * part
            mixed = mixed / denom
            for j in range(group):
                cols = slice((g * group + j) * hd, (g * group + j + 1) * hd)
                attn_ref[:, cols] = mixed[
                    j * DEVICE_REQUESTS : (j + 1) * DEVICE_REQUESTS, :
                ].astype(attn_ref.dtype)

    my_slot = (r * (depth * CORES) + e) // QUART
    chunk = replicas * rows

    def gather(zo):
        for k in range(1, replicas):
            got = xb.at[(z + depth - zo) % depth, (r + replicas - k) % replicas]
            remote(got, got, r_send.at[zo, k], r_recv.at[zo, k], cdev).wait_recv()

    def expert(group_of):
        tall = len(group_of) * chunk
        block = jnp.concatenate(
            [xb[(z + depth - zo) % depth].reshape(chunk, width + PAD) for zo in group_of], axis=0
        )
        slane = lax.broadcasted_iota(jnp.int32, (tall, PAD), 1)
        mine = (slane % experts == my_slot) & (slane < 3 * experts)
        gain = jnp.sum(
            jnp.where(mine, block[:, width:].astype(jnp.float32), 0.0), axis=1, keepdims=True
        )
        halves = jnp.dot(block[:, :width], wgu[...], preferred_element_type=jnp.float32)
        acts = []
        for n in range(CORES):
            gate = halves[:, 2 * n * quarter : (2 * n + 1) * quarter]
            up = halves[:, (2 * n + 1) * quarter : (2 * n + 2) * quarter]
            acts.append((gate / (1.0 + jnp.exp(-gate)) * up).astype(jnp.bfloat16))
        step = width // 4
        for m in range(4):
            cols = slice(m * step, (m + 1) * step)
            part = jnp.dot(acts[0], wd[:quarter, cols], preferred_element_type=jnp.float32)
            part = part + jnp.dot(acts[1], wd[quarter:, cols], preferred_element_type=jnp.float32)
            part = part * gain
            for i, zo in enumerate(group_of):
                own_part = part[i * chunk : (i + 1) * chunk]
                pf[zo, :, cols] = own_part
                xs[zo, :, :, cols] = own_part.astype(jnp.bfloat16).reshape(replicas, rows, step)
        for zo in group_of:
            for k in range(1, replicas):
                to = (r + k) % replicas
                push(xs.at[zo, to], xr.at[zo, k], xs_send.at[zo, k], xs_recv.at[zo, k], rdev(k))

    def along(zo):
        total = pf[zo, pl.ds(pl.multiple_of(r * rows, rows), rows), :]
        for k in range(1, replicas):
            remote(
                xr.at[zo, k], xr.at[zo, k], xs_send.at[zo, k], xs_recv.at[zo, k], cdev
            ).wait_recv()
            total = total + xr[zo, k].astype(jnp.float32)
        if zo == 0:
            zf[...] = total
        else:
            zs[zo] = total.astype(jnp.bfloat16)
            push(zs.at[zo], zr.at[zo], zs_send.at[zo], zs_recv.at[zo], zdev(depth - zo))

    ml = head(0, jnp.zeros((total, PAD), jnp.float32))
    if depth > 2:
        onward(2)
    gather(0)
    done = 1
    if heads > 1:
        ml = head(1, ml)
        done = 2
    for zo in range(3, depth):
        onward(zo)
    loads[0].wait()
    loads[1].wait()
    for d in weights_in():
        d.wait_recv()
    gather(1)
    expert((0, 1))
    for g in range(done, heads):
        ml = head(g, ml)
    hand_back(ml)
    for zo in range(2, depth):
        gather(zo)
        expert((zo,))
        along(zo - 2)
    for zo in range(max(depth - 2, 0), depth):
        if zo == depth - 1:
            finish_attention()
        along(zo)
    result = zf[...]
    for zo in range(1, depth):
        remote(zr.at[zo], zr.at[zo], zs_send.at[zo], zs_recv.at[zo], cdev).wait_recv()
        result = result + zr[zo].astype(jnp.float32)
    moe_ref[...] = result.astype(moe_ref.dtype)
    for d in sent:
        d.wait_send()


def place_results(moe_ref, attn_ref, moe_out, attn_out, moe_v, attn_v, sem):
    ins = [
        pltpu.make_async_copy(moe_ref, moe_v, sem.at[0]),
        pltpu.make_async_copy(attn_ref, attn_v, sem.at[1]),
    ]
    outs = [
        pltpu.make_async_copy(moe_v, moe_out, sem.at[2]),
        pltpu.make_async_copy(attn_v, attn_out, sem.at[3]),
    ]
    for d in ins:
        d.start()
    for i, o in zip(ins, outs):
        i.wait()
        o.start()
    for o in outs:
        o.wait()


def fused(
    moe_input,
    expert_ids,
    route_weight,
    expert_slot,
    w_gate_up,
    w_down,
    queries,
    incoming_key_value,
    key_value_pool,
    block_owner,
    block_tokens,
):
    replicas = lax.axis_size("replica")
    depth = lax.axis_size("expert") // CORES
    experts = expert_slot.shape[0]
    rows, width = moe_input.shape
    group = QUERY_HEADS // KEY_VALUE_HEADS
    per = DEVICE_REQUESTS * group
    hd = HEAD_DIMENSION
    keys = key_value_pool.shape[0] * key_value_pool.shape[1]
    smem = pl.BlockSpec(memory_space=pltpu.SMEM)
    vmem = pl.BlockSpec(memory_space=pltpu.VMEM)
    hbm = pl.BlockSpec(memory_space=pl.ANY)
    bf, f32 = jnp.bfloat16, jnp.float32
    dma = pltpu.SemaphoreType.DMA
    moe_out, attn = pl.pallas_call(
        functools.partial(fused_kernel, replicas, depth, experts),
        out_shape=(
            jax.ShapeDtypeStruct((rows, width), bf),
            jax.ShapeDtypeStruct(queries.shape, bf),
        ),
        in_specs=[smem] * 3 + [hbm] * 8,
        out_specs=(vmem, vmem),
        scratch_shapes=[
            pltpu.VMEM(expert_ids.shape[::-1], expert_ids.dtype),
            pltpu.VMEM(route_weight.shape[::-1], f32),
            pltpu.VMEM(queries.shape, bf),
            pltpu.VMEM(incoming_key_value.shape, bf),
            pltpu.VMEM((depth, replicas, rows, width + PAD), bf),
            pltpu.VMEM((width, CORES * w_gate_up.shape[1]), bf),
            pltpu.VMEM((CORES * w_down.shape[0], width), bf),
            pltpu.VMEM((keys, key_value_pool.shape[2]), bf),
            pltpu.VMEM((depth, replicas * rows, width), f32),
            pltpu.VMEM((depth, replicas, rows, width), bf),
            pltpu.VMEM((depth, replicas, rows, width), bf),
            pltpu.VMEM((rows, width), f32),
            pltpu.VMEM((depth, rows, width), bf),
            pltpu.VMEM((depth, rows, width), bf),
            pltpu.VMEM((replicas, KEY_VALUE_HEADS * per, hd), bf),
            pltpu.VMEM((replicas, KEY_VALUE_HEADS, per, hd), f32),
            pltpu.VMEM((replicas, KEY_VALUE_HEADS, per, hd), bf),
            pltpu.VMEM((replicas, per, PAD), f32),
            pltpu.VMEM((replicas, KEY_VALUE_HEADS, per, hd), bf),
            pltpu.VMEM((replicas, per, PAD), f32),
            dma((8,)),
            dma((depth,)),
            dma((depth,)),
            dma((depth, replicas)),
            dma((depth, replicas)),
            dma((5,)),
            dma((5,)),
            dma((replicas,)),
            dma((replicas,)),
            dma((depth, replicas)),
            dma((depth, replicas)),
            dma((depth,)),
            dma((depth,)),
            dma((replicas,)),
            dma((replicas,)),
            dma((replicas,)),
            dma((replicas,)),
        ],
        compiler_params=pltpu.CompilerParams(
            collective_id=0, has_side_effects=True, vmem_limit_bytes=VMEM_LIMIT
        ),
    )(
        expert_slot,
        block_owner,
        block_tokens,
        expert_ids.T,
        route_weight.T,
        queries,
        incoming_key_value,
        moe_input,
        w_gate_up,
        w_down,
        key_value_pool.reshape(keys, key_value_pool.shape[2]),
    )
    return pl.pallas_call(
        place_results,
        out_shape=(
            jax.ShapeDtypeStruct(moe_out.shape, bf),
            jax.ShapeDtypeStruct(attn.shape, bf),
        ),
        in_specs=[hbm] * 2,
        out_specs=(hbm, hbm),
        scratch_shapes=[
            pltpu.VMEM(moe_out.shape, bf),
            pltpu.VMEM(attn.shape, bf),
            dma((4,)),
        ],
        compiler_params=pltpu.CompilerParams(vmem_limit_bytes=VMEM_LIMIT),
    )(moe_out, attn)


def shards(
    moe_input,
    expert_ids,
    route_weight,
    expert_slot,
    w_gate_up,
    w_down,
    queries,
    incoming_key_value,
    key_value_pool,
    block_owner,
    block_tokens,
):
    if fits_fused(expert_ids, expert_slot):
        return fused(
            moe_input,
            expert_ids,
            route_weight,
            expert_slot,
            w_gate_up,
            w_down,
            queries,
            incoming_key_value,
            key_value_pool,
            block_owner,
            block_tokens,
        )
    moe_out = mixture(moe_input, expert_ids, route_weight, expert_slot, w_gate_up, w_down)
    scale = 1.0 / math.sqrt(HEAD_DIMENSION)
    query_rows = queries.reshape(
        DEVICE_REQUESTS, KEY_VALUE_HEADS, QUERY_HEADS // KEY_VALUE_HEADS, HEAD_DIMENSION
    )
    latest_keys = incoming_key_value[:, : KEY_VALUE_HEADS * HEAD_DIMENSION].reshape(
        DEVICE_REQUESTS, KEY_VALUE_HEADS, HEAD_DIMENSION
    )
    new_score = (
        jnp.einsum("rgjd,rgd->rgj", query_rows, latest_keys, preferred_element_type=jnp.float32)
        * scale
    )
    incoming_values = (
        incoming_key_value[:, KEY_VALUE_HEADS * HEAD_DIMENSION :]
        .reshape(DEVICE_REQUESTS, KEY_VALUE_HEADS, 1, HEAD_DIMENSION)
        .astype(jnp.float32)
    )
    maxima, totals, weighted = attend_migrate(
        query_rows, key_value_pool, block_owner, block_tokens, scale
    )
    attn_out = (
        finish(maxima, totals, weighted, new_score, incoming_values)
        .reshape(DEVICE_REQUESTS, QUERY_HEADS * HEAD_DIMENSION)
        .astype(jnp.bfloat16)
    )
    return (moe_out, attn_out)


def solution(mesh):
    placed = (
        P(("replica", "expert"), None),
        P(("replica", "expert"), None),
        P(("replica", "expert"), None),
        P(),
        P(None, ("replica", "expert")),
        P(("replica", "expert"), None),
        P(("replica", "expert"), None),
        P(("replica", "expert"), None),
        P(("replica", "expert"), None, None),
        P(("replica", "expert")),
        P(("replica", "expert")),
    )
    return jax.shard_map(
        shards,
        mesh=mesh,
        in_specs=placed,
        out_specs=(P(("replica", "expert"), None), P(("replica", "expert"), None)),
        check_vma=False,
    )
```

```python
import functools
import math

import jax
import jax.numpy as jnp
from jax import lax
from jax.experimental import pallas as pl
from jax.experimental.pallas import tpu as pltpu
from jax.sharding import PartitionSpec as P

QUART = 4
QUERY_HEADS = 64
KEY_VALUE_HEADS = 4
HEAD_DIMENSION = 128
DEVICE_REQUESTS = 2
DEVICE_BLOCKS = 16
BLOCK_SLOTS = 64
MIG = 2


HIGHEST = lax.Precision.HIGHEST


def partial_state(query_rows, rows, mask, scale):
    heads_kv = query_rows.shape[1]
    head_size = query_rows.shape[3]
    maxima = []
    totals = []
    weighted = []
    for head in range(heads_kv):
        cached_key_rows = rows[:, head * head_size : (head + 1) * head_size]
        cached_value_rows = rows[
            :, (heads_kv + head) * head_size : (heads_kv + head + 1) * head_size
        ].astype(jnp.float32)
        scores = (
            jnp.einsum(
                "rjd,nd->rjn",
                query_rows[:, head],
                cached_key_rows,
                preferred_element_type=jnp.float32,
            )
            * scale
        )
        keep = mask[:, None, :]
        largest = jnp.max(jnp.where(keep, scores, -1e30), axis=2)
        weights = jnp.where(keep, jnp.exp(scores - largest[:, :, None]), 0.0)
        maxima.append(largest)
        totals.append(jnp.sum(weights, axis=2))
        weighted.append(jnp.einsum("rjn,nd->rjd", weights, cached_value_rows, precision=HIGHEST))
    return (jnp.stack(maxima, 1), jnp.stack(totals, 1), jnp.stack(weighted, 1))


def finish(maxima, totals, weighted, new_score, incoming_values):
    best = jnp.maximum(jnp.max(maxima, axis=0), new_score)
    own_weight = jnp.exp(new_score - best)
    factor = jnp.exp(maxima - best[None])
    denom = own_weight + jnp.sum(factor * totals, axis=0)
    mixed = own_weight[..., None] * incoming_values + jnp.sum(factor[..., None] * weighted, axis=0)
    return mixed / denom[..., None]


def attend_migrate(query_rows, key_value_pool, block_owner, block_tokens, scale):
    replicas = lax.axis_size("replica")
    mine = lax.axis_index("replica")
    kv_width = key_value_pool.shape[2]
    target = block_owner // DEVICE_REQUESTS
    request = block_owner % DEVICE_REQUESTS
    leaving = target != mine
    to_replica = (
        (target[:, None] == jnp.arange(replicas, dtype=jnp.int32)[None, :]) & leaving[:, None]
    ).astype(jnp.int32)
    before = jnp.cumsum(to_replica, axis=0) - to_replica
    place = target * MIG + jnp.sum(before * to_replica, axis=1)
    select = (place[None, :] == jnp.arange(replicas * MIG, dtype=jnp.int32)[:, None]) & leaving[
        None, :
    ]
    chosen = select.astype(jnp.int32)
    send_blocks = jnp.dot(
        select.astype(jnp.bfloat16),
        key_value_pool.reshape(DEVICE_BLOCKS, BLOCK_SLOTS * kv_width),
        preferred_element_type=jnp.float32,
    ).astype(jnp.bfloat16)
    send_request = jnp.sum(chosen * request[None, :], axis=1)
    send_count = jnp.sum(chosen * block_tokens[None, :], axis=1)
    got_blocks, got_request, got_count = (
        lax.all_to_all(
            send_blocks.reshape(replicas, MIG, BLOCK_SLOTS * kv_width),
            "replica",
            split_axis=0,
            concat_axis=0,
            tiled=True,
        ),
        lax.all_to_all(
            send_request.reshape(replicas, MIG), "replica", split_axis=0, concat_axis=0, tiled=True
        ),
        lax.all_to_all(
            send_count.reshape(replicas, MIG), "replica", split_axis=0, concat_axis=0, tiled=True
        ),
    )
    positions = jnp.arange(BLOCK_SLOTS, dtype=jnp.int32)
    requests = jnp.arange(DEVICE_REQUESTS, dtype=jnp.int32)
    local_valid = (positions[None, :] < block_tokens[:, None]).reshape(-1)
    local_owner = jnp.repeat(block_owner, BLOCK_SLOTS)
    local_mask = (local_owner[None, :] == mine * DEVICE_REQUESTS + requests[:, None]) & local_valid[
        None, :
    ]
    local_state = partial_state(
        query_rows, key_value_pool.reshape(DEVICE_BLOCKS * BLOCK_SLOTS, kv_width), local_mask, scale
    )
    got_valid = (positions[None, :] < got_count.reshape(-1)[:, None]).reshape(-1)
    got_owner = jnp.repeat(got_request.reshape(-1), BLOCK_SLOTS)
    got_mask = (got_owner[None, :] == requests[:, None]) & got_valid[None, :]
    got_state = partial_state(query_rows, got_blocks.reshape(-1, kv_width), got_mask, scale)
    maxima = jnp.stack([local_state[0], got_state[0]], axis=0)
    totals = jnp.stack([local_state[1], got_state[1]], axis=0)
    weighted = jnp.stack([local_state[2], got_state[2]], axis=0)
    return (maxima, totals, weighted)


def expert_local(rows, w_gate_up, w_down):
    quarter = w_down.shape[0]
    halves = jnp.dot(rows, w_gate_up, preferred_element_type=jnp.float32)
    activation = (jax.nn.silu(halves[:, :quarter]) * halves[:, quarter:]).astype(jnp.bfloat16)
    return jnp.dot(activation, w_down, preferred_element_type=jnp.float32).astype(jnp.bfloat16)


def mixture(moe_input, expert_ids, route_weight, expert_slot, w_gate_up, w_down):
    token_rows = moe_input.shape[0]
    width = moe_input.shape[1]
    top_k = expert_ids.shape[1]
    experts = expert_slot.shape[0]
    replicas = lax.axis_size("replica")
    columns = lax.axis_size("expert")
    capacity = min(token_rows, max(2, 2 * token_rows * top_k // experts))
    flat_ids = expert_ids.reshape(-1)
    onehot = (flat_ids[:, None] == jnp.arange(experts, dtype=jnp.int32)[None, :]).astype(jnp.int32)
    before = jnp.cumsum(onehot, axis=0) - onehot
    position = jnp.sum(before * onehot, axis=1)
    slot_of = jnp.sum(onehot * expert_slot[None, :], axis=1)
    target = slot_of * capacity + position
    assign = (target[:, None] == jnp.arange(experts * capacity, dtype=jnp.int32)[None, :]).reshape(
        token_rows, top_k, experts * capacity
    )
    dispatch_map = jnp.sum(assign.astype(jnp.int32), axis=1).astype(jnp.bfloat16)
    send_rows = jnp.einsum(
        "tc,td->cd", dispatch_map, moe_input, preferred_element_type=jnp.float32
    ).astype(jnp.bfloat16)
    send = jnp.broadcast_to(
        send_rows.reshape(experts, 1, capacity, width), (experts, QUART, capacity, width)
    )
    send = send.reshape(replicas, columns, capacity, width)
    received = lax.all_to_all(
        lax.all_to_all(send, "replica", split_axis=0, concat_axis=0, tiled=True),
        "expert",
        split_axis=1,
        concat_axis=1,
        tiled=True,
    )
    quarter_part = expert_local(received.reshape(-1, width), w_gate_up, w_down)
    returned = lax.all_to_all(
        lax.all_to_all(
            quarter_part.reshape(send.shape), "replica", split_axis=0, concat_axis=0, tiled=True
        ),
        "expert",
        split_axis=1,
        concat_axis=1,
        tiled=True,
    )
    expert_out = jnp.sum(
        returned.reshape(experts, QUART, capacity, width).astype(jnp.float32), axis=1
    ).reshape(experts * capacity, width)
    mixing = jnp.sum(assign.astype(jnp.float32) * route_weight[:, :, None], axis=1)
    return jnp.dot(
        mixing, expert_out, precision=HIGHEST, preferred_element_type=jnp.float32
    ).astype(jnp.bfloat16)


CORES = 2
PAD = 128
VMEM_LIMIT = 60 * 1024 * 1024
MESH = pl.DeviceIdType.MESH


def fits_fused(expert_ids, expert_slot):
    experts = expert_slot.shape[0]
    devices = lax.axis_size("replica") * lax.axis_size("expert")
    return (
        expert_ids.shape[1] == experts
        and 3 * experts <= PAD
        and devices == experts * QUART
        and lax.axis_size("expert") % CORES == 0
        and lax.axis_size("expert") >= 2 * CORES
        and QUART % CORES == 0
    )


def fused_kernel(
    replicas,
    depth,
    experts,
    slot_ref,
    owner_ref,
    tokens_ref,
    ids_hbm,
    rw_hbm,
    q_hbm,
    new_hbm,
    x_hbm,
    wgu_hbm,
    wd_hbm,
    kv_hbm,
    moe_ref,
    attn_ref,
    ids_ref,
    rw_ref,
    q_ref,
    new_ref,
    xb,
    wgu,
    wd,
    kv,
    pf,
    xs,
    xr,
    zf,
    zs,
    zr,
    qb,
    accf,
    accb,
    mlb,
    ar,
    mr,
    load_sem,
    z_send,
    z_recv,
    r_send,
    r_recv,
    w_send,
    w_recv,
    q_send,
    q_recv,
    xs_send,
    xs_recv,
    zs_send,
    zs_recv,
    a_send,
    a_recv,
    m_send,
    m_recv,
):
    r = lax.axis_index("replica")
    e = lax.axis_index("expert")
    z = e // CORES
    c = e % CORES
    sib = 1 - c
    rows, width = x_hbm.shape
    quarter = wd_hbm.shape[0]
    heads = KEY_VALUE_HEADS
    hd = HEAD_DIMENSION
    group = QUERY_HEADS // KEY_VALUE_HEADS
    per = DEVICE_REQUESTS * group
    scale = 1.0 / math.sqrt(HEAD_DIMENSION)
    sent = []

    def rdev(k):
        return ((r + k) % replicas, e)

    def zdev(k):
        return (r, ((z + k) % depth) * CORES + c)

    cdev = (r, z * CORES + sib)

    def remote(src, dst, ssem, rsem, dev):
        return pltpu.make_async_remote_copy(
            src_ref=src, dst_ref=dst, send_sem=ssem, recv_sem=rsem, device_id=dev, device_id_type=MESH
        )

    def push(*args):
        d = remote(*args)
        d.start()
        sent.append(d)

    loads = [
        pltpu.make_async_copy(wgu_hbm, wgu.at[:, pl.ds(0, 2 * quarter)], load_sem.at[0]),
        pltpu.make_async_copy(wd_hbm, wd.at[pl.ds(0, quarter)], load_sem.at[1]),
        pltpu.make_async_copy(kv_hbm, kv, load_sem.at[2]),
        pltpu.make_async_copy(x_hbm, xb.at[z, r, :, pl.ds(0, width)], load_sem.at[3]),
        pltpu.make_async_copy(ids_hbm, ids_ref, load_sem.at[4]),
        pltpu.make_async_copy(rw_hbm, rw_ref, load_sem.at[5]),
        pltpu.make_async_copy(q_hbm, q_ref, load_sem.at[6]),
        pltpu.make_async_copy(new_hbm, new_ref, load_sem.at[7]),
    ]
    for n in (3, 4, 5, 6, 7, 2, 0, 1):
        loads[n].start()

    barrier = pltpu.get_barrier_semaphore()
    for k in range(1, replicas):
        pl.semaphore_signal(barrier, inc=1, device_id=rdev(k), device_id_type=MESH)
    for k in range(1, depth):
        pl.semaphore_signal(barrier, inc=1, device_id=zdev(k), device_id_type=MESH)
    pl.semaphore_signal(barrier, inc=1, device_id=cdev, device_id_type=MESH)

    loads[4].wait()
    loads[5].wait()
    line = lax.broadcasted_iota(jnp.int32, (PAD, rows), 0)
    mix = jnp.zeros((PAD, rows), jnp.float32)
    for k in range(experts):
        chosen = ids_ref[k : k + 1, :]
        slot = jnp.zeros((1, rows), jnp.int32)
        for n in range(experts):
            slot = jnp.where(chosen == n, slot_ref[n], slot)
        mix = mix + jnp.where(line % experts == slot, rw_ref[k : k + 1, :], 0.0)
    high = mix.astype(jnp.bfloat16).astype(jnp.float32)
    rest = mix - high
    mid = rest.astype(jnp.bfloat16).astype(jnp.float32)
    low = rest - mid
    terms = jnp.where(line < experts, high, jnp.where(line < 2 * experts, mid, low))
    unit = (
        lax.broadcasted_iota(jnp.int32, (rows, rows), 0)
        == lax.broadcasted_iota(jnp.int32, (rows, rows), 1)
    ).astype(jnp.bfloat16)
    xb[z, r, :, width:] = lax.dot_general(
        unit,
        terms.astype(jnp.bfloat16),
        (((1,), (1,)), ((), ())),
        preferred_element_type=jnp.float32,
    ).astype(jnp.bfloat16)
    loads[6].wait()
    asked = q_ref[...].astype(jnp.float32)
    for g in range(heads):
        pieces = [asked[:, (g * group + j) * hd : (g * group + j + 1) * hd] for j in range(group)]
        qb[r, g * per : (g + 1) * per, :] = jnp.concatenate(pieces, axis=0).astype(jnp.bfloat16)
    loads[3].wait()

    pl.semaphore_wait(barrier, replicas - 1 + depth - 1 + 1)

    def xy_out(zo):
        piece = xb.at[(z + depth - zo) % depth, r]
        for k in range(1, replicas):
            push(piece, piece, r_send.at[zo, k], r_recv.at[zo, k], rdev(k))

    def weights_in():
        both = [
            (
                wgu_hbm.at[pl.ds(n * (width // 4), width // 4)],
                wgu.at[pl.ds(n * (width // 4), width // 4), pl.ds(2 * quarter, 2 * quarter)],
            )
            for n in range(4)
        ] + [(wd_hbm, wd.at[pl.ds(quarter, quarter)])]
        return [
            remote(src, dst, w_send.at[n], w_recv.at[n], cdev) for n, (src, dst) in enumerate(both)
        ]

    own = xb.at[z, r]
    for k in range(1, depth):
        push(own, own, z_send.at[k], z_recv.at[k], zdev(k))
    for k in range(1, replicas):
        push(qb.at[r], qb.at[r], q_send.at[k], q_recv.at[k], rdev(k))
    xy_out(0)
    for d in weights_in():
        d.start()
        sent.append(d)

    def onward(zo):
        got = xb.at[(z + depth - zo) % depth, r]
        remote(got, got, z_send.at[zo], z_recv.at[zo], cdev).wait_recv()
        xy_out(zo)

    if depth > 1:
        onward(1)

    for k in range(1, replicas):
        got = qb.at[(r + replicas - k) % replicas]
        remote(got, got, q_send.at[k], q_recv.at[k], cdev).wait_recv()
    loads[2].wait()
    blocks, slots = owner_ref.shape[0], kv.shape[0] // owner_ref.shape[0]
    keys = kv.shape[0]
    place = lax.broadcasted_iota(jnp.int32, (1, keys), 1)
    holder = jnp.full((1, keys), -1, jnp.int32)
    for b in range(blocks):
        inside = (place >= b * slots) & (place < b * slots + tokens_ref[b])
        holder = jnp.where(inside, owner_ref[b], holder)
    total = replicas * per
    row = lax.broadcasted_iota(jnp.int32, (total, 1), 0)
    asker = row // per * DEVICE_REQUESTS + row % DEVICE_REQUESTS
    keep = holder == asker
    mlane = lax.broadcasted_iota(jnp.int32, (total, PAD), 1)

    def head(g, ml):
        col = slice(g * hd, (g + 1) * hd)
        vcol = slice((heads + g) * hd, (heads + g + 1) * hd)
        qg = qb[:, g * per : (g + 1) * per, :].reshape(total, hd)
        scores = (
            lax.dot_general(
                qg, kv[:, col], (((1,), (1,)), ((), ())), preferred_element_type=jnp.float32
            )
            * scale
        )
        top = jnp.max(jnp.where(keep, scores, -1e30), axis=1, keepdims=True)
        weights = jnp.where(keep, jnp.exp(scores - top), 0.0)
        mass = jnp.sum(weights, axis=1, keepdims=True)
        acc = jnp.dot(
            weights.astype(jnp.bfloat16), kv[:, vcol], preferred_element_type=jnp.float32
        ).reshape(replicas, per, hd)
        accf[:, g] = acc
        accb[:, g] = acc.astype(jnp.bfloat16)
        return jnp.where(mlane == g, top, jnp.where(mlane == heads + g, mass, ml))

    def hand_back(ml):
        mlb[...] = ml.reshape(replicas, per, PAD)
        for k in range(1, replicas):
            to = (r + k) % replicas
            push(accb.at[to], ar.at[k], a_send.at[k], a_recv.at[k], rdev(k))
            push(mlb.at[to], mr.at[k], m_send.at[k], m_recv.at[k], rdev(k))

    def finish_attention():
        loads[7].wait()
        for k in range(1, replicas):
            remote(ar.at[k], ar.at[k], a_send.at[k], a_recv.at[k], cdev).wait_recv()
            remote(mr.at[k], mr.at[k], m_send.at[k], m_recv.at[k], cdev).wait_recv()
        plane = lax.broadcasted_iota(jnp.int32, (per, PAD), 1)
        mls = [mlb[r]] + [mr[k] for k in range(1, replicas)]

        def pick(values, n):
            return jnp.sum(jnp.where(plane == n, values, 0.0), axis=1, keepdims=True)

        turn = lax.broadcasted_iota(jnp.int32, (per, hd), 0) % DEVICE_REQUESTS

        def spread(n):
            values = new_ref[:, n * hd : (n + 1) * hd].astype(jnp.float32)
            wide = values[:1]
            for i in range(1, DEVICE_REQUESTS):
                wide = jnp.where(turn == i, values[i : i + 1], wide)
            return jnp.broadcast_to(wide, (per, hd))

        for g in range(heads):
            query = qb[r, g * per : (g + 1) * per, :].astype(jnp.float32)
            fresh = jnp.sum(query * spread(g), axis=1, keepdims=True) * scale
            tops = [pick(v, g) for v in mls]
            best = fresh
            for t in tops:
                best = jnp.maximum(best, t)
            weight = jnp.exp(fresh - best)
            denom = weight
            mixed = weight * spread(heads + g)
            for k in range(replicas):
                factor = jnp.exp(tops[k] - best)
                part = accf[r, g] if k == 0 else ar[k, g].astype(jnp.float32)
                denom = denom + factor * pick(mls[k], heads + g)
                mixed = mixed + factor * part
            mixed = mixed / denom
            for j in range(group):
                cols = slice((g * group + j) * hd, (g * group + j + 1) * hd)
                attn_ref[:, cols] = mixed[
                    j * DEVICE_REQUESTS : (j + 1) * DEVICE_REQUESTS, :
                ].astype(attn_ref.dtype)

    my_slot = (r * (depth * CORES) + e) // QUART
    chunk = replicas * rows

    def gather(zo):
        for k in range(1, replicas):
            got = xb.at[(z + depth - zo) % depth, (r + replicas - k) % replicas]
            remote(got, got, r_send.at[zo, k], r_recv.at[zo, k], cdev).wait_recv()

    def expert(group_of):
        tall = len(group_of) * chunk
        block = jnp.concatenate(
            [xb[(z + depth - zo) % depth].reshape(chunk, width + PAD) for zo in group_of], axis=0
        )
        slane = lax.broadcasted_iota(jnp.int32, (tall, PAD), 1)
        mine = (slane % experts == my_slot) & (slane < 3 * experts)
        gain = jnp.sum(
            jnp.where(mine, block[:, width:].astype(jnp.float32), 0.0), axis=1, keepdims=True
        )
        halves = jnp.dot(block[:, :width], wgu[...], preferred_element_type=jnp.float32)
        acts = []
        for n in range(CORES):
            gate = halves[:, 2 * n * quarter : (2 * n + 1) * quarter]
            up = halves[:, (2 * n + 1) * quarter : (2 * n + 2) * quarter]
            acts.append((gate / (1.0 + jnp.exp(-gate)) * up).astype(jnp.bfloat16))
        step = width // 4
        for m in range(4):
            cols = slice(m * step, (m + 1) * step)
            part = jnp.dot(acts[0], wd[:quarter, cols], preferred_element_type=jnp.float32)
            part = part + jnp.dot(acts[1], wd[quarter:, cols], preferred_element_type=jnp.float32)
            part = part * gain
            for i, zo in enumerate(group_of):
                own_part = part[i * chunk : (i + 1) * chunk]
                pf[zo, :, cols] = own_part
                xs[zo, :, :, cols] = own_part.astype(jnp.bfloat16).reshape(replicas, rows, step)
        for zo in group_of:
            for k in range(1, replicas):
                to = (r + k) % replicas
                push(xs.at[zo, to], xr.at[zo, k], xs_send.at[zo, k], xs_recv.at[zo, k], rdev(k))

    def along(zo):
        total = pf[zo, pl.ds(pl.multiple_of(r * rows, rows), rows), :]
        for k in range(1, replicas):
            remote(
                xr.at[zo, k], xr.at[zo, k], xs_send.at[zo, k], xs_recv.at[zo, k], cdev
            ).wait_recv()
            total = total + xr[zo, k].astype(jnp.float32)
        if zo == 0:
            zf[...] = total
        else:
            zs[zo] = total.astype(jnp.bfloat16)
            push(zs.at[zo], zr.at[zo], zs_send.at[zo], zs_recv.at[zo], zdev(depth - zo))

    ml = head(0, jnp.zeros((total, PAD), jnp.float32))
    if depth > 2:
        onward(2)
    gather(0)
    done = 1
    if heads > 1:
        ml = head(1, ml)
        done = 2
    for zo in range(3, depth):
        onward(zo)
    for g in range(done, heads):
        ml = head(g, ml)
    hand_back(ml)
    loads[0].wait()
    loads[1].wait()
    for d in weights_in():
        d.wait_recv()
    gather(1)
    expert((0, 1))
    for zo in range(2, depth):
        gather(zo)
        expert((zo,))
        along(zo - 2)
    for zo in range(max(depth - 2, 0), depth):
        if zo == depth - 1:
            finish_attention()
        along(zo)
    result = zf[...]
    for zo in range(1, depth):
        remote(zr.at[zo], zr.at[zo], zs_send.at[zo], zs_recv.at[zo], cdev).wait_recv()
        result = result + zr[zo].astype(jnp.float32)
    moe_ref[...] = result.astype(moe_ref.dtype)
    for d in sent:
        d.wait_send()


def place_results(moe_ref, attn_ref, moe_out, attn_out, moe_v, attn_v, sem):
    ins = [
        pltpu.make_async_copy(moe_ref, moe_v, sem.at[0]),
        pltpu.make_async_copy(attn_ref, attn_v, sem.at[1]),
    ]
    outs = [
        pltpu.make_async_copy(moe_v, moe_out, sem.at[2]),
        pltpu.make_async_copy(attn_v, attn_out, sem.at[3]),
    ]
    for d in ins:
        d.start()
    for i, o in zip(ins, outs):
        i.wait()
        o.start()
    for o in outs:
        o.wait()


def fused(
    moe_input,
    expert_ids,
    route_weight,
    expert_slot,
    w_gate_up,
    w_down,
    queries,
    incoming_key_value,
    key_value_pool,
    block_owner,
    block_tokens,
):
    replicas = lax.axis_size("replica")
    depth = lax.axis_size("expert") // CORES
    experts = expert_slot.shape[0]
    rows, width = moe_input.shape
    group = QUERY_HEADS // KEY_VALUE_HEADS
    per = DEVICE_REQUESTS * group
    hd = HEAD_DIMENSION
    keys = key_value_pool.shape[0] * key_value_pool.shape[1]
    smem = pl.BlockSpec(memory_space=pltpu.SMEM)
    vmem = pl.BlockSpec(memory_space=pltpu.VMEM)
    hbm = pl.BlockSpec(memory_space=pl.ANY)
    bf, f32 = jnp.bfloat16, jnp.float32
    dma = pltpu.SemaphoreType.DMA
    moe_out, attn = pl.pallas_call(
        functools.partial(fused_kernel, replicas, depth, experts),
        out_shape=(
            jax.ShapeDtypeStruct((rows, width), bf),
            jax.ShapeDtypeStruct(queries.shape, bf),
        ),
        in_specs=[smem] * 3 + [hbm] * 8,
        out_specs=(vmem, vmem),
        scratch_shapes=[
            pltpu.VMEM(expert_ids.shape[::-1], expert_ids.dtype),
            pltpu.VMEM(route_weight.shape[::-1], f32),
            pltpu.VMEM(queries.shape, bf),
            pltpu.VMEM(incoming_key_value.shape, bf),
            pltpu.VMEM((depth, replicas, rows, width + PAD), bf),
            pltpu.VMEM((width, CORES * w_gate_up.shape[1]), bf),
            pltpu.VMEM((CORES * w_down.shape[0], width), bf),
            pltpu.VMEM((keys, key_value_pool.shape[2]), bf),
            pltpu.VMEM((depth, replicas * rows, width), f32),
            pltpu.VMEM((depth, replicas, rows, width), bf),
            pltpu.VMEM((depth, replicas, rows, width), bf),
            pltpu.VMEM((rows, width), f32),
            pltpu.VMEM((depth, rows, width), bf),
            pltpu.VMEM((depth, rows, width), bf),
            pltpu.VMEM((replicas, KEY_VALUE_HEADS * per, hd), bf),
            pltpu.VMEM((replicas, KEY_VALUE_HEADS, per, hd), f32),
            pltpu.VMEM((replicas, KEY_VALUE_HEADS, per, hd), bf),
            pltpu.VMEM((replicas, per, PAD), f32),
            pltpu.VMEM((replicas, KEY_VALUE_HEADS, per, hd), bf),
            pltpu.VMEM((replicas, per, PAD), f32),
            dma((8,)),
            dma((depth,)),
            dma((depth,)),
            dma((depth, replicas)),
            dma((depth, replicas)),
            dma((5,)),
            dma((5,)),
            dma((replicas,)),
            dma((replicas,)),
            dma((depth, replicas)),
            dma((depth, replicas)),
            dma((depth,)),
            dma((depth,)),
            dma((replicas,)),
            dma((replicas,)),
            dma((replicas,)),
            dma((replicas,)),
        ],
        compiler_params=pltpu.CompilerParams(
            collective_id=0, has_side_effects=True, vmem_limit_bytes=VMEM_LIMIT
        ),
    )(
        expert_slot,
        block_owner,
        block_tokens,
        expert_ids.T,
        route_weight.T,
        queries,
        incoming_key_value,
        moe_input,
        w_gate_up,
        w_down,
        key_value_pool.reshape(keys, key_value_pool.shape[2]),
    )
    return pl.pallas_call(
        place_results,
        out_shape=(
            jax.ShapeDtypeStruct(moe_out.shape, bf),
            jax.ShapeDtypeStruct(attn.shape, bf),
        ),
        in_specs=[hbm] * 2,
        out_specs=(hbm, hbm),
        scratch_shapes=[
            pltpu.VMEM(moe_out.shape, bf),
            pltpu.VMEM(attn.shape, bf),
            dma((4,)),
        ],
        compiler_params=pltpu.CompilerParams(vmem_limit_bytes=VMEM_LIMIT),
    )(moe_out, attn)


def shards(
    moe_input,
    expert_ids,
    route_weight,
    expert_slot,
    w_gate_up,
    w_down,
    queries,
    incoming_key_value,
    key_value_pool,
    block_owner,
    block_tokens,
):
    if fits_fused(expert_ids, expert_slot):
        return fused(
            moe_input,
            expert_ids,
            route_weight,
            expert_slot,
            w_gate_up,
            w_down,
            queries,
            incoming_key_value,
            key_value_pool,
            block_owner,
            block_tokens,
        )
    moe_out = mixture(moe_input, expert_ids, route_weight, expert_slot, w_gate_up, w_down)
    scale = 1.0 / math.sqrt(HEAD_DIMENSION)
    query_rows = queries.reshape(
        DEVICE_REQUESTS, KEY_VALUE_HEADS, QUERY_HEADS // KEY_VALUE_HEADS, HEAD_DIMENSION
    )
    latest_keys = incoming_key_value[:, : KEY_VALUE_HEADS * HEAD_DIMENSION].reshape(
        DEVICE_REQUESTS, KEY_VALUE_HEADS, HEAD_DIMENSION
    )
    new_score = (
        jnp.einsum("rgjd,rgd->rgj", query_rows, latest_keys, preferred_element_type=jnp.float32)
        * scale
    )
    incoming_values = (
        incoming_key_value[:, KEY_VALUE_HEADS * HEAD_DIMENSION :]
        .reshape(DEVICE_REQUESTS, KEY_VALUE_HEADS, 1, HEAD_DIMENSION)
        .astype(jnp.float32)
    )
    maxima, totals, weighted = attend_migrate(
        query_rows, key_value_pool, block_owner, block_tokens, scale
    )
    attn_out = (
        finish(maxima, totals, weighted, new_score, incoming_values)
        .reshape(DEVICE_REQUESTS, QUERY_HEADS * HEAD_DIMENSION)
        .astype(jnp.bfloat16)
    )
    return (moe_out, attn_out)


def solution(mesh):
    placed = (
        P(("replica", "expert"), None),
        P(("replica", "expert"), None),
        P(("replica", "expert"), None),
        P(),
        P(None, ("replica", "expert")),
        P(("replica", "expert"), None),
        P(("replica", "expert"), None),
        P(("replica", "expert"), None),
        P(("replica", "expert"), None, None),
        P(("replica", "expert")),
        P(("replica", "expert")),
    )
    return jax.shard_map(
        shards,
        mesh=mesh,
        in_specs=placed,
        out_specs=(P(("replica", "expert"), None), P(("replica", "expert"), None)),
        check_vma=False,
    )
```

```python
import functools
import math

import jax
import jax.numpy as jnp
from jax import lax
from jax.experimental import pallas as pl
from jax.experimental.pallas import tpu as pltpu
from jax.sharding import PartitionSpec as P

QUART = 4
QUERY_HEADS = 64
KEY_VALUE_HEADS = 4
HEAD_DIMENSION = 128
DEVICE_REQUESTS = 2
DEVICE_BLOCKS = 16
BLOCK_SLOTS = 64
MIG = 2


HIGHEST = lax.Precision.HIGHEST


def partial_state(query_rows, rows, mask, scale):
    heads_kv = query_rows.shape[1]
    head_size = query_rows.shape[3]
    maxima = []
    totals = []
    weighted = []
    for head in range(heads_kv):
        cached_key_rows = rows[:, head * head_size : (head + 1) * head_size]
        cached_value_rows = rows[
            :, (heads_kv + head) * head_size : (heads_kv + head + 1) * head_size
        ].astype(jnp.float32)
        scores = (
            jnp.einsum(
                "rjd,nd->rjn",
                query_rows[:, head],
                cached_key_rows,
                preferred_element_type=jnp.float32,
            )
            * scale
        )
        keep = mask[:, None, :]
        largest = jnp.max(jnp.where(keep, scores, -1e30), axis=2)
        weights = jnp.where(keep, jnp.exp(scores - largest[:, :, None]), 0.0)
        maxima.append(largest)
        totals.append(jnp.sum(weights, axis=2))
        weighted.append(jnp.einsum("rjn,nd->rjd", weights, cached_value_rows, precision=HIGHEST))
    return (jnp.stack(maxima, 1), jnp.stack(totals, 1), jnp.stack(weighted, 1))


def finish(maxima, totals, weighted, new_score, incoming_values):
    best = jnp.maximum(jnp.max(maxima, axis=0), new_score)
    own_weight = jnp.exp(new_score - best)
    factor = jnp.exp(maxima - best[None])
    denom = own_weight + jnp.sum(factor * totals, axis=0)
    mixed = own_weight[..., None] * incoming_values + jnp.sum(factor[..., None] * weighted, axis=0)
    return mixed / denom[..., None]


def attend_migrate(query_rows, key_value_pool, block_owner, block_tokens, scale):
    replicas = lax.axis_size("replica")
    mine = lax.axis_index("replica")
    kv_width = key_value_pool.shape[2]
    target = block_owner // DEVICE_REQUESTS
    request = block_owner % DEVICE_REQUESTS
    leaving = target != mine
    to_replica = (
        (target[:, None] == jnp.arange(replicas, dtype=jnp.int32)[None, :]) & leaving[:, None]
    ).astype(jnp.int32)
    before = jnp.cumsum(to_replica, axis=0) - to_replica
    place = target * MIG + jnp.sum(before * to_replica, axis=1)
    select = (place[None, :] == jnp.arange(replicas * MIG, dtype=jnp.int32)[:, None]) & leaving[
        None, :
    ]
    chosen = select.astype(jnp.int32)
    send_blocks = jnp.dot(
        select.astype(jnp.bfloat16),
        key_value_pool.reshape(DEVICE_BLOCKS, BLOCK_SLOTS * kv_width),
        preferred_element_type=jnp.float32,
    ).astype(jnp.bfloat16)
    send_request = jnp.sum(chosen * request[None, :], axis=1)
    send_count = jnp.sum(chosen * block_tokens[None, :], axis=1)
    got_blocks, got_request, got_count = (
        lax.all_to_all(
            send_blocks.reshape(replicas, MIG, BLOCK_SLOTS * kv_width),
            "replica",
            split_axis=0,
            concat_axis=0,
            tiled=True,
        ),
        lax.all_to_all(
            send_request.reshape(replicas, MIG), "replica", split_axis=0, concat_axis=0, tiled=True
        ),
        lax.all_to_all(
            send_count.reshape(replicas, MIG), "replica", split_axis=0, concat_axis=0, tiled=True
        ),
    )
    positions = jnp.arange(BLOCK_SLOTS, dtype=jnp.int32)
    requests = jnp.arange(DEVICE_REQUESTS, dtype=jnp.int32)
    local_valid = (positions[None, :] < block_tokens[:, None]).reshape(-1)
    local_owner = jnp.repeat(block_owner, BLOCK_SLOTS)
    local_mask = (local_owner[None, :] == mine * DEVICE_REQUESTS + requests[:, None]) & local_valid[
        None, :
    ]
    local_state = partial_state(
        query_rows, key_value_pool.reshape(DEVICE_BLOCKS * BLOCK_SLOTS, kv_width), local_mask, scale
    )
    got_valid = (positions[None, :] < got_count.reshape(-1)[:, None]).reshape(-1)
    got_owner = jnp.repeat(got_request.reshape(-1), BLOCK_SLOTS)
    got_mask = (got_owner[None, :] == requests[:, None]) & got_valid[None, :]
    got_state = partial_state(query_rows, got_blocks.reshape(-1, kv_width), got_mask, scale)
    maxima = jnp.stack([local_state[0], got_state[0]], axis=0)
    totals = jnp.stack([local_state[1], got_state[1]], axis=0)
    weighted = jnp.stack([local_state[2], got_state[2]], axis=0)
    return (maxima, totals, weighted)


def expert_local(rows, w_gate_up, w_down):
    quarter = w_down.shape[0]
    halves = jnp.dot(rows, w_gate_up, preferred_element_type=jnp.float32)
    activation = (jax.nn.silu(halves[:, :quarter]) * halves[:, quarter:]).astype(jnp.bfloat16)
    return jnp.dot(activation, w_down, preferred_element_type=jnp.float32).astype(jnp.bfloat16)


def mixture(moe_input, expert_ids, route_weight, expert_slot, w_gate_up, w_down):
    token_rows = moe_input.shape[0]
    width = moe_input.shape[1]
    top_k = expert_ids.shape[1]
    experts = expert_slot.shape[0]
    replicas = lax.axis_size("replica")
    columns = lax.axis_size("expert")
    capacity = min(token_rows, max(2, 2 * token_rows * top_k // experts))
    flat_ids = expert_ids.reshape(-1)
    onehot = (flat_ids[:, None] == jnp.arange(experts, dtype=jnp.int32)[None, :]).astype(jnp.int32)
    before = jnp.cumsum(onehot, axis=0) - onehot
    position = jnp.sum(before * onehot, axis=1)
    slot_of = jnp.sum(onehot * expert_slot[None, :], axis=1)
    target = slot_of * capacity + position
    assign = (target[:, None] == jnp.arange(experts * capacity, dtype=jnp.int32)[None, :]).reshape(
        token_rows, top_k, experts * capacity
    )
    dispatch_map = jnp.sum(assign.astype(jnp.int32), axis=1).astype(jnp.bfloat16)
    send_rows = jnp.einsum(
        "tc,td->cd", dispatch_map, moe_input, preferred_element_type=jnp.float32
    ).astype(jnp.bfloat16)
    send = jnp.broadcast_to(
        send_rows.reshape(experts, 1, capacity, width), (experts, QUART, capacity, width)
    )
    send = send.reshape(replicas, columns, capacity, width)
    received = lax.all_to_all(
        lax.all_to_all(send, "replica", split_axis=0, concat_axis=0, tiled=True),
        "expert",
        split_axis=1,
        concat_axis=1,
        tiled=True,
    )
    quarter_part = expert_local(received.reshape(-1, width), w_gate_up, w_down)
    returned = lax.all_to_all(
        lax.all_to_all(
            quarter_part.reshape(send.shape), "replica", split_axis=0, concat_axis=0, tiled=True
        ),
        "expert",
        split_axis=1,
        concat_axis=1,
        tiled=True,
    )
    expert_out = jnp.sum(
        returned.reshape(experts, QUART, capacity, width).astype(jnp.float32), axis=1
    ).reshape(experts * capacity, width)
    mixing = jnp.sum(assign.astype(jnp.float32) * route_weight[:, :, None], axis=1)
    return jnp.dot(
        mixing, expert_out, precision=HIGHEST, preferred_element_type=jnp.float32
    ).astype(jnp.bfloat16)


CORES = 2
PAD = 128
VMEM_LIMIT = 60 * 1024 * 1024
MESH = pl.DeviceIdType.MESH


def fits_fused(expert_ids, expert_slot):
    experts = expert_slot.shape[0]
    devices = lax.axis_size("replica") * lax.axis_size("expert")
    return (
        expert_ids.shape[1] == experts
        and 3 * experts <= PAD
        and devices == experts * QUART
        and lax.axis_size("expert") % CORES == 0
        and lax.axis_size("expert") >= 2 * CORES
        and QUART % CORES == 0
    )


def fused_kernel(
    replicas,
    depth,
    experts,
    slot_ref,
    owner_ref,
    tokens_ref,
    ids_hbm,
    rw_hbm,
    q_hbm,
    new_hbm,
    x_hbm,
    wgu_hbm,
    wd_hbm,
    kv_hbm,
    moe_ref,
    attn_ref,
    ids_ref,
    rw_ref,
    q_ref,
    new_ref,
    xb,
    wgu,
    wd,
    kv,
    pf,
    xs,
    xr,
    zf,
    zs,
    zr,
    qb,
    accf,
    accb,
    mlb,
    ar,
    mr,
    load_sem,
    z_send,
    z_recv,
    r_send,
    r_recv,
    w_send,
    w_recv,
    q_send,
    q_recv,
    xs_send,
    xs_recv,
    zs_send,
    zs_recv,
    a_send,
    a_recv,
    m_send,
    m_recv,
):
    r = lax.axis_index("replica")
    e = lax.axis_index("expert")
    z = e // CORES
    c = e % CORES
    sib = 1 - c
    rows, width = x_hbm.shape
    quarter = wd_hbm.shape[0]
    heads = KEY_VALUE_HEADS
    hd = HEAD_DIMENSION
    group = QUERY_HEADS // KEY_VALUE_HEADS
    per = DEVICE_REQUESTS * group
    scale = 1.0 / math.sqrt(HEAD_DIMENSION)
    sent = []

    def rdev(k):
        return ((r + k) % replicas, e)

    def zdev(k):
        return (r, ((z + k) % depth) * CORES + c)

    cdev = (r, z * CORES + sib)

    def remote(src, dst, ssem, rsem, dev):
        return pltpu.make_async_remote_copy(
            src_ref=src, dst_ref=dst, send_sem=ssem, recv_sem=rsem, device_id=dev, device_id_type=MESH
        )

    def push(*args):
        d = remote(*args)
        d.start()
        sent.append(d)

    loads = [
        pltpu.make_async_copy(wgu_hbm, wgu.at[:, pl.ds(0, 2 * quarter)], load_sem.at[0]),
        pltpu.make_async_copy(wd_hbm, wd.at[pl.ds(0, quarter)], load_sem.at[1]),
        pltpu.make_async_copy(kv_hbm, kv, load_sem.at[2]),
        pltpu.make_async_copy(x_hbm, xb.at[z, r, :, pl.ds(0, width)], load_sem.at[3]),
        pltpu.make_async_copy(ids_hbm, ids_ref, load_sem.at[4]),
        pltpu.make_async_copy(rw_hbm, rw_ref, load_sem.at[5]),
        pltpu.make_async_copy(q_hbm, q_ref, load_sem.at[6]),
        pltpu.make_async_copy(new_hbm, new_ref, load_sem.at[7]),
    ]
    for n in (3, 4, 5, 6, 7, 2, 0, 1):
        loads[n].start()

    barrier = pltpu.get_barrier_semaphore()
    for k in range(1, replicas):
        pl.semaphore_signal(barrier, inc=1, device_id=rdev(k), device_id_type=MESH)
    for k in range(1, depth):
        pl.semaphore_signal(barrier, inc=1, device_id=zdev(k), device_id_type=MESH)
    pl.semaphore_signal(barrier, inc=1, device_id=cdev, device_id_type=MESH)

    loads[4].wait()
    loads[5].wait()
    line = lax.broadcasted_iota(jnp.int32, (PAD, rows), 0)
    mix = jnp.zeros((PAD, rows), jnp.float32)
    for k in range(experts):
        chosen = ids_ref[k : k + 1, :]
        slot = jnp.zeros((1, rows), jnp.int32)
        for n in range(experts):
            slot = jnp.where(chosen == n, slot_ref[n], slot)
        mix = mix + jnp.where(line % experts == slot, rw_ref[k : k + 1, :], 0.0)
    high = mix.astype(jnp.bfloat16).astype(jnp.float32)
    rest = mix - high
    mid = rest.astype(jnp.bfloat16).astype(jnp.float32)
    low = rest - mid
    terms = jnp.where(line < experts, high, jnp.where(line < 2 * experts, mid, low))
    unit = (
        lax.broadcasted_iota(jnp.int32, (rows, rows), 0)
        == lax.broadcasted_iota(jnp.int32, (rows, rows), 1)
    ).astype(jnp.bfloat16)
    xb[z, r, :, width:] = lax.dot_general(
        unit,
        terms.astype(jnp.bfloat16),
        (((1,), (1,)), ((), ())),
        preferred_element_type=jnp.float32,
    ).astype(jnp.bfloat16)
    loads[6].wait()
    asked = q_ref[...].astype(jnp.float32)
    for g in range(heads):
        pieces = [asked[:, (g * group + j) * hd : (g * group + j + 1) * hd] for j in range(group)]
        qb[r, g * per : (g + 1) * per, :] = jnp.concatenate(pieces, axis=0).astype(jnp.bfloat16)
    loads[3].wait()

    pl.semaphore_wait(barrier, replicas - 1 + depth - 1 + 1)

    def xy_out(zo):
        piece = xb.at[(z + depth - zo) % depth, r]
        for k in range(1, replicas):
            push(piece, piece, r_send.at[zo, k], r_recv.at[zo, k], rdev(k))

    def weights_in():
        both = [
            (
                wgu_hbm.at[pl.ds(n * (width // 4), width // 4)],
                wgu.at[pl.ds(n * (width // 4), width // 4), pl.ds(2 * quarter, 2 * quarter)],
            )
            for n in range(4)
        ] + [(wd_hbm, wd.at[pl.ds(quarter, quarter)])]
        return [
            remote(src, dst, w_send.at[n], w_recv.at[n], cdev) for n, (src, dst) in enumerate(both)
        ]

    own = xb.at[z, r]
    for k in range(1, depth):
        push(own, own, z_send.at[k], z_recv.at[k], zdev(k))
    for k in range(1, replicas):
        push(qb.at[r], qb.at[r], q_send.at[k], q_recv.at[k], rdev(k))
    xy_out(0)
    for d in weights_in():
        d.start()
        sent.append(d)

    def onward(zo):
        got = xb.at[(z + depth - zo) % depth, r]
        remote(got, got, z_send.at[zo], z_recv.at[zo], cdev).wait_recv()
        xy_out(zo)

    if depth > 1:
        onward(1)

    for k in range(1, replicas):
        got = qb.at[(r + replicas - k) % replicas]
        remote(got, got, q_send.at[k], q_recv.at[k], cdev).wait_recv()
    loads[2].wait()
    blocks, slots = owner_ref.shape[0], kv.shape[0] // owner_ref.shape[0]
    keys = kv.shape[0]
    place = lax.broadcasted_iota(jnp.int32, (1, keys), 1)
    holder = jnp.full((1, keys), -1, jnp.int32)
    for b in range(blocks):
        inside = (place >= b * slots) & (place < b * slots + tokens_ref[b])
        holder = jnp.where(inside, owner_ref[b], holder)
    total = replicas * per
    row = lax.broadcasted_iota(jnp.int32, (total, 1), 0)
    asker = row // per * DEVICE_REQUESTS + row % DEVICE_REQUESTS
    keep = holder == asker
    mlane = lax.broadcasted_iota(jnp.int32, (total, PAD), 1)

    def head(g, ml):
        col = slice(g * hd, (g + 1) * hd)
        vcol = slice((heads + g) * hd, (heads + g + 1) * hd)
        qg = qb[:, g * per : (g + 1) * per, :].reshape(total, hd)
        scores = (
            lax.dot_general(
                qg, kv[:, col], (((1,), (1,)), ((), ())), preferred_element_type=jnp.float32
            )
            * scale
        )
        top = jnp.max(jnp.where(keep, scores, -1e30), axis=1, keepdims=True)
        weights = jnp.where(keep, jnp.exp(scores - top), 0.0)
        mass = jnp.sum(weights, axis=1, keepdims=True)
        acc = jnp.dot(
            weights.astype(jnp.bfloat16), kv[:, vcol], preferred_element_type=jnp.float32
        ).reshape(replicas, per, hd)
        accf[:, g] = acc
        accb[:, g] = acc.astype(jnp.bfloat16)
        return jnp.where(mlane == g, top, jnp.where(mlane == heads + g, mass, ml))

    def hand_back(ml):
        mlb[...] = ml.reshape(replicas, per, PAD)
        for k in range(1, replicas):
            to = (r + k) % replicas
            push(accb.at[to], ar.at[k], a_send.at[k], a_recv.at[k], rdev(k))
            push(mlb.at[to], mr.at[k], m_send.at[k], m_recv.at[k], rdev(k))

    def finish_attention():
        loads[7].wait()
        for k in range(1, replicas):
            remote(ar.at[k], ar.at[k], a_send.at[k], a_recv.at[k], cdev).wait_recv()
            remote(mr.at[k], mr.at[k], m_send.at[k], m_recv.at[k], cdev).wait_recv()
        plane = lax.broadcasted_iota(jnp.int32, (per, PAD), 1)
        mls = [mlb[r]] + [mr[k] for k in range(1, replicas)]

        def pick(values, n):
            return jnp.sum(jnp.where(plane == n, values, 0.0), axis=1, keepdims=True)

        turn = lax.broadcasted_iota(jnp.int32, (per, hd), 0) % DEVICE_REQUESTS

        def spread(n):
            values = new_ref[:, n * hd : (n + 1) * hd].astype(jnp.float32)
            wide = values[:1]
            for i in range(1, DEVICE_REQUESTS):
                wide = jnp.where(turn == i, values[i : i + 1], wide)
            return jnp.broadcast_to(wide, (per, hd))

        for g in range(heads):
            query = qb[r, g * per : (g + 1) * per, :].astype(jnp.float32)
            fresh = jnp.sum(query * spread(g), axis=1, keepdims=True) * scale
            tops = [pick(v, g) for v in mls]
            best = fresh
            for t in tops:
                best = jnp.maximum(best, t)
            weight = jnp.exp(fresh - best)
            denom = weight
            mixed = weight * spread(heads + g)
            for k in range(replicas):
                factor = jnp.exp(tops[k] - best)
                part = accf[r, g] if k == 0 else ar[k, g].astype(jnp.float32)
                denom = denom + factor * pick(mls[k], heads + g)
                mixed = mixed + factor * part
            mixed = mixed / denom
            for j in range(group):
                cols = slice((g * group + j) * hd, (g * group + j + 1) * hd)
                attn_ref[:, cols] = mixed[
                    j * DEVICE_REQUESTS : (j + 1) * DEVICE_REQUESTS, :
                ].astype(attn_ref.dtype)

    my_slot = (r * (depth * CORES) + e) // QUART
    chunk = replicas * rows

    def gather(zo):
        for k in range(1, replicas):
            got = xb.at[(z + depth - zo) % depth, (r + replicas - k) % replicas]
            remote(got, got, r_send.at[zo, k], r_recv.at[zo, k], cdev).wait_recv()

    def expert(group_of):
        tall = len(group_of) * chunk
        block = jnp.concatenate(
            [xb[(z + depth - zo) % depth].reshape(chunk, width + PAD) for zo in group_of], axis=0
        )
        slane = lax.broadcasted_iota(jnp.int32, (tall, PAD), 1)
        mine = (slane % experts == my_slot) & (slane < 3 * experts)
        gain = jnp.sum(
            jnp.where(mine, block[:, width:].astype(jnp.float32), 0.0), axis=1, keepdims=True
        )
        halves = jnp.dot(block[:, :width], wgu[...], preferred_element_type=jnp.float32)
        acts = []
        for n in range(CORES):
            gate = halves[:, 2 * n * quarter : (2 * n + 1) * quarter]
            up = halves[:, (2 * n + 1) * quarter : (2 * n + 2) * quarter]
            acts.append((gate / (1.0 + jnp.exp(-gate)) * up).astype(jnp.bfloat16))
        step = width // 4
        for m in range(4):
            cols = slice(m * step, (m + 1) * step)
            part = jnp.dot(acts[0], wd[:quarter, cols], preferred_element_type=jnp.float32)
            part = part + jnp.dot(acts[1], wd[quarter:, cols], preferred_element_type=jnp.float32)
            part = part * gain
            for i, zo in enumerate(group_of):
                own_part = part[i * chunk : (i + 1) * chunk]
                pf[zo, :, cols] = own_part
                xs[zo, :, :, cols] = own_part.astype(jnp.bfloat16).reshape(replicas, rows, step)
        for zo in group_of:
            for k in range(1, replicas):
                to = (r + k) % replicas
                push(xs.at[zo, to], xr.at[zo, k], xs_send.at[zo, k], xs_recv.at[zo, k], rdev(k))

    def along(zo):
        total = pf[zo, pl.ds(pl.multiple_of(r * rows, rows), rows), :]
        for k in range(1, replicas):
            remote(
                xr.at[zo, k], xr.at[zo, k], xs_send.at[zo, k], xs_recv.at[zo, k], cdev
            ).wait_recv()
            total = total + xr[zo, k].astype(jnp.float32)
        if zo == 0:
            zf[...] = total
        else:
            zs[zo] = total.astype(jnp.bfloat16)
            push(zs.at[zo], zr.at[zo], zs_send.at[zo], zs_recv.at[zo], zdev(depth - zo))

    ml = head(0, jnp.zeros((total, PAD), jnp.float32))
    if depth > 2:
        onward(2)
    gather(0)
    done = 1
    if heads > 1:
        ml = head(1, ml)
        done = 2
    for zo in range(3, depth):
        onward(zo)
    for g in range(done, heads):
        ml = head(g, ml)
    hand_back(ml)
    loads[0].wait()
    loads[1].wait()
    for d in weights_in():
        d.wait_recv()
    expert((0,))
    gather(1)
    expert((1,))
    for zo in range(2, depth):
        gather(zo)
        expert((zo,))
        along(zo - 2)
    for zo in range(max(depth - 2, 0), depth):
        if zo == depth - 1:
            finish_attention()
        along(zo)
    result = zf[...]
    for zo in range(1, depth):
        remote(zr.at[zo], zr.at[zo], zs_send.at[zo], zs_recv.at[zo], cdev).wait_recv()
        result = result + zr[zo].astype(jnp.float32)
    moe_ref[...] = result.astype(moe_ref.dtype)
    for d in sent:
        d.wait_send()


def place_results(moe_ref, attn_ref, moe_out, attn_out, moe_v, attn_v, sem):
    ins = [
        pltpu.make_async_copy(moe_ref, moe_v, sem.at[0]),
        pltpu.make_async_copy(attn_ref, attn_v, sem.at[1]),
    ]
    outs = [
        pltpu.make_async_copy(moe_v, moe_out, sem.at[2]),
        pltpu.make_async_copy(attn_v, attn_out, sem.at[3]),
    ]
    for d in ins:
        d.start()
    for i, o in zip(ins, outs):
        i.wait()
        o.start()
    for o in outs:
        o.wait()


def fused(
    moe_input,
    expert_ids,
    route_weight,
    expert_slot,
    w_gate_up,
    w_down,
    queries,
    incoming_key_value,
    key_value_pool,
    block_owner,
    block_tokens,
):
    replicas = lax.axis_size("replica")
    depth = lax.axis_size("expert") // CORES
    experts = expert_slot.shape[0]
    rows, width = moe_input.shape
    group = QUERY_HEADS // KEY_VALUE_HEADS
    per = DEVICE_REQUESTS * group
    hd = HEAD_DIMENSION
    keys = key_value_pool.shape[0] * key_value_pool.shape[1]
    smem = pl.BlockSpec(memory_space=pltpu.SMEM)
    vmem = pl.BlockSpec(memory_space=pltpu.VMEM)
    hbm = pl.BlockSpec(memory_space=pl.ANY)
    bf, f32 = jnp.bfloat16, jnp.float32
    dma = pltpu.SemaphoreType.DMA
    moe_out, attn = pl.pallas_call(
        functools.partial(fused_kernel, replicas, depth, experts),
        out_shape=(
            jax.ShapeDtypeStruct((rows, width), bf),
            jax.ShapeDtypeStruct(queries.shape, bf),
        ),
        in_specs=[smem] * 3 + [hbm] * 8,
        out_specs=(vmem, vmem),
        scratch_shapes=[
            pltpu.VMEM(expert_ids.shape[::-1], expert_ids.dtype),
            pltpu.VMEM(route_weight.shape[::-1], f32),
            pltpu.VMEM(queries.shape, bf),
            pltpu.VMEM(incoming_key_value.shape, bf),
            pltpu.VMEM((depth, replicas, rows, width + PAD), bf),
            pltpu.VMEM((width, CORES * w_gate_up.shape[1]), bf),
            pltpu.VMEM((CORES * w_down.shape[0], width), bf),
            pltpu.VMEM((keys, key_value_pool.shape[2]), bf),
            pltpu.VMEM((depth, replicas * rows, width), f32),
            pltpu.VMEM((depth, replicas, rows, width), bf),
            pltpu.VMEM((depth, replicas, rows, width), bf),
            pltpu.VMEM((rows, width), f32),
            pltpu.VMEM((depth, rows, width), bf),
            pltpu.VMEM((depth, rows, width), bf),
            pltpu.VMEM((replicas, KEY_VALUE_HEADS * per, hd), bf),
            pltpu.VMEM((replicas, KEY_VALUE_HEADS, per, hd), f32),
            pltpu.VMEM((replicas, KEY_VALUE_HEADS, per, hd), bf),
            pltpu.VMEM((replicas, per, PAD), f32),
            pltpu.VMEM((replicas, KEY_VALUE_HEADS, per, hd), bf),
            pltpu.VMEM((replicas, per, PAD), f32),
            dma((8,)),
            dma((depth,)),
            dma((depth,)),
            dma((depth, replicas)),
            dma((depth, replicas)),
            dma((5,)),
            dma((5,)),
            dma((replicas,)),
            dma((replicas,)),
            dma((depth, replicas)),
            dma((depth, replicas)),
            dma((depth,)),
            dma((depth,)),
            dma((replicas,)),
            dma((replicas,)),
            dma((replicas,)),
            dma((replicas,)),
        ],
        compiler_params=pltpu.CompilerParams(
            collective_id=0, has_side_effects=True, vmem_limit_bytes=VMEM_LIMIT
        ),
    )(
        expert_slot,
        block_owner,
        block_tokens,
        expert_ids.T,
        route_weight.T,
        queries,
        incoming_key_value,
        moe_input,
        w_gate_up,
        w_down,
        key_value_pool.reshape(keys, key_value_pool.shape[2]),
    )
    return pl.pallas_call(
        place_results,
        out_shape=(
            jax.ShapeDtypeStruct(moe_out.shape, bf),
            jax.ShapeDtypeStruct(attn.shape, bf),
        ),
        in_specs=[hbm] * 2,
        out_specs=(hbm, hbm),
        scratch_shapes=[
            pltpu.VMEM(moe_out.shape, bf),
            pltpu.VMEM(attn.shape, bf),
            dma((4,)),
        ],
        compiler_params=pltpu.CompilerParams(vmem_limit_bytes=VMEM_LIMIT),
    )(moe_out, attn)


def shards(
    moe_input,
    expert_ids,
    route_weight,
    expert_slot,
    w_gate_up,
    w_down,
    queries,
    incoming_key_value,
    key_value_pool,
    block_owner,
    block_tokens,
):
    if fits_fused(expert_ids, expert_slot):
        return fused(
            moe_input,
            expert_ids,
            route_weight,
            expert_slot,
            w_gate_up,
            w_down,
            queries,
            incoming_key_value,
            key_value_pool,
            block_owner,
            block_tokens,
        )
    moe_out = mixture(moe_input, expert_ids, route_weight, expert_slot, w_gate_up, w_down)
    scale = 1.0 / math.sqrt(HEAD_DIMENSION)
    query_rows = queries.reshape(
        DEVICE_REQUESTS, KEY_VALUE_HEADS, QUERY_HEADS // KEY_VALUE_HEADS, HEAD_DIMENSION
    )
    latest_keys = incoming_key_value[:, : KEY_VALUE_HEADS * HEAD_DIMENSION].reshape(
        DEVICE_REQUESTS, KEY_VALUE_HEADS, HEAD_DIMENSION
    )
    new_score = (
        jnp.einsum("rgjd,rgd->rgj", query_rows, latest_keys, preferred_element_type=jnp.float32)
        * scale
    )
    incoming_values = (
        incoming_key_value[:, KEY_VALUE_HEADS * HEAD_DIMENSION :]
        .reshape(DEVICE_REQUESTS, KEY_VALUE_HEADS, 1, HEAD_DIMENSION)
        .astype(jnp.float32)
    )
    maxima, totals, weighted = attend_migrate(
        query_rows, key_value_pool, block_owner, block_tokens, scale
    )
    attn_out = (
        finish(maxima, totals, weighted, new_score, incoming_values)
        .reshape(DEVICE_REQUESTS, QUERY_HEADS * HEAD_DIMENSION)
        .astype(jnp.bfloat16)
    )
    return (moe_out, attn_out)


def solution(mesh):
    placed = (
        P(("replica", "expert"), None),
        P(("replica", "expert"), None),
        P(("replica", "expert"), None),
        P(),
        P(None, ("replica", "expert")),
        P(("replica", "expert"), None),
        P(("replica", "expert"), None),
        P(("replica", "expert"), None),
        P(("replica", "expert"), None, None),
        P(("replica", "expert")),
        P(("replica", "expert")),
    )
    return jax.shard_map(
        shards,
        mesh=mesh,
        in_specs=placed,
        out_specs=(P(("replica", "expert"), None), P(("replica", "expert"), None)),
        check_vma=False,
    )
```
